32 devices in a mesh: groups: 2 (over y), replica: 4 (over x, core), mp: 4 (over z).
Axes of the slice: x: 2, y: 2, z: 4, core: 2. Of those that a mesh axis runs over, the one named last changes fastest.
Arguments:
- layer_input: bfloat16 [2, 64, 8192], P(None, ('groups', 'replica'), 'mp'), parts along dimension 1, may hold values from -6 to 6
- kv_weight: bfloat16 [8192, 1024], P('mp'), may hold values from -0.0625 to 0.0625
- queries: bfloat16 [2, 64, 4096], P(None, ('groups', 'replica'), 'mp'), parts along dimension 1, may hold values from -15 to 15
- kv_pool: bfloat16 [8, 4, 8, 128, 1024], P(('groups', 'replica'), 'mp'), parts along dimension 0, may hold values from -6 to 6
- lengths: int32 [64], P(('groups', 'replica')), parts along dimension 0, may hold values from 1 to 510, 4096 in all
- block_table: int32 [64, 4], P(('groups', 'replica')), parts along dimension 0, may hold values from 0 to 31, as said below
- new_table: int32 [64, 4], P(('groups', 'replica')), parts along dimension 0, may hold values from 0 to 31, as said below
- migrations: int32 [16, 2], P('groups'), parts along dimension 0, may hold values from 0 to 31, as said below
Outputs:
- attn_first: bfloat16 [64, 4096], P(('groups', 'replica'), 'mp'), parts along dimension 0
- attn_second: bfloat16 [64, 4096], P(('groups', 'replica'), 'mp'), parts along dimension 0
- pool_after: bfloat16 [8, 4, 8, 128, 1024], P(('groups', 'replica'), 'mp'), parts along dimension 0
The draws below stay inside these ranges and needn't reach their ends.
There are 2 independent parts, one for each index of `groups`. The reference program is written for one: setup_inputs(seed, part) draws one part's arguments, and reference() takes and returns one part's arrays. A program takes and returns all parts, laid end to end along the dimension named above; an argument that names none is the same for every part. Nothing has to cross between parts.
Inputs may be any that keep to these rules, and one draw needn't show every extreme that they name: block_table[r, p] = m * 8 + s names slot s of device m along mp in row r's replica, holding tokens 128 * p to 128 * p + 127 of row r; every slot of a replica is named once, and every row has exactly 1 page on each device along mp. `new_table`: as block_table, for the rows after migration; a row that keeps its request keeps its entries, and every page of a migrating request keeps its device index along mp. `migrations`: each row (b, a): the request in row b moves to row a of another replica. Each replica sends exactly 2 requests, to 2 different replicas, and receives exactly 2, into the rows that it sends from.
All inputs are finite; a program needn't handle non-finite values. No bound on the sum of `lengths` on one device may be relied on, other than what follows from the above.
Results may differ from the reference program's by a relative error of at most 0.0052.
Values may be sent and summed in bfloat16 or wider, within the bound.
No kernel may reach another device: no remote copies, remote signals or barrier semaphores. Data moves between devices by JAX's collectives and lax.ppermute only.
A program may use at most 64 MiB of HBM per device.

```python
import math
import jax
import jax.numpy as jnp
import numpy as np
from jax import lax

D = 8192
H = 32
KVH = 4
HD = 128
KVW = 1024
PAGE = 128
PPD = 1
REQ = 8
MAXP = 4
SLOTS = 8
MIG = 2
REQS = 32
N_REPLICA = 4
N_MP = 4


def permutations(base_key, count, length):
    return jax.vmap(lambda subkey: jax.random.permutation(subkey, length))(jax.random.split(base_key, count)).astype(jnp.int32)


def plan(key):
    key_page, key_slot, key_label, key_shift, key_rows, key_arrive, key_shuffle = jax.random.split(key, 7)
    row_ids = jnp.arange(REQS, dtype=jnp.int32)
    page_perm = permutations(key_page, REQS, MAXP)
    slot_perm = permutations(key_slot, N_REPLICA * N_MP, SLOTS).reshape(N_REPLICA, N_MP, SLOTS)
    position = jnp.arange(MAXP, dtype=jnp.int32)
    device = position % N_MP
    within = position // N_MP
    replica_of = row_ids // REQ
    local_row = row_ids % REQ
    slot_value = device[None, :] * SLOTS + slot_perm[replica_of[:, None], device[None, :], local_row[:, None] * PPD + within[None, :]]
    inverse = jnp.argsort(page_perm, axis=1).astype(jnp.int32)
    block_table = jnp.take_along_axis(slot_value, inverse, axis=1).astype(jnp.int32)
    relabel = jax.random.permutation(key_label, N_REPLICA).astype(jnp.int32)
    position_of = jnp.argsort(relabel).astype(jnp.int32)
    shifts = 1 + jax.random.permutation(key_shift, N_REPLICA - 1).astype(jnp.int32)[:MIG]
    chosen = permutations(key_rows, N_REPLICA, REQ)[:, :MIG]
    arrival_order = permutations(key_arrive, N_REPLICA, MIG)
    replica_ids = jnp.arange(N_REPLICA, dtype=jnp.int32)
    destination = relabel[(position_of[:, None] + shifts[None, :]) % N_REPLICA]
    moved_from = replica_ids[:, None] * REQ + chosen
    slot_ids = jnp.arange(MIG, dtype=jnp.int32)[None, :]
    moved_to = destination * REQ + chosen[destination, arrival_order[destination, slot_ids]]
    migrations = jnp.stack([moved_from.reshape(-1), moved_to.reshape(-1)], axis=1).astype(jnp.int32)
    holder = row_ids.at[moved_to.reshape(-1)].set(moved_from.reshape(-1))
    arrival = jnp.zeros((REQS,), bool).at[moved_to.reshape(-1)].set(True)
    arrival_slot = jnp.zeros((REQS,), jnp.int32).at[moved_from.reshape(-1)].set(jnp.tile(jnp.arange(MIG, dtype=jnp.int32), N_REPLICA))
    device_of = block_table // SLOTS
    same_device = device_of[:, :, None] == device_of[:, None, :]
    earlier = position[:, None] > position[None, :]
    page_rank = jnp.sum(same_device & earlier[None, :, :], axis=2).astype(jnp.int32)
    own_slots = jnp.zeros((REQS, N_MP, PPD), jnp.int32).at[row_ids[:, None], device_of, page_rank].set(block_table % SLOTS)
    freed_slots = own_slots[moved_from].transpose(0, 2, 1, 3).reshape(N_REPLICA, N_MP, MIG * PPD)
    slot_shuffle = permutations(key_shuffle, N_REPLICA * N_MP, MIG * PPD).reshape(N_REPLICA, N_MP, MIG * PPD)
    source_device = device_of[holder]
    source_rank = page_rank[holder]
    item_index = arrival_slot[:, None] * PPD + source_rank
    row_replica = (row_ids // REQ)[:, None]
    picked = slot_shuffle[row_replica, source_device, item_index]
    moved_slot = source_device * SLOTS + freed_slots[row_replica, source_device, picked]
    new_table = jnp.where(arrival[:, None], moved_slot, block_table).astype(jnp.int32)
    return (block_table, new_table, migrations)


def draw_block_table(key, part):
    return plan(key)[0]


def draw_new_table(key, part):
    return plan(key)[1]


def draw_migrations(key, part):
    return plan(key)[2]


def level_of(own_key, extent, pieces, least, largest):
    level = 1.0
    for axis_at, blocks in pieces:
        heights = jax.random.uniform(jax.random.fold_in(jax.random.fold_in(own_key, 6), axis_at), (blocks,), jnp.float32, least / len(pieces), largest / len(pieces))
        level = level * jnp.repeat(jnp.exp(heights), extent[axis_at] // blocks).reshape((-1,) + (1,) * (len(extent) - 1 - axis_at))
    return level


def length_profile(number_of, total, reach, slope):
    weights = [(1 << 20) // math.isqrt(standing ** slope) + 1 for standing in range(2, number_of + 1)]
    spare, counts = total - reach - (number_of - 1), [1] * (number_of - 1)
    while spare > 0:
        movable = [i for i in range(number_of - 1) if counts[i] < reach]
        whole, remaining = sum([weights[i] for i in movable]), spare
        for i in movable:
            addition = min(reach - counts[i], max(1, remaining * weights[i] // whole), spare)
            counts[i] = counts[i] + addition
            spare = spare - addition
    return np.array([reach] + counts)


def uneven_parts(stream_key, count, total, reach, lean):
    if count == 2:
        one = jax.random.randint(stream_key, (), max(1, total - reach), min(reach, total - 1) + 1)
        return jnp.stack([one, total - one])
    sizes = jnp.asarray(length_profile(count, total, reach, lean), jnp.int32)
    couples = (count - 1) // 2
    source_of, sink = sizes[1:1 + 2 * couples:2], sizes[2:2 + 2 * couples:2]
    margin = jnp.minimum(source_of - 1, reach - sink)
    passed = jax.random.randint(jax.random.fold_in(stream_key, 1), (couples,), 0, 1 << 20) % (margin + 1)
    sizes = sizes.at[1:1 + 2 * couples:2].set(source_of - passed).at[2:2 + 2 * couples:2].set(sink + passed)
    return sizes[jax.random.permutation(jax.random.fold_in(stream_key, 2), count)]


def gaussian(stream_key, extent, scale, reach, cuts=(), kind=jnp.bfloat16):
    entries = scale * jax.random.normal(stream_key, extent, jnp.float32)
    if cuts:
        entries = entries * level_of(stream_key, extent, cuts, -0.22, 0.18)
    return jnp.clip(entries, -reach, reach).astype(kind)


def setup_inputs(seed: int = 0, part: int = 0) -> dict:
    streams_of = jax.random.split(jax.random.key(seed), 9)
    part_keys = jax.random.split(jax.random.fold_in(streams_of[8], part), 9)
    layer_input = gaussian(part_keys[0], (2, REQS, D), 1.0, 6.0, ((1, 4), (2, 4)))
    kv_weight = gaussian(streams_of[1], (D, KVW), D ** -0.5, 0.0625, ((0, 4),))
    queries = gaussian(part_keys[2], (2, REQS, H * HD), 2.5, 15.0, ((1, 4), (2, 4)))
    kv_pool = gaussian(part_keys[3], (N_REPLICA, N_MP, SLOTS, PAGE, KVW), 1.0, 6.0, ((0, 4), (1, 4)))
    lengths = uneven_parts(part_keys[4], REQS, REQS * PAGE * PPD * N_MP // 4, PAGE * PPD * N_MP - 2, 2).astype(jnp.int32)
    block_table = draw_block_table(jax.random.fold_in(jax.random.fold_in(streams_of[8], part), 71), part)
    new_table = draw_new_table(jax.random.fold_in(jax.random.fold_in(streams_of[8], part), 71), part)
    migrations = draw_migrations(jax.random.fold_in(jax.random.fold_in(streams_of[8], part), 71), part)
    return dict(layer_input=layer_input, kv_weight=kv_weight, queries=queries, kv_pool=kv_pool, lengths=lengths, block_table=block_table, new_table=new_table, migrations=migrations)


CAP = 20.0

def write_rows(flat_pool, new_rows, table_rows, positions):
    row_ids = jnp.arange(REQS, dtype=jnp.int32)
    page_of = (positions // PAGE).astype(jnp.int32)
    global_slot = jnp.take_along_axis(table_rows, page_of[:, None], axis=1)[:, 0]
    flat_index = row_ids // REQ * (N_MP * SLOTS) + global_slot
    return flat_pool.at[flat_index, positions % PAGE].set(new_rows)

def attend(query_rows, flat_pool, table_rows, positions):
    row_ids = jnp.arange(REQS, dtype=jnp.int32)
    flat_index = (row_ids // REQ * (N_MP * SLOTS))[:, None] + table_rows
    scale = 1.0 / math.sqrt(HD)

    def one_row(row_item):
        query_row, page_ids, last_token = row_item
        page_rows = flat_pool[page_ids].reshape(MAXP * PAGE, KVW).astype(jnp.float32)
        key_rows = page_rows[:, :KVH * HD].reshape(MAXP * PAGE, KVH, HD)
        value_rows = page_rows[:, KVH * HD:].reshape(MAXP * PAGE, KVH, HD)
        grouped = query_row.astype(jnp.float32).reshape(KVH, H // KVH, HD)
        scores = jnp.einsum('kge,tke->kgt', grouped, key_rows, precision=lax.Precision.HIGHEST) * scale
        capped = CAP * jnp.tanh(scores / CAP)
        inside = jnp.arange(MAXP * PAGE) <= last_token
        weight = jnp.where(inside[None, None, :], jnp.exp(capped), 0.0)
        weight_low = lax.optimization_barrier(weight.astype(jnp.bfloat16)).astype(jnp.float32)
        numerator = jnp.einsum('kgt,tke->kge', weight_low, value_rows, precision=lax.Precision.HIGHEST)
        denominator = lax.optimization_barrier(jnp.sum(weight, axis=2))
        return (numerator / denominator[:, :, None]).reshape(H * HD).astype(jnp.bfloat16)
    return lax.map(one_row, (query_rows, flat_index, positions))

def reference(layer_input, kv_weight, queries, kv_pool, lengths, block_table, new_table, migrations):
    flat_pool = kv_pool.reshape(N_REPLICA * N_MP * SLOTS, PAGE, KVW)
    kv_first = jnp.dot(layer_input[0], kv_weight, preferred_element_type=jnp.float32).astype(jnp.bfloat16)
    cache_one = write_rows(flat_pool, kv_first, block_table, lengths)
    attn_first = attend(queries[0], cache_one, block_table, lengths)
    row_ids = jnp.arange(REQS, dtype=jnp.int32)
    holder = row_ids.at[migrations[:, 1]].set(migrations[:, 0])
    stride = N_MP * SLOTS
    source = (holder // REQ * stride)[:, None] + block_table[holder]
    target = (row_ids // REQ * stride)[:, None] + new_table
    cache_two = jnp.zeros_like(cache_one).at[target.reshape(-1)].set(cache_one[source.reshape(-1)])
    lengths_after = (lengths[holder] + 1).astype(jnp.int32)
    kv_second = jnp.dot(layer_input[1], kv_weight, preferred_element_type=jnp.float32).astype(jnp.bfloat16)
    pool_after = write_rows(cache_two, kv_second, new_table, lengths_after)
    attn_second = attend(queries[1], pool_after, new_table, lengths_after)
    return (attn_first, attn_second, pool_after.reshape(N_REPLICA, N_MP, SLOTS, PAGE, KVW))
```

```python
import functools
import math

import jax
import jax.numpy as jnp
from jax import lax
from jax.experimental import pallas as pl
from jax.experimental.pallas import tpu as pltpu
from jax.sharding import PartitionSpec as P

H = 32
KVH = 4
HD = 128
GROUP = H // KVH
CAP = 20.0
SCALE = 1.0 / math.sqrt(HD)
WINDOW = 32
KV_ROWS = 24

SMEM = pl.BlockSpec(memory_space=pltpu.SMEM)
VMEM = pl.BlockSpec(memory_space=pltpu.VMEM)
ANY = pl.BlockSpec(memory_space=pl.ANY)
SEND = jnp.bfloat16


def shift_by(value, axis, amount):
    size = lax.axis_size(axis)
    return lax.ppermute(value, axis, [(i, (i + amount) % size) for i in range(size)])


def exchange(messages, axis):
    return [shift_by(message, axis, s + 1) for s, message in enumerate(messages)]


def count_up(limit, step, start):
    return lax.fori_loop(0, limit, step, start)


def locate(table, row, column, slots):
    def step(p, found):
        entry = table[row, p]
        here = entry // slots == column
        return jnp.where(here, p, found[0]), jnp.where(here, entry % slots, found[1])

    return count_up(table.shape[1], step, (jnp.int32(0), jnp.int32(0)))


def pair_row(moves, source, target, rows, side):
    def step(j, found):
        match = (moves[j, 0] // rows == source) & (moves[j, 1] // rows == target)
        return (
            jnp.where(match, jnp.int32(1), found[0]),
            jnp.where(match, moves[j, side] % rows, found[1]),
        )

    return count_up(moves.shape[0], step, (jnp.int32(0), jnp.int32(0)))


def source_of(axis, shift):
    size = lax.axis_size(axis)
    return lax.rem(lax.axis_index(axis) + (size - shift), size)


def target_of(axis, shift):
    return lax.rem(lax.axis_index(axis) + shift, lax.axis_size(axis))


def head_columns(device, local_heads):
    return pl.ds(pl.multiple_of(device * local_heads // GROUP * HD, HD), HD)


def weight_of(score):
    return jnp.exp(CAP * jnp.tanh(score * (SCALE / CAP)))


def leave_kernel(rows, moves, table, pool, *refs):
    outs, sems = refs[:-1], refs[-1]
    me, column = lax.axis_index("replica"), lax.axis_index("mp")
    copies = []
    for s, out in enumerate(outs):
        _, row = pair_row(moves, me, target_of("replica", s + 1), rows, 0)
        _, slot = locate(table, row, column, pool.shape[0])
        copies.append(pltpu.make_async_copy(pool.at[slot], out, sems.at[s]))
        copies[-1].start()
    for copy in copies:
        copy.wait()


def project_kernel(count, local_heads, x, weight, q, *refs):
    outs, total = refs[:-1], refs[-1]
    step = pl.program_id(0)
    rows = q.shape[1]
    query_rows = 2 * local_heads * rows

    @pl.when(step == 0)
    def _():
        total[...] = jnp.zeros_like(total)
        wide = [q[i].astype(jnp.float32) for i in range(2)]
        blocks = [wide[i][:, h * HD : (h + 1) * HD] for i in range(2) for h in range(local_heads)]
        packed = jnp.concatenate(blocks, axis=0).astype(jnp.bfloat16)
        for out in outs:
            out[:query_rows, :] = packed

    total[...] += jnp.dot(x[...], weight[...], preferred_element_type=jnp.float32)

    @pl.when(step == pl.num_programs(0) - 1)
    def _():
        for s, out in enumerate(outs):
            columns = head_columns(target_of("mp", s), local_heads)
            parts = []
            for half in range(2):
                part = total.at[:, pl.ds(half * KVH * HD, KVH * HD)][:, columns]
                high = part.astype(jnp.bfloat16)
                parts += [high, (part - high.astype(jnp.float32)).astype(jnp.bfloat16)]
            out[query_rows:, :] = jnp.concatenate(parts, axis=0)


def token_kernel(count, replicas, rows, moves, lengths, *refs):
    messages, kv, outs = refs[:count], refs[count], refs[count + 1 :]
    tokens = 2 * rows
    base = messages[0].shape[0] - 4 * tokens
    me = lax.axis_index("replica")
    for half in range(2):
        total = jnp.zeros((tokens, HD), jnp.float32)
        for message in messages:
            start = base + 2 * half * tokens
            total += message[start : start + tokens, :].astype(jnp.float32)
            total += message[start + tokens : start + 2 * tokens, :].astype(jnp.float32)
        kv[half] = total.astype(jnp.bfloat16).astype(jnp.float32)
    for s, out in enumerate(outs):
        _, row = pair_row(moves, me, target_of("replica", s + 1), rows, 0)
        out[...] = jnp.zeros_like(out)
        out[0:1, :] = kv[0, pl.ds(row, 1), :]
        out[1:2, :] = kv[1, pl.ds(row, 1), :]
        out[2:3, :] = jnp.full((1, HD), lengths[row], jnp.int32).astype(jnp.float32)


def page_attention(q, keys, values, inside):
    scores = lax.dot_general(
        q, keys, (((1,), (1,)), ((), ())), preferred_element_type=jnp.float32
    )
    weight = jnp.where(inside, weight_of(scores), 0.0)
    numerator = jnp.dot(weight.astype(jnp.bfloat16), values, preferred_element_type=jnp.float32)
    return numerator, jnp.sum(weight, axis=1, keepdims=True)


def attend_kernel(count, local_heads, table, lengths, pool, *refs):
    messages = refs[:count]
    num, den, pool_out, pages, wide, in_sems, out_sems = refs[count:]
    column = lax.axis_index("mp")
    rows = lengths.shape[0]
    slots, page_size, width = pool.shape
    both = 2 * local_heads
    places = [locate(table, r, column, slots) for r in range(rows)]
    loads = [
        pltpu.make_async_copy(pool.at[places[r][1]], pages.at[r], in_sems.at[r]) for r in range(rows)
    ]
    stores = [
        pltpu.make_async_copy(pages.at[r], pool_out.at[places[r][1]], out_sems.at[r])
        for r in range(rows)
    ]
    for load in loads:
        load.start()
    for s, message in enumerate(messages):
        wide[s] = message[: both * rows, :].astype(jnp.float32)
    lane = lax.broadcasted_iota(jnp.int32, (both, HD), 1)
    token = lax.broadcasted_iota(jnp.int32, (both, page_size), 1)
    denominators = [jnp.zeros((both, HD), jnp.float32) for _ in range(count)]
    for r in range(rows):
        loads[r].wait()
        stores[r].start()
        inside = token < lengths[r] - places[r][0] * page_size
        for s in range(count):
            columns = head_columns(source_of("mp", s), local_heads)
            q = wide[s, pl.ds(r, both, stride=rows), :].astype(jnp.bfloat16)
            keys = pages.at[r, :, pl.ds(0, width // 2)][:, columns]
            values = pages.at[r, :, pl.ds(width // 2, width // 2)][:, columns]
            numerator, denominator = page_attention(q, keys, values, inside)
            num[s, pl.ds(r, both, stride=rows), :] = numerator
            denominators[s] += jnp.where(lane == r, denominator, 0.0)
    for s in range(count):
        den[s] = denominators[s]
    for store in stores:
        store.wait()


def arrive_kernel(count, replicas, local_heads, moves, table, kv, *refs):
    rows, slots = table.shape[0], table.shape[0]
    refs = list(refs)
    take = lambda n: [refs.pop(0) for _ in range(n)]
    pages_in, tokens_in, messages = take(replicas - 1), take(replicas - 1), take(count)
    num_in, den_in = take(2)
    outs = take(count - 1)
    own_num, own_den, num, den, pages, wide, sems = refs
    me, column = lax.axis_index("replica"), lax.axis_index("mp")
    page_size, width = pages_in[0].shape
    half_rows = local_heads * rows
    loads = [
        pltpu.make_async_copy(page, pages.at[s], sems.at[s]) for s, page in enumerate(pages_in)
    ]
    for load in loads:
        load.start()
    num[...] = num_in[...]
    den[...] = den_in[...]
    for s, message in enumerate(messages):
        wide[s] = message[half_rows : 2 * half_rows, :].astype(jnp.float32)
    lane = lax.broadcasted_iota(jnp.int32, (local_heads, HD), 1)
    token = lax.broadcasted_iota(jnp.int32, (local_heads, page_size), 1)
    for shift in range(1, replicas):
        loads[shift - 1].wait()
        valid, row = pair_row(moves, source_of("replica", shift), me, rows, 1)

        @pl.when(valid == 1)
        def _():
            index, _ = locate(table, row, column, slots)
            length = tokens_in[shift - 1][2:3, :]
            inside = (token + index * page_size).astype(jnp.float32) < length
            for s in range(count):
                columns = head_columns(source_of("mp", s), local_heads)
                q = wide[s, pl.ds(row, local_heads, stride=rows), :].astype(jnp.bfloat16)
                keys = pages.at[shift - 1, :, pl.ds(0, width // 2)][:, columns]
                values = pages.at[shift - 1, :, pl.ds(width // 2, width // 2)][:, columns]
                numerator, denominator = page_attention(q, keys, values, inside)
                num[s, pl.ds(half_rows + row, local_heads, stride=rows), :] = numerator
                old = den[s, pl.ds(local_heads, local_heads), :]
                den[s, pl.ds(local_heads, local_heads), :] = jnp.where(lane == row, denominator, old)

    own_num[...] = num[0]
    own_den[...] = den[0]
    filler = jnp.zeros((KV_ROWS - 2 * rows - (replicas - 1), HD), jnp.float32)
    all_kv = []
    for half in range(2):
        all_kv += [kv[half]] + [arrived[half : half + 1, :] for arrived in tokens_in] + [filler]
    all_kv = jnp.concatenate(all_kv, axis=0)
    for s, out in enumerate(outs):
        at = count - 1 - s
        parts = den[at]
        high = parts.astype(SEND).astype(jnp.float32)
        parts = high + pltpu.roll(parts - high, HD // 2, 1)
        out[...] = jnp.concatenate([num[at], parts, all_kv], axis=0).astype(SEND)


def finish_kernel(count, replicas, local_heads, moves, table, lengths, kv, q, num, den, *refs):
    refs = list(refs)
    take = lambda n: [refs.pop(0) for _ in range(n)]
    pages_in, tokens_in, messages = take(replicas - 1), take(replicas - 1), take(count - 1)
    pool_raw, _, first, second, pool = take(5)
    held, full, windows, page_sems, read_sems, write_sems = refs
    me, column = lax.axis_index("replica"), lax.axis_index("mp")
    rows = lengths.shape[0]
    slots, page_size, width = pool_raw.shape
    both = 2 * local_heads

    arrivals, copies = [], []
    for shift in range(1, replicas):
        valid, row = pair_row(moves, source_of("replica", shift), me, rows, 1)
        length = jnp.max(tokens_in[shift - 1][2:3, :]).astype(jnp.int32)
        _, slot = locate(table, row, column, slots)
        arrivals.append((valid == 1, row, length))
        copies.append(
            pltpu.make_async_copy(pages_in[shift - 1], pool.at[slot], page_sems.at[shift - 1])
        )
        pl.when(valid == 1)(copies[-1].start)

    plans = []
    for r in range(rows):
        origin, length = jnp.int32(0), lengths[r]
        for s, (valid, row, arrived) in enumerate(arrivals):
            here = valid & (row == r)
            origin = jnp.where(here, s + 1, origin)
            length = jnp.where(here, arrived, length)
        index, slot = locate(table, r, column, slots)
        at = length - index * page_size
        touched = (at >= -1) & (at < page_size)
        start = jnp.clip(at, 0, page_size - WINDOW) // 16 * 16
        start = pl.multiple_of(start, 16)
        span = pl.ds(start, WINDOW)
        sources = [pool_raw.at[slot]] + list(pages_in)
        for s, source in enumerate(sources):

            @pl.when(touched & (origin == s))
            def _(source=source, span=span, r=r):
                pltpu.make_async_copy(source.at[span], windows.at[r], read_sems.at[r]).start()

        plans.append((touched, origin, at - start, pool.at[slot, span], pool_raw.at[slot, span]))

    for half in range(2):
        held[half] = kv[half, :rows, :]
        for s, (valid, row, _) in enumerate(arrivals):

            @pl.when(valid)
            def _(half=half, s=s, row=row):
                held[half, pl.ds(row, 1), :] = tokens_in[s][half : half + 1, :]

    query_rows = both * rows
    kv_base = messages[0].shape[0] - 2 * KV_ROWS
    filler = jnp.zeros((KV_ROWS - 2 * rows - (replicas - 1), HD), jnp.float32)
    for s in range(count):
        device = source_of("mp", s)
        for half in range(2):
            if s == 0:
                chunk = jnp.concatenate(
                    [kv[half]] + [arrived[half : half + 1, :] for arrived in tokens_in] + [filler],
                    axis=0,
                )
            else:
                start = kv_base + half * KV_ROWS
                chunk = messages[s - 1][start : start + KV_ROWS, :].astype(jnp.float32)

            def place(half=half, device=device, chunk=chunk):
                columns = head_columns(device, local_heads)
                full.at[:, pl.ds(half * (width // 2), width // 2)][:, columns] = chunk

            if local_heads == GROUP:
                place()
            else:
                pl.when(lax.rem(device * local_heads, GROUP) == 0)(place)

    sums = den[...]
    for message in messages:
        part = message[query_rows : query_rows + both, :].astype(jnp.float32)
        sums += part + pltpu.roll(part, HD // 2, 1)
    sums = jnp.transpose(sums)[:rows, :]
    for step, out in enumerate((first, second)):
        results = []
        for h in range(local_heads):
            at = (step * local_heads + h) * rows
            query = q[at : at + rows, :].astype(jnp.float32)
            numerator = num[at : at + rows, :]
            for message in messages:
                numerator += message[at : at + rows, :].astype(jnp.float32)
            denominator = sums[:, step * local_heads + h : step * local_heads + h + 1]
            extra = [(kv[0, :rows, :], kv[1, :rows, :])]
            if step == 1:
                extra = [(held[0], held[1]), (kv[0, rows:, :], kv[1, rows:, :])]
            for key, value in extra:
                weight = weight_of(jnp.sum(query * key, axis=1, keepdims=True))
                numerator += weight.astype(jnp.bfloat16).astype(jnp.float32) * value
                denominator += weight
            results.append(numerator / denominator)
        out[...] = jnp.concatenate(results, axis=1).astype(out.dtype)

    for (valid, _, _), copy in zip(arrivals, copies):
        pl.when(valid)(copy.wait)
    place_ids = lax.broadcasted_iota(jnp.int32, (WINDOW, width), 0)
    for r, (touched, origin, offset, target, source) in enumerate(plans):

        @pl.when(touched)
        def _(r=r, origin=origin, offset=offset, target=target, source=source):
            pltpu.make_async_copy(source, windows.at[r], read_sems.at[r]).wait()
            row = jnp.where(origin == 0, r, 2 * rows + origin - 1)
            old = windows[r].astype(jnp.float32)
            new = jnp.where(place_ids == offset, full[pl.ds(row, 1), :], old)
            new = jnp.where(place_ids == offset + 1, full[rows + r : rows + r + 1, :], new)
            windows[r] = new.astype(jnp.bfloat16)
            pltpu.make_async_copy(windows.at[r], target, write_sems.at[r]).start()

    for r, (touched, _, _, target, _) in enumerate(plans):

        @pl.when(touched)
        def _(r=r, target=target):
            pltpu.make_async_copy(windows.at[r], target, write_sems.at[r]).wait()


def params(megabytes=32, **rest):
    return pltpu.CompilerParams(vmem_limit_bytes=megabytes << 20, **rest)


def body(layer_input, kv_weight, queries, kv_pool, lengths, block_table, new_table, migrations):
    replicas, count = lax.axis_size("replica"), lax.axis_size("mp")
    rows = lengths.shape[0]
    pool = kv_pool[0, 0]
    slots, page_size, width = pool.shape
    local_heads = queries.shape[2] // HD
    both = 2 * local_heads
    query_rows = both * rows
    depth = layer_input.shape[2]
    f32, bf16 = jnp.float32, jnp.bfloat16
    shape = jax.ShapeDtypeStruct

    leaving = pl.pallas_call(
        functools.partial(leave_kernel, rows),
        out_shape=[shape((page_size, width), bf16)] * (replicas - 1),
        in_specs=[SMEM, SMEM, ANY],
        out_specs=[ANY] * (replicas - 1),
        scratch_shapes=[pltpu.SemaphoreType.DMA((replicas - 1,))],
        compiler_params=params(),
        name="leave",
    )(migrations, block_table, pool)
    pages_in = exchange(leaving, "replica")

    block = math.gcd(depth, 512)
    message_rows = query_rows + 8 * rows
    sent = pl.pallas_call(
        functools.partial(project_kernel, count, local_heads),
        grid=(depth // block,),
        out_shape=[shape((message_rows, HD), bf16)] * count,
        in_specs=[
            pl.BlockSpec((2 * rows, block), lambda k: (0, k)),
            pl.BlockSpec((block, width), lambda k: (k, 0)),
            pl.BlockSpec(queries.shape, lambda k: (0, 0, 0)),
        ],
        out_specs=[pl.BlockSpec((message_rows, HD), lambda k: (0, 0))] * count,
        scratch_shapes=[pltpu.VMEM((2 * rows, width), f32)],
        compiler_params=params(),
        name="project",
    )(layer_input.reshape(2 * rows, depth), kv_weight, queries)
    messages = [sent[0]] + exchange(sent[1:], "mp")

    kv, *tokens = pl.pallas_call(
        functools.partial(token_kernel, count, replicas, rows),
        out_shape=[shape((2, 2 * rows, HD), f32)] + [shape((8, HD), f32)] * (replicas - 1),
        in_specs=[SMEM, SMEM] + [VMEM] * count,
        out_specs=[VMEM] * replicas,
        compiler_params=params(),
        name="token",
    )(migrations, lengths, *messages)
    tokens_in = exchange(tokens, "replica")

    num, den, pool_copy = pl.pallas_call(
        functools.partial(attend_kernel, count, local_heads),
        out_shape=[
            shape((count, query_rows, HD), f32),
            shape((count, both, HD), f32),
            shape(pool.shape, bf16),
        ],
        in_specs=[SMEM, SMEM, ANY] + [VMEM] * count,
        out_specs=[VMEM, VMEM, ANY],
        scratch_shapes=[
            pltpu.VMEM((rows, page_size, width), bf16),
            pltpu.VMEM((count, query_rows, HD), f32),
            pltpu.SemaphoreType.DMA((rows,)),
            pltpu.SemaphoreType.DMA((rows,)),
        ],
        compiler_params=params(),
        name="attend",
    )(block_table, lengths, pool, *messages)

    sum_rows = query_rows + both + 2 * KV_ROWS
    *sums, num, den = pl.pallas_call(
        functools.partial(arrive_kernel, count, replicas, local_heads),
        out_shape=[shape((sum_rows, HD), SEND)] * (count - 1)
        + [shape((query_rows, HD), f32), shape((both, HD), f32)],
        in_specs=[SMEM, SMEM, VMEM]
        + [ANY] * (replicas - 1)
        + [VMEM] * (replicas - 1)
        + [VMEM] * count
        + [VMEM] * 2,
        out_specs=[VMEM] * (count + 1),
        scratch_shapes=[
            pltpu.VMEM((count, query_rows, HD), f32),
            pltpu.VMEM((count, both, HD), f32),
            pltpu.VMEM((replicas - 1, page_size, width), bf16),
            pltpu.VMEM((count, query_rows // 2, HD), f32),
            pltpu.SemaphoreType.DMA((replicas - 1,)),
        ],
        compiler_params=params(),
        name="arrive",
    )(migrations, new_table, kv, *pages_in, *tokens_in, *messages, num, den)
    sums_in = exchange(sums, "mp")

    first, second, pool_after = pl.pallas_call(
        functools.partial(finish_kernel, count, replicas, local_heads),
        out_shape=[
            shape((rows, local_heads * HD), bf16),
            shape((rows, local_heads * HD), bf16),
            shape(pool.shape, bf16),
        ],
        in_specs=[SMEM, SMEM, SMEM]
        + [VMEM] * 4
        + [ANY] * (replicas - 1)
        + [VMEM] * (replicas - 1)
        + [VMEM] * (count - 1)
        + [ANY, ANY],
        out_specs=[VMEM, VMEM, ANY],
        scratch_shapes=[
            pltpu.VMEM((2, rows, HD), f32),
            pltpu.VMEM((KV_ROWS, width), f32),
            pltpu.VMEM((rows, WINDOW, width), bf16),
            pltpu.SemaphoreType.DMA((replicas - 1,)),
            pltpu.SemaphoreType.DMA((rows,)),
            pltpu.SemaphoreType.DMA((rows,)),
        ],
        input_output_aliases={7 + 2 * (replicas - 1) + (count - 1) + 1: 2},
        compiler_params=params(),
        name="finish",
    )(migrations, new_table, lengths, kv, messages[0], num, den, *pages_in, *tokens_in, *sums_in, pool, pool_copy)
    return first, second, pool_after[None, None]


def solution(mesh):
    return jax.shard_map(
        body,
        mesh=mesh,
        in_specs=(
            P(None, ("groups", "replica"), "mp"),
            P("mp", None),
            P(None, ("groups", "replica"), "mp"),
            P(("groups", "replica"), "mp", None, None, None),
            P(("groups", "replica")),
            P(("groups", "replica"), None),
            P(("groups", "replica"), None),
            P("groups", None),
        ),
        out_specs=(
            P(("groups", "replica"), "mp"),
            P(("groups", "replica"), "mp"),
            P(("groups", "replica"), "mp", None, None, None),
        ),
        check_vma=False,
    )
```

```python
import functools
import math

import jax
import jax.numpy as jnp
from jax import lax
from jax.experimental import pallas as pl
from jax.experimental.pallas import tpu as pltpu
from jax.sharding import PartitionSpec as P

H = 32
KVH = 4
HD = 128
GROUP = H // KVH
CAP = 20.0
SCALE = 1.0 / math.sqrt(HD)
WINDOW = 32
KV_ROWS = 24

SMEM = pl.BlockSpec(memory_space=pltpu.SMEM)
VMEM = pl.BlockSpec(memory_space=pltpu.VMEM)
ANY = pl.BlockSpec(memory_space=pl.ANY)
HBM = pl.BlockSpec(memory_space=pltpu.HBM)
SEND = jnp.bfloat16


def swap(value, axis, distance):
    size = lax.axis_size(axis)
    return lax.ppermute(value, axis, [(i, i ^ distance) for i in range(size)])


def exchange(messages, axis):
    return [swap(message, axis, d + 1) for d, message in enumerate(messages)]


def partner(axis, distance):
    return lax.axis_index(axis) ^ distance


def split(value, size):
    if size & (size - 1) == 0:
        return lax.shift_right_logical(value, size.bit_length() - 1), value & (size - 1)
    return lax.div(value, size), lax.rem(value, size)


def count_up(limit, step, state):
    if limit > 8:
        return lax.fori_loop(0, limit, step, state)
    for i in range(limit):
        state = step(i, state)
    return state


def locate(table, row, column, slots):
    def step(p, found):
        device, slot = split(table[p, row], slots)
        here = device == column
        return jnp.where(here, p, found[0]), jnp.where(here, slot, found[1])

    return count_up(table.shape[0], step, (jnp.int32(0), jnp.int32(0)))


def pair_row(moves, source, target, rows, side):
    def step(j, found):
        ends = [split(moves[i, j], rows) for i in range(2)]
        match = (ends[0][0] == source) & (ends[1][0] == target)
        return (
            jnp.where(match, jnp.int32(1), found[0]),
            jnp.where(match, ends[side][1], found[1]),
        )

    return count_up(moves.shape[1], step, (jnp.int32(0), jnp.int32(0)))


def head_columns(device, local_heads):
    return pl.ds(pl.multiple_of(split(device * local_heads, GROUP)[0] * HD, HD), HD)


def weight_of(score):
    return jnp.exp(CAP * jnp.tanh(score * (SCALE / CAP)))


def leave_kernel(rows, moves, table, pool, *refs):
    outs, sems = refs[:-1], refs[-1]
    me, column = lax.axis_index("replica"), lax.axis_index("mp")
    copies = []
    for s, out in enumerate(outs):
        _, row = pair_row(moves, me, partner("replica", s + 1), rows, 0)
        _, slot = locate(table, row, column, pool.shape[0])
        copies.append(pltpu.make_async_copy(pool.at[slot], out, sems.at[s]))
        copies[-1].start()
    for copy in copies:
        copy.wait()


def project_kernel(count, local_heads, x, weight, q, *refs):
    outs, total = refs[:-1], refs[-1]
    step = pl.program_id(0)
    rows = q.shape[1]
    query_rows = 2 * local_heads * rows

    @pl.when(step == 0)
    def _():
        total[...] = jnp.zeros_like(total)
        wide = [q[i].astype(jnp.float32) for i in range(2)]
        blocks = [wide[i][:, h * HD : (h + 1) * HD] for i in range(2) for h in range(local_heads)]
        packed = jnp.concatenate(blocks, axis=0).astype(jnp.bfloat16)
        for out in outs:
            out[:query_rows, :] = packed

    total[...] += jnp.dot(x[...], weight[...], preferred_element_type=jnp.float32)

    @pl.when(step == pl.num_programs(0) - 1)
    def _():
        for s, out in enumerate(outs):
            columns = head_columns(partner("mp", s), local_heads)
            parts = []
            for half in range(2):
                part = total.at[:, pl.ds(half * KVH * HD, KVH * HD)][:, columns]
                high = part.astype(jnp.bfloat16)
                parts += [high, (part - high.astype(jnp.float32)).astype(jnp.bfloat16)]
            out[query_rows:, :] = jnp.concatenate(parts, axis=0)


def token_kernel(count, replicas, rows, moves, lengths, *refs):
    messages, kv, outs = refs[:count], refs[count], refs[count + 1 :]
    tokens = 2 * rows
    base = messages[0].shape[0] - 4 * tokens
    me = lax.axis_index("replica")
    for half in range(2):
        total = jnp.zeros((tokens, HD), jnp.float32)
        for message in messages:
            start = base + 2 * half * tokens
            total += message[start : start + tokens, :].astype(jnp.float32)
            total += message[start + tokens : start + 2 * tokens, :].astype(jnp.float32)
        kv[half] = total.astype(jnp.bfloat16).astype(jnp.float32)
    for s, out in enumerate(outs):
        _, row = pair_row(moves, me, partner("replica", s + 1), rows, 0)
        out[...] = jnp.zeros_like(out)
        out[0:1, :] = kv[0, pl.ds(row, 1), :]
        out[1:2, :] = kv[1, pl.ds(row, 1), :]
        out[2:3, :] = jnp.full((1, HD), lengths[row], jnp.int32).astype(jnp.float32)


def scores_of(q, keys):
    return lax.dot_general(q, keys, (((1,), (1,)), ((), ())), preferred_element_type=jnp.float32)


def attend_kernel(count, local_heads, table, lengths, pool, *refs):
    messages = refs[:count]
    num, den, pool_out, wide, sem = refs[count:]
    column = lax.axis_index("mp")
    rows = lengths.shape[0]
    slots, page_size, width = pool.shape
    both = 2 * local_heads
    store = pltpu.make_async_copy(pool, pool_out, sem)
    store.start()
    for s, message in enumerate(messages):
        wide[s] = message[: both * rows, :].astype(jnp.float32)
    lane = lax.broadcasted_iota(jnp.int32, (both, HD), 1)
    token = lax.broadcasted_iota(jnp.int32, (both, page_size), 1)
    places = [locate(table, r, column, slots) for r in range(rows)]
    columns = [head_columns(partner("mp", s), local_heads) for s in range(count)]
    keys = pool.at[:, :, pl.ds(0, width // 2)]
    values = pool.at[:, :, pl.ds(width // 2, width // 2)]
    cases = [(r, s) for r in range(rows) for s in range(count)]
    scores = {}
    for r, s in cases:
        q = wide[s, pl.ds(r, both, stride=rows), :].astype(jnp.bfloat16)
        scores[r, s] = scores_of(q, keys[places[r][1], :, columns[s]])
    weights = {}
    denominators = [jnp.zeros((both, HD), jnp.float32) for _ in range(count)]
    for r, s in cases:
        inside = token < lengths[r] - places[r][0] * page_size
        weight = jnp.where(inside, weight_of(scores[r, s]), 0.0)
        weights[r, s] = weight.astype(jnp.bfloat16)
        total = jnp.sum(weight, axis=1, keepdims=True)
        denominators[s] += jnp.where(lane == r, total, 0.0)
    for r, s in cases:
        num[s, pl.ds(r, both, stride=rows), :] = jnp.dot(
            weights[r, s], values[places[r][1], :, columns[s]], preferred_element_type=jnp.float32
        )
    for s in range(count):
        den[s] = denominators[s]
    store.wait()


def arrive_kernel(count, replicas, local_heads, slots, moves, table, kv, *refs):
    rows = table.shape[1]
    refs = list(refs)
    take = lambda n: [refs.pop(0) for _ in range(n)]
    pages_in, tokens_in, messages = take(replicas - 1), take(replicas - 1), take(count)
    num_in, den_in = take(2)
    outs = take(count - 1)
    own_num, own_den, num, den, wide = refs
    me, column = lax.axis_index("replica"), lax.axis_index("mp")
    page_size, width = pages_in[0].shape
    half_rows = local_heads * rows
    num[...] = num_in[...]
    den[...] = den_in[...]
    for s, message in enumerate(messages):
        wide[s] = message[half_rows : 2 * half_rows, :].astype(jnp.float32)
    lane = lax.broadcasted_iota(jnp.int32, (local_heads, HD), 1)
    token = lax.broadcasted_iota(jnp.int32, (local_heads, page_size), 1)
    columns = [head_columns(partner("mp", s), local_heads) for s in range(count)]
    cases = [(d, s) for d in range(1, replicas) for s in range(count)]
    arrivals = [pair_row(moves, partner("replica", d), me, rows, 1) for d in range(1, replicas)]
    scores, weights, totals = {}, {}, {}
    for d, s in cases:
        row = arrivals[d - 1][1]
        q = wide[s, pl.ds(row, local_heads, stride=rows), :].astype(jnp.bfloat16)
        scores[d, s] = scores_of(q, pages_in[d - 1].at[:, pl.ds(0, width // 2)][:, columns[s]])
    for d, s in cases:
        index, _ = locate(table, arrivals[d - 1][1], column, slots)
        inside = (token + index * page_size).astype(jnp.float32) < tokens_in[d - 1][2:3, :]
        weight = jnp.where(inside, weight_of(scores[d, s]), 0.0)
        weights[d, s] = weight.astype(jnp.bfloat16)
        totals[d, s] = jnp.sum(weight, axis=1, keepdims=True)
    for d, s in cases:
        values = pages_in[d - 1].at[:, pl.ds(width // 2, width // 2)][:, columns[s]]
        scores[d, s] = jnp.dot(weights[d, s], values, preferred_element_type=jnp.float32)
    for d, (valid, row) in enumerate(arrivals, 1):

        @pl.when(valid == 1)
        def _(d=d, row=row):
            for s in range(count):
                num[s, pl.ds(half_rows + row, local_heads, stride=rows), :] = scores[d, s]
                old = den[s, pl.ds(local_heads, local_heads), :]
                den[s, pl.ds(local_heads, local_heads), :] = jnp.where(lane == row, totals[d, s], old)

    own_num[...] = num[0]
    own_den[...] = den[0]
    filler = jnp.zeros((KV_ROWS - 2 * rows - (replicas - 1), HD), jnp.float32)
    all_kv = []
    for half in range(2):
        all_kv += [kv[half]] + [arrived[half : half + 1, :] for arrived in tokens_in] + [filler]
    all_kv = jnp.concatenate(all_kv, axis=0)
    for s, out in enumerate(outs):
        at = s + 1
        parts = den[at]
        high = parts.astype(SEND).astype(jnp.float32)
        parts = high + pltpu.roll(parts - high, HD // 2, 1)
        out[...] = jnp.concatenate([num[at], parts, all_kv], axis=0).astype(SEND)


def finish_kernel(count, replicas, local_heads, moves, table, lengths, kv, q, num, den, *refs):
    refs = list(refs)
    take = lambda n: [refs.pop(0) for _ in range(n)]
    pages_in, tokens_in, messages = take(replicas - 1), take(replicas - 1), take(count - 1)
    pool_raw, _, first, second, pool = take(5)
    held, full, windows, page_sems, read_sems, write_sems = refs
    me, column = lax.axis_index("replica"), lax.axis_index("mp")
    rows = lengths.shape[0]
    slots, page_size, width = pool_raw.shape
    both = 2 * local_heads

    arrivals, copies, kept, plans = [], [], [jnp.bool_(True)] * rows, []

    def add_plan(active, row, length, first_token, source, r=None):
        index, slot = locate(table, row, column, slots)
        at = length - index * page_size
        touched = active & (at >= -1) & (at < page_size)
        start = jnp.clip(at, 0, page_size - WINDOW) & -16
        span = pl.ds(pl.multiple_of(start, 16), WINDOW)
        n = len(plans)
        source = source.at[slot] if r is not None else source
        read = pltpu.make_async_copy(source.at[span], windows.at[n], read_sems.at[n])
        write = pltpu.make_async_copy(windows.at[n], pool.at[slot, span], write_sems.at[n])
        plans.append((touched, read, write, first_token, rows + row, at - start))
        pl.when(touched)(read.start)
        return slot

    for s, page in enumerate(pages_in):
        valid, row = pair_row(moves, partner("replica", s + 1), me, rows, 1)
        valid = valid == 1
        length = jnp.max(tokens_in[s][2:3, :]).astype(jnp.int32)
        slot = add_plan(valid, row, length, 2 * rows + s, page)
        copies.append(pltpu.make_async_copy(page, pool.at[slot], page_sems.at[s]))
        pl.when(valid)(copies[-1].start)
        arrivals.append((valid, row))
        kept = [stays & ~(valid & (row == r)) for r, stays in enumerate(kept)]
    for r in range(rows):
        add_plan(kept[r], r, lengths[r], r, pool_raw, r)

    for half in range(2):
        held[half] = kv[half, :rows, :]
        for s, (valid, row) in enumerate(arrivals):

            @pl.when(valid)
            def _(half=half, s=s, row=row):
                held[half, pl.ds(row, 1), :] = tokens_in[s][half : half + 1, :]

    query_rows = both * rows
    kv_base = messages[0].shape[0] - 2 * KV_ROWS
    filler = jnp.zeros((KV_ROWS - 2 * rows - (replicas - 1), HD), jnp.float32)
    for s in range(count):
        device = partner("mp", s)
        for half in range(2):
            if s == 0:
                chunk = jnp.concatenate(
                    [kv[half]] + [arrived[half : half + 1, :] for arrived in tokens_in] + [filler],
                    axis=0,
                )
            else:
                start = kv_base + half * KV_ROWS
                chunk = messages[s - 1][start : start + KV_ROWS, :].astype(jnp.float32)

            def place(half=half, device=device, chunk=chunk):
                columns = head_columns(device, local_heads)
                full.at[:, pl.ds(half * (width // 2), width // 2)][:, columns] = chunk

            if local_heads == GROUP:
                place()
            else:
                pl.when(split(device * local_heads, GROUP)[1] == 0)(place)

    sums = den[...]
    for message in messages:
        part = message[query_rows : query_rows + both, :].astype(jnp.float32)
        sums += part + pltpu.roll(part, HD // 2, 1)
    sums = jnp.transpose(sums)[:rows, :]
    for step, out in enumerate((first, second)):
        results = []
        for h in range(local_heads):
            at = (step * local_heads + h) * rows
            query = q[at : at + rows, :].astype(jnp.float32)
            numerator = num[at : at + rows, :]
            for message in messages:
                numerator += message[at : at + rows, :].astype(jnp.float32)
            denominator = sums[:, step * local_heads + h : step * local_heads + h + 1]
            extra = [(kv[0, :rows, :], kv[1, :rows, :])]
            if step == 1:
                extra = [(held[0], held[1]), (kv[0, rows:, :], kv[1, rows:, :])]
            for key, value in extra:
                weight = weight_of(jnp.sum(query * key, axis=1, keepdims=True))
                numerator += weight.astype(jnp.bfloat16).astype(jnp.float32) * value
                denominator += weight
            results.append(numerator / denominator)
        out[...] = jnp.concatenate(results, axis=1).astype(out.dtype)

    for (valid, _), copy in zip(arrivals, copies):
        pl.when(valid)(copy.wait)
    place_ids = lax.broadcasted_iota(jnp.int32, (WINDOW, width), 0)
    for n, (touched, read, write, token, next_token, offset) in enumerate(plans):

        @pl.when(touched)
        def _(n=n, read=read, write=write, token=token, next_token=next_token, offset=offset):
            read.wait()
            old = windows[n].astype(jnp.float32)
            new = jnp.where(place_ids == offset, full[pl.ds(token, 1), :], old)
            new = jnp.where(place_ids == offset + 1, full[pl.ds(next_token, 1), :], new)
            windows[n] = new.astype(jnp.bfloat16)
            write.start()

    for touched, _, write, _, _, _ in plans:
        pl.when(touched)(write.wait)


def params(megabytes=32, **rest):
    return pltpu.CompilerParams(vmem_limit_bytes=megabytes << 20, **rest)


def body(layer_input, kv_weight, queries, kv_pool, lengths, block_table, new_table, migrations):
    replicas, count = lax.axis_size("replica"), lax.axis_size("mp")
    rows = lengths.shape[0]
    pool = kv_pool[0, 0]
    slots, page_size, width = pool.shape
    local_heads = queries.shape[2] // HD
    both = 2 * local_heads
    query_rows = both * rows
    depth = layer_input.shape[2]
    f32, bf16 = jnp.float32, jnp.bfloat16
    moves, old_table, table_after = migrations.T, block_table.T, new_table.T
    shape = jax.ShapeDtypeStruct

    leaving = pl.pallas_call(
        functools.partial(leave_kernel, rows),
        out_shape=[shape((page_size, width), bf16)] * (replicas - 1),
        in_specs=[SMEM, SMEM, HBM],
        out_specs=[ANY] * (replicas - 1),
        scratch_shapes=[pltpu.SemaphoreType.DMA((replicas - 1,))],
        compiler_params=params(),
        name="leave",
    )(moves, old_table, pool)
    pages_in = exchange(leaving, "replica")

    block = math.gcd(depth, 512)
    message_rows = query_rows + 8 * rows
    sent = pl.pallas_call(
        functools.partial(project_kernel, count, local_heads),
        grid=(depth // block,),
        out_shape=[shape((message_rows, HD), bf16)] * count,
        in_specs=[
            pl.BlockSpec((2 * rows, block), lambda k: (0, k)),
            pl.BlockSpec((block, width), lambda k: (k, 0), memory_space=pltpu.VMEM),
            pl.BlockSpec(queries.shape, lambda k: (0, 0, 0)),
        ],
        out_specs=[pl.BlockSpec((message_rows, HD), lambda k: (0, 0))] * count,
        scratch_shapes=[pltpu.VMEM((2 * rows, width), f32)],
        compiler_params=params(),
        name="project",
    )(layer_input.reshape(2 * rows, depth), kv_weight, queries)
    sent, pages_in[0] = lax.optimization_barrier((sent, pages_in[0]))
    messages = [sent[0]] + exchange(sent[1:], "mp")

    kv, *tokens = pl.pallas_call(
        functools.partial(token_kernel, count, replicas, rows),
        out_shape=[shape((2, 2 * rows, HD), f32)] + [shape((8, HD), f32)] * (replicas - 1),
        in_specs=[SMEM, SMEM] + [VMEM] * count,
        out_specs=[VMEM] * replicas,
        compiler_params=params(),
        name="token",
    )(moves, lengths, *messages)
    tokens_in = exchange(tokens, "replica")

    num, den, pool_copy = pl.pallas_call(
        functools.partial(attend_kernel, count, local_heads),
        out_shape=[
            shape((count, query_rows, HD), f32),
            shape((count, both, HD), f32),
            shape(pool.shape, bf16),
        ],
        in_specs=[SMEM, SMEM, VMEM] + [VMEM] * count,
        out_specs=[VMEM, VMEM, ANY],
        scratch_shapes=[
            pltpu.VMEM((count, query_rows, HD), f32),
            pltpu.SemaphoreType.DMA(()),
        ],
        compiler_params=params(),
        name="attend",
    )(old_table, lengths, pool, *messages)

    sum_rows = query_rows + both + 2 * KV_ROWS
    *sums, num, den = pl.pallas_call(
        functools.partial(arrive_kernel, count, replicas, local_heads, slots),
        out_shape=[shape((sum_rows, HD), SEND)] * (count - 1)
        + [shape((query_rows, HD), f32), shape((both, HD), f32)],
        in_specs=[SMEM, SMEM, VMEM]
        + [VMEM] * (replicas - 1)
        + [VMEM] * (replicas - 1)
        + [VMEM] * count
        + [VMEM] * 2,
        out_specs=[VMEM] * (count + 1),
        scratch_shapes=[
            pltpu.VMEM((count, query_rows, HD), f32),
            pltpu.VMEM((count, both, HD), f32),
            pltpu.VMEM((count, query_rows // 2, HD), f32),
        ],
        compiler_params=params(),
        name="arrive",
    )(moves, table_after, kv, *pages_in, *tokens_in, *messages, num, den)
    sums_in = exchange(sums, "mp")

    first, second, pool_after = pl.pallas_call(
        functools.partial(finish_kernel, count, replicas, local_heads),
        out_shape=[
            shape((rows, local_heads * HD), bf16),
            shape((rows, local_heads * HD), bf16),
            shape(pool.shape, bf16),
        ],
        in_specs=[SMEM, SMEM, SMEM]
        + [VMEM] * 4
        + [ANY] * (replicas - 1)
        + [VMEM] * (replicas - 1)
        + [VMEM] * (count - 1)
        + [ANY, ANY],
        out_specs=[VMEM, VMEM, ANY],
        scratch_shapes=[
            pltpu.VMEM((2, rows, HD), f32),
            pltpu.VMEM((KV_ROWS, width), f32),
            pltpu.VMEM((rows + replicas - 1, WINDOW, width), bf16),
            pltpu.SemaphoreType.DMA((replicas - 1,)),
            pltpu.SemaphoreType.DMA((rows + replicas - 1,)),
            pltpu.SemaphoreType.DMA((rows + replicas - 1,)),
        ],
        input_output_aliases={7 + 2 * (replicas - 1) + (count - 1) + 1: 2},
        compiler_params=params(),
        name="finish",
    )(moves, table_after, lengths, kv, messages[0], num, den, *pages_in, *tokens_in, *sums_in, pool, pool_copy)
    return first, second, pool_after[None, None]


def solution(mesh):
    return jax.shard_map(
        body,
        mesh=mesh,
        in_specs=(
            P(None, ("groups", "replica"), "mp"),
            P("mp", None),
            P(None, ("groups", "replica"), "mp"),
            P(("groups", "replica"), "mp", None, None, None),
            P(("groups", "replica")),
            P(("groups", "replica"), None),
            P(("groups", "replica"), None),
            P("groups", None),
        ),
        out_specs=(
            P(("groups", "replica"), "mp"),
            P(("groups", "replica"), "mp"),
            P(("groups", "replica"), "mp", None, None, None),
        ),
        check_vma=False,
    )
```

```python
import functools
import math

import jax
import jax.numpy as jnp
from jax import lax
from jax.experimental import pallas as pl
from jax.experimental.pallas import tpu as pltpu
from jax.sharding import PartitionSpec as P

H = 32
KVH = 4
HD = 128
GROUP = H // KVH
CAP = 20.0
SCALE = 1.0 / math.sqrt(HD)
WINDOW = 32
KV_ROWS = 24
OPEN_MB = 32

SMEM = pl.BlockSpec(memory_space=pltpu.SMEM)
VMEM = pl.BlockSpec(memory_space=pltpu.VMEM)
ANY = pl.BlockSpec(memory_space=pl.ANY)
HBM = pl.BlockSpec(memory_space=pltpu.HBM)
SEND = jnp.bfloat16


def swap(value, axis, distance):
    size = lax.axis_size(axis)
    return lax.ppermute(value, axis, [(i, i ^ distance) for i in range(size)])


def exchange(messages, axis):
    received = [swap(messages[d], axis, d + 1) for d in reversed(range(len(messages)))]
    return received[::-1]


def partner(axis, distance):
    return lax.axis_index(axis) ^ distance


def split(value, size):
    if size & (size - 1) == 0:
        return lax.shift_right_logical(value, size.bit_length() - 1), value & (size - 1)
    return lax.div(value, size), lax.rem(value, size)


def count_up(limit, step, state):
    if limit > 8:
        return lax.fori_loop(0, limit, step, state)
    for i in range(limit):
        state = step(i, state)
    return state


def locate(table, row, column, slots):
    def step(p, found):
        device, slot = split(table[p, row], slots)
        here = device == column
        return jnp.where(here, p, found[0]), jnp.where(here, slot, found[1])

    return count_up(table.shape[0], step, (jnp.int32(0), jnp.int32(0)))


def pair_row(moves, source, target, rows, side):
    def step(j, found):
        ends = [split(moves[i, j], rows) for i in range(2)]
        match = (ends[0][0] == source) & (ends[1][0] == target)
        return (
            jnp.where(match, jnp.int32(1), found[0]),
            jnp.where(match, ends[side][1], found[1]),
        )

    return count_up(moves.shape[1], step, (jnp.int32(0), jnp.int32(0)))


def head_columns(device, local_heads):
    return pl.ds(pl.multiple_of(split(device * local_heads, GROUP)[0] * HD, HD), HD)


def weight_of(score):
    return jnp.exp(CAP * jnp.tanh(score * (SCALE / CAP)))


def open_kernel(count, replicas, local_heads, moves_all, table_all, x_all, q_all, weight, pool, *refs):
    outs, pages = refs[:count], refs[count : count + replicas - 1]
    held, x, q, moves, table, weight_sems, page_sems, rest_sems = refs[count + replicas - 1 :]
    me, column = lax.axis_index("replica"), lax.axis_index("mp")
    rows = q.shape[1]
    tokens, depth = x.shape
    chunks = weight_sems.shape[0]
    loads = []
    pairs = ((moves_all, moves), (table_all, table), (x_all, x), (q_all, q))
    rest = [pltpu.make_async_copy(*pair, rest_sems.at[i]) for i, pair in enumerate(pairs)]
    for copy in rest:
        copy.start()
    for c in range(chunks):
        span = pl.ds(c * (depth // chunks), depth // chunks)
        loads.append(pltpu.make_async_copy(weight.at[span], held.at[span], weight_sems.at[c]))
        loads[-1].start()
    copies = []
    for copy in rest[:2]:
        copy.wait()
    for s, page in enumerate(pages):
        _, row = pair_row(moves, me, partner("replica", s + 1), rows, 0)
        _, slot = locate(table, row, column, pool.shape[0])
        copies.append(pltpu.make_async_copy(pool.at[slot], page, page_sems.at[s]))
        copies[-1].start()

    for copy in rest[2:]:
        copy.wait()
    wide = [q[i].astype(jnp.float32) for i in range(2)]
    blocks = [wide[i][:, h * HD : (h + 1) * HD] for i in range(2) for h in range(local_heads)]
    packed = jnp.concatenate(blocks, axis=0).astype(jnp.bfloat16)
    query_rows = packed.shape[0]
    for out in outs:
        out[:query_rows, :] = packed
    total = jnp.zeros((tokens, held.shape[1]), jnp.float32)
    for c, load in enumerate(loads):
        load.wait()
        span = pl.ds(c * (depth // chunks), depth // chunks)
        total += jnp.dot(x[:, span], held[span, :], preferred_element_type=jnp.float32)
    for j in range(KVH):
        parts = []
        for half in range(2):
            start = (half * KVH + j) * HD
            part = total[:, start : start + HD]
            high = part.astype(jnp.bfloat16)
            parts += [high, (part - high.astype(jnp.float32)).astype(jnp.bfloat16)]
        parts = jnp.concatenate(parts, axis=0)
        for s, out in enumerate(outs):

            @pl.when(split(partner("mp", s) * local_heads, GROUP)[0] == j)
            def _(out=out, parts=parts):
                out[query_rows:, :] = parts

    for copy in copies:
        copy.wait()


def token_kernel(count, moves, lengths, *refs):
    messages, kv, outs = refs[:count][::-1], refs[count], refs[count + 1 :]
    rows = lengths.shape[0]
    tokens = 2 * rows
    base = messages[0].shape[0] - 4 * tokens
    me = lax.axis_index("replica")
    for half in range(2):
        total = jnp.zeros((tokens, HD), jnp.float32)
        for message in messages:
            start = base + 2 * half * tokens
            total += message[start : start + tokens, :].astype(jnp.float32)
            total += message[start + tokens : start + 2 * tokens, :].astype(jnp.float32)
        kv[half] = total.astype(jnp.bfloat16).astype(jnp.float32)
    sublane = lax.broadcasted_iota(jnp.int32, (8, HD), 0)
    for s, out in enumerate(outs):
        _, row = pair_row(moves, me, partner("replica", s + 1), rows, 0)
        value = jnp.full((8, HD), lengths[row], jnp.int32).astype(jnp.float32)
        for half in range(2):
            value = jnp.where(sublane == half, kv[half, pl.ds(row, 1), :], value)
        out[...] = value


def arrived_token(part):
    return part[0:1], part[1:2], part[2:3]


def scores_of(q, keys):
    return lax.dot_general(q, keys, (((1,), (1,)), ((), ())), preferred_element_type=jnp.float32)


def attend_kernel(count, local_heads, table, lengths, pool, *refs):
    messages = refs[:count][::-1]
    num, den, pool_out, wide, sem = refs[count:]
    column = lax.axis_index("mp")
    rows = lengths.shape[0]
    slots, page_size, width = pool.shape
    both = 2 * local_heads
    store = pltpu.make_async_copy(pool, pool_out, sem)
    store.start()
    for s, message in enumerate(messages):
        wide[s] = message[: both * rows, :].astype(jnp.float32)
    lane = lax.broadcasted_iota(jnp.int32, (both, HD), 1)
    token = lax.broadcasted_iota(jnp.int32, (both, page_size), 1)
    places = [locate(table, r, column, slots) for r in range(rows)]
    columns = [head_columns(partner("mp", s), local_heads) for s in range(count)]
    keys = pool.at[:, :, pl.ds(0, width // 2)]
    values = pool.at[:, :, pl.ds(width // 2, width // 2)]
    cases = [(r, s) for r in range(rows) for s in range(count)]
    scores = {}
    for r, s in cases:
        q = wide[s, pl.ds(r, both, stride=rows), :].astype(jnp.bfloat16)
        scores[r, s] = scores_of(q, keys[places[r][1], :, columns[s]])
    weights = {}
    denominators = [jnp.zeros((both, HD), jnp.float32) for _ in range(count)]
    for r, s in cases:
        inside = token < lengths[r] - places[r][0] * page_size
        weight = jnp.where(inside, weight_of(scores[r, s]), 0.0)
        weights[r, s] = weight.astype(jnp.bfloat16)
        total = jnp.sum(weight, axis=1, keepdims=True)
        denominators[s] += jnp.where(lane == r, total, 0.0)
    for r, s in cases:
        num[s, pl.ds(r, both, stride=rows), :] = jnp.dot(
            weights[r, s], values[places[r][1], :, columns[s]], preferred_element_type=jnp.float32
        )
    for s in range(count):
        den[s] = denominators[s]
    store.wait()


def arrive_kernel(count, replicas, local_heads, slots, *refs):
    refs = list(refs)
    take = lambda n: [refs.pop(0) for _ in range(n)]
    pages_in = take(replicas - 2)
    moves, table, kv = take(3)
    pages_in, tokens_in, messages = take(1) + pages_in, take(replicas - 1), take(count)[::-1]
    rows = table.shape[1]
    page_size, width = pages_in[0].shape
    tokens_in = [arrived_token(part) for part in tokens_in]
    num_in, den_in = take(2)
    outs = take(count - 1)
    own_num, own_den, num, den, wide = refs
    me, column = lax.axis_index("replica"), lax.axis_index("mp")
    half_rows = local_heads * rows
    num[...] = num_in[...]
    den[...] = den_in[...]
    for s, message in enumerate(messages):
        wide[s] = message[half_rows : 2 * half_rows, :].astype(jnp.float32)
    lane = lax.broadcasted_iota(jnp.int32, (local_heads, HD), 1)
    token = lax.broadcasted_iota(jnp.int32, (local_heads, page_size), 1)
    columns = [head_columns(partner("mp", s), local_heads) for s in range(count)]
    cases = [(d, s) for d in range(1, replicas) for s in range(count)]
    arrivals = [pair_row(moves, partner("replica", d), me, rows, 1) for d in range(1, replicas)]
    scores, weights, totals = {}, {}, {}
    for d, s in cases:
        row = arrivals[d - 1][1]
        q = wide[s, pl.ds(row, local_heads, stride=rows), :].astype(jnp.bfloat16)
        scores[d, s] = scores_of(q, pages_in[d - 1].at[:, pl.ds(0, width // 2)][:, columns[s]])
    for d, s in cases:
        index, _ = locate(table, arrivals[d - 1][1], column, slots)
        inside = (token + index * page_size).astype(jnp.float32) < tokens_in[d - 1][2]
        weight = jnp.where(inside, weight_of(scores[d, s]), 0.0)
        weights[d, s] = weight.astype(jnp.bfloat16)
        totals[d, s] = jnp.sum(weight, axis=1, keepdims=True)
    for d, s in cases:
        values = pages_in[d - 1].at[:, pl.ds(width // 2, width // 2)][:, columns[s]]
        scores[d, s] = jnp.dot(weights[d, s], values, preferred_element_type=jnp.float32)
    for d, (valid, row) in enumerate(arrivals, 1):

        @pl.when(valid == 1)
        def _(d=d, row=row):
            for s in range(count):
                num[s, pl.ds(half_rows + row, local_heads, stride=rows), :] = scores[d, s]
                old = den[s, pl.ds(local_heads, local_heads), :]
                den[s, pl.ds(local_heads, local_heads), :] = jnp.where(lane == row, totals[d, s], old)

    own_num[...] = num[0]
    own_den[...] = den[0]
    filler = jnp.zeros((KV_ROWS - 2 * rows - (replicas - 1), HD), jnp.float32)
    all_kv = []
    for half in range(2):
        all_kv += [kv[half]] + [arrived[half] for arrived in tokens_in] + [filler]
    all_kv = jnp.concatenate(all_kv, axis=0)
    for s, out in enumerate(outs):
        at = s + 1
        parts = den[at]
        high = parts.astype(SEND).astype(jnp.float32)
        parts = high + pltpu.roll(parts - high, HD // 2, 1)
        out[...] = jnp.concatenate([num[at], parts, all_kv], axis=0).astype(SEND)


def finish_kernel(count, replicas, local_heads, *refs):
    refs = list(refs)
    take = lambda n: [refs.pop(0) for _ in range(n)]
    pages_in = take(replicas - 2)
    moves, table, lengths, kv, q, num, den = take(7)
    pages_in, tokens_in, messages = take(1) + pages_in, take(replicas - 1), take(count - 1)[::-1]
    pool_raw, _, first, second, pool = take(5)
    tokens_in = [arrived_token(part) for part in tokens_in]
    held, full, windows, page_sems, read_sems, write_sems = refs
    me, column = lax.axis_index("replica"), lax.axis_index("mp")
    rows = lengths.shape[0]
    slots, page_size, width = pool_raw.shape
    both = 2 * local_heads

    arrivals, copies, kept, plans = [], [], [jnp.bool_(True)] * rows, []

    def add_plan(active, row, length, first_token, source, r=None):
        index, slot = locate(table, row, column, slots)
        at = length - index * page_size
        touched = active & (at >= -1) & (at < page_size)
        start = jnp.clip(at, 0, page_size - WINDOW) & -16
        span = pl.ds(pl.multiple_of(start, 16), WINDOW)
        n = len(plans)
        source = source.at[slot] if r is not None else source
        read = pltpu.make_async_copy(source.at[span], windows.at[n], read_sems.at[n])
        write = pltpu.make_async_copy(windows.at[n], pool.at[slot, span], write_sems.at[n])
        plans.append((touched, read, write, first_token, rows + row, at - start))
        pl.when(touched)(read.start)
        return slot

    for s, page in enumerate(pages_in):
        valid, row = pair_row(moves, partner("replica", s + 1), me, rows, 1)
        valid = valid == 1
        length = jnp.max(tokens_in[s][2]).astype(jnp.int32)
        slot = add_plan(valid, row, length, 2 * rows + s, page)
        copies.append(pltpu.make_async_copy(page, pool.at[slot], page_sems.at[s]))
        pl.when(valid)(copies[-1].start)
        arrivals.append((valid, row))
        kept = [stays & ~(valid & (row == r)) for r, stays in enumerate(kept)]
    for r in range(rows):
        add_plan(kept[r], r, lengths[r], r, pool_raw, r)

    for half in range(2):
        held[half] = kv[half, :rows, :]
        for s, (valid, row) in enumerate(arrivals):

            @pl.when(valid)
            def _(half=half, s=s, row=row):
                held[half, pl.ds(row, 1), :] = tokens_in[s][half]

    query_rows = both * rows
    kv_base = messages[0].shape[0] - 2 * KV_ROWS
    filler = jnp.zeros((KV_ROWS - 2 * rows - (replicas - 1), HD), jnp.float32)
    for s in range(count):
        device = partner("mp", s)
        for half in range(2):
            if s == 0:
                chunk = jnp.concatenate(
                    [kv[half]] + [arrived[half] for arrived in tokens_in] + [filler],
                    axis=0,
                )
            else:
                start = kv_base + half * KV_ROWS
                chunk = messages[s - 1][start : start + KV_ROWS, :].astype(jnp.float32)

            def place(half=half, device=device, chunk=chunk):
                columns = head_columns(device, local_heads)
                full.at[:, pl.ds(half * (width // 2), width // 2)][:, columns] = chunk

            if local_heads == GROUP:
                place()
            else:
                pl.when(split(device * local_heads, GROUP)[1] == 0)(place)

    sums = den[...]
    for message in messages:
        part = message[query_rows : query_rows + both, :].astype(jnp.float32)
        sums += part + pltpu.roll(part, HD // 2, 1)
    sums = jnp.transpose(sums)[:rows, :]
    for step, out in enumerate((first, second)):
        results = []
        for h in range(local_heads):
            at = (step * local_heads + h) * rows
            query = q[at : at + rows, :].astype(jnp.float32)
            numerator = num[at : at + rows, :]
            for message in messages:
                numerator += message[at : at + rows, :].astype(jnp.float32)
            denominator = sums[:, step * local_heads + h : step * local_heads + h + 1]
            extra = [(kv[0, :rows, :], kv[1, :rows, :])]
            if step == 1:
                extra = [(held[0], held[1]), (kv[0, rows:, :], kv[1, rows:, :])]
            for key, value in extra:
                weight = weight_of(jnp.sum(query * key, axis=1, keepdims=True))
                numerator += weight.astype(jnp.bfloat16).astype(jnp.float32) * value
                denominator += weight
            results.append(numerator / denominator)
        out[...] = jnp.concatenate(results, axis=1).astype(out.dtype)

    for (valid, _), copy in zip(arrivals, copies):
        pl.when(valid)(copy.wait)
    place_ids = lax.broadcasted_iota(jnp.int32, (WINDOW, width), 0)
    for n, (touched, read, write, token, next_token, offset) in enumerate(plans):

        @pl.when(touched)
        def _(n=n, read=read, write=write, token=token, next_token=next_token, offset=offset):
            read.wait()
            old = windows[n].astype(jnp.float32)
            new = jnp.where(place_ids == offset, full[pl.ds(token, 1), :], old)
            new = jnp.where(place_ids == offset + 1, full[pl.ds(next_token, 1), :], new)
            windows[n] = new.astype(jnp.bfloat16)
            write.start()

    for touched, _, write, _, _, _ in plans:
        pl.when(touched)(write.wait)


def cost(microseconds):
    return pl.CostEstimate(flops=0, transcendentals=0, bytes_accessed=int(microseconds * 3.5e6))


def in_hbm(value):
    return pltpu.with_memory_space_constraint(value, pltpu.HBM)


def params(megabytes=32, **rest):
    return pltpu.CompilerParams(vmem_limit_bytes=megabytes << 20, **rest)


def body(layer_input, kv_weight, queries, kv_pool, lengths, block_table, new_table, migrations):
    replicas, count = lax.axis_size("replica"), lax.axis_size("mp")
    rows = lengths.shape[0]
    pool = kv_pool[0, 0]
    slots, page_size, width = pool.shape
    local_heads = queries.shape[2] // HD
    both = 2 * local_heads
    query_rows = both * rows
    depth = layer_input.shape[2]
    f32, bf16 = jnp.float32, jnp.bfloat16
    moves, old_table, table_after = migrations.T, block_table.T, new_table.T
    shape = jax.ShapeDtypeStruct

    message_rows = query_rows + 8 * rows
    chunks = 8
    sent = pl.pallas_call(
        functools.partial(open_kernel, count, replicas, local_heads),
        out_shape=[shape((message_rows, HD), bf16)] * count
        + [shape((page_size, width), bf16)] * (replicas - 1),
        in_specs=[HBM] * 6,
        out_specs=[VMEM] * count + [ANY] * (replicas - 1),
        scratch_shapes=[
            pltpu.VMEM((depth, width), bf16),
            pltpu.VMEM((2 * rows, depth), bf16),
            pltpu.VMEM(queries.shape, bf16),
            pltpu.SMEM(moves.shape, jnp.int32),
            pltpu.SMEM(old_table.shape, jnp.int32),
            pltpu.SemaphoreType.DMA((chunks,)),
            pltpu.SemaphoreType.DMA((replicas - 1,)),
            pltpu.SemaphoreType.DMA((4,)),
        ],
        compiler_params=params(OPEN_MB),
        cost_estimate=cost(2.8),
        name="open",
    )(*map(in_hbm, (moves, old_table, layer_input.reshape(2 * rows, depth), queries, kv_weight, pool)))
    sent, leaving = list(sent[:count]), list(sent[count:])
    messages = [sent[0]] + exchange(sent[1:], "mp")
    pages_in = [swap(page, "replica", d + 1) for d, page in enumerate(leaving) if d > 0]

    kv, *tokens = pl.pallas_call(
        functools.partial(token_kernel, count),
        out_shape=[shape((2, 2 * rows, HD), f32)] + [shape((8, HD), f32)] * (replicas - 1),
        in_specs=[SMEM, SMEM] + [VMEM] * count,
        out_specs=[VMEM] * replicas,
        compiler_params=params(),
        cost_estimate=cost(0.6),
        name="token",
    )(moves, lengths, *messages[::-1])
    tokens_in = exchange(tokens, "replica")

    num, den, pool_copy = pl.pallas_call(
        functools.partial(attend_kernel, count, local_heads),
        out_shape=[
            shape((count, query_rows, HD), f32),
            shape((count, both, HD), f32),
            shape(pool.shape, bf16),
        ],
        in_specs=[SMEM, SMEM, VMEM] + [VMEM] * count,
        out_specs=[VMEM, VMEM, ANY],
        scratch_shapes=[
            pltpu.VMEM((count, query_rows, HD), f32),
            pltpu.SemaphoreType.DMA(()),
        ],
        compiler_params=params(),
        cost_estimate=cost(2.7),
        name="attend",
    )(old_table, lengths, pool, *messages[::-1])

    near, num = lax.optimization_barrier((leaving[0], num))
    pages_in.insert(0, swap(near, "replica", 1))

    sum_rows = query_rows + both + 2 * KV_ROWS
    *sums, num, den = pl.pallas_call(
        functools.partial(arrive_kernel, count, replicas, local_heads, slots),
        out_shape=[shape((sum_rows, HD), SEND)] * (count - 1)
        + [shape((query_rows, HD), f32), shape((both, HD), f32)],
        in_specs=[VMEM] * (replicas - 2)
        + [SMEM, SMEM, VMEM]
        + [VMEM] * replicas
        + [VMEM] * count
        + [VMEM] * 2,
        out_specs=[VMEM] * (count + 1),
        scratch_shapes=[
            pltpu.VMEM((count, query_rows, HD), f32),
            pltpu.VMEM((count, both, HD), f32),
            pltpu.VMEM((count, query_rows // 2, HD), f32),
        ],
        compiler_params=params(),
        cost_estimate=cost(1.2),
        name="arrive",
    )(*pages_in[1:], moves, table_after, kv, pages_in[0], *tokens_in, *messages[::-1], num, den)
    sums_in = exchange(sums, "mp")

    first, second, pool_after = pl.pallas_call(
        functools.partial(finish_kernel, count, replicas, local_heads),
        out_shape=[
            shape((rows, local_heads * HD), bf16),
            shape((rows, local_heads * HD), bf16),
            shape(pool.shape, bf16),
        ],
        in_specs=[VMEM] * (replicas - 2)
        + [SMEM, SMEM, SMEM]
        + [VMEM] * 4
        + [VMEM] * replicas
        + [VMEM] * (count - 1)
        + [ANY, ANY],
        out_specs=[VMEM, VMEM, ANY],
        scratch_shapes=[
            pltpu.VMEM((2, rows, HD), f32),
            pltpu.VMEM((KV_ROWS, width), f32),
            pltpu.VMEM((rows + replicas - 1, WINDOW, width), bf16),
            pltpu.SemaphoreType.DMA((replicas - 1,)),
            pltpu.SemaphoreType.DMA((rows + replicas - 1,)),
            pltpu.SemaphoreType.DMA((rows + replicas - 1,)),
        ],
        input_output_aliases={7 + 2 * replicas - 2 + (count - 1) + 1: 2},
        compiler_params=params(),
        cost_estimate=cost(3.4),
        name="finish",
    )(*pages_in[1:], moves, table_after, lengths, kv, messages[0], num, den, pages_in[0], *tokens_in, *sums_in[::-1], pool, pool_copy)
    return first, second, pool_after[None, None]


def solution(mesh):
    return jax.shard_map(
        body,
        mesh=mesh,
        in_specs=(
            P(None, ("groups", "replica"), "mp"),
            P("mp", None),
            P(None, ("groups", "replica"), "mp"),
            P(("groups", "replica"), "mp", None, None, None),
            P(("groups", "replica")),
            P(("groups", "replica"), None),
            P(("groups", "replica"), None),
            P("groups", None),
        ),
        out_specs=(
            P(("groups", "replica"), "mp"),
            P(("groups", "replica"), "mp"),
            P(("groups", "replica"), "mp", None, None, None),
        ),
        check_vma=False,
    )
```

```python
import functools
import math

import jax
import jax.numpy as jnp
from jax import lax
from jax.experimental import pallas as pl
from jax.experimental.pallas import tpu as pltpu
from jax.sharding import PartitionSpec as P

H = 32
KVH = 4
HD = 128
GROUP = H // KVH
CAP = 20.0
SCALE = 1.0 / math.sqrt(HD)
WINDOW = 32
KV_ROWS = 24
EXTRA = 8

SMEM = pl.BlockSpec(memory_space=pltpu.SMEM)
VMEM = pl.BlockSpec(memory_space=pltpu.VMEM)
ANY = pl.BlockSpec(memory_space=pl.ANY)
HBM = pl.BlockSpec(memory_space=pltpu.HBM)
SEND = jnp.bfloat16


def swap(value, axis, distance):
    size = lax.axis_size(axis)
    return lax.ppermute(value, axis, [(i, i ^ distance) for i in range(size)])


def exchange(messages, axis):
    received = [swap(messages[d], axis, d + 1) for d in reversed(range(len(messages)))]
    return received[::-1]


def partner(axis, distance):
    return lax.axis_index(axis) ^ distance


def split(value, size):
    if size & (size - 1) == 0:
        return lax.shift_right_logical(value, size.bit_length() - 1), value & (size - 1)
    return lax.div(value, size), lax.rem(value, size)


def count_up(limit, step, state):
    if limit > 8:
        return lax.fori_loop(0, limit, step, state)
    for i in range(limit):
        state = step(i, state)
    return state


def locate(table, row, column, slots):
    def step(p, found):
        device, slot = split(table[p, row], slots)
        here = device == column
        return jnp.where(here, p, found[0]), jnp.where(here, slot, found[1])

    return count_up(table.shape[0], step, (jnp.int32(0), jnp.int32(0)))


def pair_row(moves, source, target, rows, side):
    def step(j, found):
        valid, row, order, number = found
        ends = [split(moves[i, j], rows) for i in range(2)]
        match = (ends[0][0] == source) & (ends[1][0] == target)
        return (
            jnp.where(match, jnp.int32(1), valid),
            jnp.where(match, ends[side][1], row),
            jnp.where(match, number, order),
            number + jnp.where(ends[side][0] == (source, target)[side], 1, 0),
        )

    return count_up(moves.shape[1], step, (jnp.int32(0),) * 4)[:3]


def head_columns(device, local_heads):
    return pl.ds(pl.multiple_of(split(device * local_heads, GROUP)[0] * HD, HD), HD)


def weight_of(score):
    return jnp.exp(CAP * jnp.tanh(score * (SCALE / CAP)))


def pieces_of(depth, width):
    return [slice(at, min(at + width, depth)) for at in range(0, depth, width)]


def start_copies(pairs, sems):
    copies = [pltpu.make_async_copy(*pair, sems.at[i]) for i, pair in enumerate(pairs)]
    for copy in copies:
        copy.start()
    return copies


def wait_for(copies):
    for copy in copies:
        copy.wait()


def leave_kernel(rows, moves_all, table_all, lengths_all, x_all, pool, *refs):
    pages, (moves, table, lengths, x, sems, page_sems) = refs[:-6], refs[-6:]
    me, column = lax.axis_index("replica"), lax.axis_index("mp")
    page_size, width = pool.shape[1:]
    depth = x.shape[1]
    rest = start_copies(
        ((moves_all, moves), (table_all, table), (lengths_all, lengths), (x_all, x)), sems
    )
    wait_for(rest[:2])
    found = [pair_row(moves, me, partner("replica", s + 1), rows, 0)[1] for s in range(len(pages))]
    copies = start_copies(
        [
            (pool.at[locate(table, row, column, pool.shape[0])[1]], page.at[pl.ds(0, page_size)])
            for row, page in zip(found, pages)
        ],
        page_sems,
    )
    wait_for(rest[2:])
    sublane = lax.broadcasted_iota(jnp.int32, (EXTRA, width), 0)
    first_rows = x[:rows, :].astype(jnp.float32)
    row_ids = lax.broadcasted_iota(jnp.int32, (rows, depth), 0)
    for row, page in zip(found, pages):
        high, low = split(lengths[row], 64)
        extra = jnp.where(sublane == 0, high, low).astype(jnp.float32)
        picked = jnp.sum(jnp.where(row_ids == row, first_rows, 0.0), axis=0, keepdims=True)
        for i, piece in enumerate(pieces_of(depth, width)):
            value = picked[:, piece]
            if value.shape[1] < width:
                value = jnp.concatenate([value, jnp.zeros((1, width - value.shape[1]), jnp.float32)], axis=1)
            extra = jnp.where(sublane == 2 + i, value, extra)
        page[page_size:, :] = extra.astype(jnp.bfloat16)
    wait_for(copies)


def open_kernel(count, local_heads, x, q, weight, *outs):
    rows = q.shape[1]
    wide = [q[i].astype(jnp.float32) for i in range(2)]
    blocks = [wide[i][:, h * HD : (h + 1) * HD] for i in range(2) for h in range(local_heads)]
    packed = jnp.concatenate(blocks, axis=0).astype(jnp.bfloat16)
    query_rows = packed.shape[0]
    for out in outs:
        out[:query_rows, :] = packed
    total = jnp.dot(x[...], weight[...], preferred_element_type=jnp.float32)
    for j in range(KVH):
        parts = []
        for half in range(2):
            start = (half * KVH + j) * HD
            part = total[:, start : start + HD]
            high = part.astype(jnp.bfloat16)
            parts += [high, (part - high.astype(jnp.float32)).astype(jnp.bfloat16)]
        parts = jnp.concatenate(parts, axis=0)
        for s, out in enumerate(outs):

            @pl.when(split(partner("mp", s) * local_heads, GROUP)[0] == j)
            def _(out=out, parts=parts):
                out[query_rows:, :] = parts


def keep_kernel(pool, pool_out, sem):
    pltpu.make_async_copy(pool, pool_out, sem).start()
    pltpu.make_async_copy(pool, pool_out, sem).wait()


def length_of(page, page_size):
    part = page[page_size:, :HD].astype(jnp.float32)
    return part[0:1] * 64.0 + part[1:2]


def own_tokens(messages, rows, query_rows, half):
    tokens = 2 * rows
    start = query_rows + 2 * half * tokens
    total = jnp.zeros((tokens, HD), jnp.float32)
    for message in messages:
        total += message[start : start + tokens, :].astype(jnp.float32)
        total += message[start + tokens : start + 2 * tokens, :].astype(jnp.float32)
    return total.astype(jnp.bfloat16).astype(jnp.float32)


def scores_of(q, keys):
    return lax.dot_general(q, keys, (((1,), (1,)), ((), ())), preferred_element_type=jnp.float32)


def attend_kernel(count, local_heads, table, lengths, pool, *refs):
    messages = refs[:count][::-1]
    num, den, wide = refs[count:]
    column = lax.axis_index("mp")
    rows = lengths.shape[0]
    slots, page_size, width = pool.shape
    both = 2 * local_heads
    for s, message in enumerate(messages):
        wide[s] = message[: both * rows, :].astype(jnp.float32)
    lane = lax.broadcasted_iota(jnp.int32, (both, HD), 1)
    token = lax.broadcasted_iota(jnp.int32, (both, page_size), 1)
    places = [locate(table, r, column, slots) for r in range(rows)]
    columns = [head_columns(partner("mp", s), local_heads) for s in range(count)]
    keys = pool.at[:, :, pl.ds(0, width // 2)]
    values = pool.at[:, :, pl.ds(width // 2, width // 2)]
    cases = [(r, s) for r in range(rows) for s in range(count)]
    scores = {}
    for r, s in cases:
        q = wide[s, pl.ds(r, both, stride=rows), :].astype(jnp.bfloat16)
        scores[r, s] = scores_of(q, keys[places[r][1], :, columns[s]])
    weights = {}
    denominators = [jnp.zeros((both, HD), jnp.float32) for _ in range(count)]
    for r, s in cases:
        inside = token < lengths[r] - places[r][0] * page_size
        weight = jnp.where(inside, weight_of(scores[r, s]), 0.0)
        weights[r, s] = weight.astype(jnp.bfloat16)
        total = jnp.sum(weight, axis=1, keepdims=True)
        denominators[s] += jnp.where(lane == r, total, 0.0)
    for r, s in cases:
        num[s, pl.ds(r, both, stride=rows), :] = jnp.dot(
            weights[r, s], values[places[r][1], :, columns[s]], preferred_element_type=jnp.float32
        )
    for s in range(count):
        den[s] = denominators[s]


def arrive_kernel(count, replicas, local_heads, slots, *refs):
    refs = list(refs)
    take = lambda n: [refs.pop(0) for _ in range(n)]
    pages_in = take(replicas - 2)
    moves, table, projection = take(3)
    pages_in, messages = take(1) + pages_in, take(count)[::-1]
    num_in, den_in = take(2)
    outs = take(count - 1)
    own_num, own_den, own_kv, own_share, num, den, wide = refs
    me, column = lax.axis_index("replica"), lax.axis_index("mp")
    rows = table.shape[1]
    page_size, width = pages_in[0].shape[0] - EXTRA, pages_in[0].shape[1]
    half_rows = local_heads * rows
    num[...] = num_in[...]
    den[...] = den_in[...]
    for s, message in enumerate(messages):
        wide[s] = message[half_rows : 2 * half_rows, :].astype(jnp.float32)
    lane = lax.broadcasted_iota(jnp.int32, (local_heads, HD), 1)
    token = lax.broadcasted_iota(jnp.int32, (local_heads, page_size), 1)
    columns = [head_columns(partner("mp", s), local_heads) for s in range(count)]
    cases = [(d, s) for d in range(1, replicas) for s in range(count)]
    arrivals = [pair_row(moves, partner("replica", d), me, rows, 1) for d in range(1, replicas)]
    movers = moves.shape[1] // replicas
    scores, weights, totals = {}, {}, {}
    for d, s in cases:
        row = arrivals[d - 1][1]
        q = wide[s, pl.ds(row, local_heads, stride=rows), :].astype(jnp.bfloat16)
        keys = pages_in[d - 1].at[pl.ds(0, page_size), pl.ds(0, width // 2)]
        scores[d, s] = scores_of(q, keys[:, columns[s]])
    for d, s in cases:
        index, _ = locate(table, arrivals[d - 1][1], column, slots)
        length = length_of(pages_in[d - 1], page_size)
        inside = (token + index * page_size).astype(jnp.float32) < length
        weight = jnp.where(inside, weight_of(scores[d, s]), 0.0)
        weights[d, s] = weight.astype(jnp.bfloat16)
        totals[d, s] = jnp.sum(weight, axis=1, keepdims=True)
    for d, s in cases:
        values = pages_in[d - 1].at[pl.ds(0, page_size), pl.ds(width // 2, width // 2)]
        scores[d, s] = jnp.dot(weights[d, s], values[:, columns[s]], preferred_element_type=jnp.float32)
    for d, (valid, row, _) in enumerate(arrivals, 1):

        @pl.when(valid == 1)
        def _(d=d, row=row):
            for s in range(count):
                num[s, pl.ds(half_rows + row, local_heads, stride=rows), :] = scores[d, s]
                old = den[s, pl.ds(local_heads, local_heads), :]
                den[s, pl.ds(local_heads, local_heads), :] = jnp.where(lane == row, totals[d, s], old)

    own_num[...] = num[0]
    own_den[...] = den[0]
    depth = projection.shape[0]
    extra = [page[page_size:, :].astype(jnp.float32) for page in pages_in]
    inputs = [
        jnp.concatenate(
            [part[2 + i : 3 + i, : piece.stop - piece.start] for i, piece in enumerate(pieces_of(depth, width))],
            axis=1,
        )
        for part in extra
    ]
    inputs += [jnp.zeros((8 - len(inputs), depth), jnp.float32)]
    inputs = jnp.concatenate(inputs, axis=0).astype(jnp.bfloat16)
    share = jnp.dot(inputs, projection[...], preferred_element_type=jnp.float32)
    arrived = []
    for number in range(movers):
        row = jnp.zeros((1, width), jnp.float32)
        for d, (valid, _, order) in enumerate(arrivals):
            row = jnp.where((valid == 1) & (order == number), share[d : d + 1], row)
        part = jnp.concatenate([row[:, j * HD : (j + 1) * HD] for j in range(2 * KVH)], axis=0)
        high = part.astype(jnp.bfloat16).astype(jnp.float32)
        arrived += [high, part - high]
        own_share[number] = part
    all_kv = []
    for half in range(2):
        own_kv[half] = own_tokens(messages, rows, 2 * half_rows, half)
        all_kv.append(own_kv[half])
    filler = [jnp.zeros((-2 * local_heads % 16, HD), jnp.float32)] if local_heads % 8 else []
    for s, out in enumerate(outs):
        at = s + 1
        parts = den[at]
        high = parts.astype(SEND).astype(jnp.float32)
        parts = high + pltpu.roll(parts - high, HD // 2, 1)
        out[...] = jnp.concatenate([num[at], parts] + filler + all_kv + arrived, axis=0).astype(SEND)


def finish_kernel(count, replicas, local_heads, *refs):
    refs = list(refs)
    take = lambda n: [refs.pop(0) for _ in range(n)]
    pages_in = take(replicas - 2)
    moves_all, table_all, lengths_all, kv, share, q, num, den = take(8)
    pages_in, messages = take(1) + pages_in, take(count - 1)[::-1]
    pool_raw, _, first, second, pool = take(5)
    moves, table, lengths, held, full, arrived, windows, results, sems, page_sems, write_sems, out_sems = refs
    tables = start_copies(((moves_all, moves), (table_all, table), (lengths_all, lengths)), sems)
    me, column = lax.axis_index("replica"), lax.axis_index("mp")
    rows = lengths.shape[0]
    slots, page_size, width = pool_raw.shape
    both = 2 * local_heads
    query_rows = both * rows
    movers = moves.shape[1] // replicas
    head = split(column * local_heads, GROUP)[0]

    kv_base = messages[0].shape[0] - 4 * rows - 16 * movers
    for s in range(count):
        device = partner("mp", s)
        for half in range(2):
            if s == 0:
                chunk = kv[half]
            else:
                start = kv_base + half * 2 * rows
                chunk = messages[s - 1][start : start + 2 * rows, :].astype(jnp.float32)

            def place(half=half, device=device, chunk=chunk):
                columns = head_columns(device, local_heads)
                full.at[pl.ds(0, 2 * rows), pl.ds(half * (width // 2), width // 2)][:, columns] = chunk

            if local_heads == GROUP:
                place()
            else:
                pl.when(split(device * local_heads, GROUP)[1] == 0)(place)
    for number in range(movers):
        total = share[number]
        for message in messages:
            start = kv_base + 4 * rows + 16 * number
            part = message[start : start + 16, :].astype(jnp.float32)
            total += part[: 2 * KVH] + part[2 * KVH :]
        total = total.astype(jnp.bfloat16).astype(jnp.float32)
        arrived[number] = total
        for j in range(2 * KVH):
            full[2 * rows + number : 2 * rows + number + 1, j * HD : (j + 1) * HD] = total[j : j + 1, :]
    sums = den[...]
    for message in messages:
        part = message[query_rows : query_rows + both, :].astype(jnp.float32)
        sums += part + pltpu.roll(part, HD // 2, 1)
    sums = jnp.transpose(sums)[:rows, :]

    wait_for(tables)
    arrivals, copies, kept, plans = [], [], [jnp.bool_(True)] * rows, []

    def add_plan(active, row, length, first_token, source, r=None):
        index, slot = locate(table, row, column, slots)
        at = length - index * page_size
        touched = active & (at >= -1) & (at < page_size)
        start = jnp.clip(at, 0, page_size - WINDOW) & -16
        span = pl.ds(pl.multiple_of(start, 16), WINDOW)
        n = len(plans)
        source = source.at[slot] if r is not None else source
        write = pltpu.make_async_copy(windows.at[n], pool.at[slot, span], write_sems.at[n])
        plans.append((touched, source, span, write, first_token, rows + row, at - start))
        return slot

    for s, page in enumerate(pages_in):
        valid, row, order = pair_row(moves, partner("replica", s + 1), me, rows, 1)
        valid = valid == 1
        length = jnp.max(length_of(page, page_size)).astype(jnp.int32)
        page = page.at[pl.ds(0, page_size)]
        slot = add_plan(valid, row, length, 2 * rows + order, page)
        copies.append(pltpu.make_async_copy(page, pool.at[slot], page_sems.at[s]))
        pl.when(valid)(copies[-1].start)
        arrivals.append((valid, row, order))
        kept = [stays & ~(valid & (row == r)) for r, stays in enumerate(kept)]
    for r in range(rows):
        add_plan(kept[r], r, lengths[r], r, pool_raw, r)

    for half in range(2):
        held[half] = kv[half, :rows, :]
        for valid, row, order in arrivals:

            @pl.when(valid)
            def _(half=half, row=row, order=order):
                held[half, pl.ds(row, 1), :] = arrived[order, pl.ds(head + half * KVH, 1), :]

    outs = []
    for step, out in enumerate((first, second)):
        pieces = []
        for h in range(local_heads):
            at = (step * local_heads + h) * rows
            query = q[at : at + rows, :].astype(jnp.float32)
            numerator = num[at : at + rows, :]
            for message in messages:
                numerator += message[at : at + rows, :].astype(jnp.float32)
            denominator = sums[:, step * local_heads + h : step * local_heads + h + 1]
            extra = [(kv[0, :rows, :], kv[1, :rows, :])]
            if step == 1:
                extra = [(held[0], held[1]), (kv[0, rows:, :], kv[1, rows:, :])]
            for key, value in extra:
                weight = weight_of(jnp.sum(query * key, axis=1, keepdims=True))
                numerator += weight.astype(jnp.bfloat16).astype(jnp.float32) * value
                denominator += weight
            pieces.append(numerator / denominator)
        results[step] = jnp.concatenate(pieces, axis=1).astype(out.dtype)
        outs.append(pltpu.make_async_copy(results.at[step], out, out_sems.at[step]))
        outs[-1].start()

    for (valid, _, _), copy in zip(arrivals, copies):
        pl.when(valid)(copy.wait)
    place_ids = lax.broadcasted_iota(jnp.int32, (WINDOW, width), 0)
    for n, (touched, source, span, write, token, next_token, offset) in enumerate(plans):

        @pl.when(touched)
        def _(n=n, source=source, span=span, write=write, token=token, next_token=next_token, offset=offset):
            old = source[span, :].astype(jnp.float32)
            new = jnp.where(place_ids == offset, full[pl.ds(token, 1), :], old)
            new = jnp.where(place_ids == offset + 1, full[pl.ds(next_token, 1), :], new)
            windows[n] = new.astype(jnp.bfloat16)
            write.start()

    for plan in plans:
        pl.when(plan[0])(plan[3].wait)
    wait_for(outs)


def cost(microseconds):
    return pl.CostEstimate(flops=0, transcendentals=0, bytes_accessed=int(microseconds * 3.5e6))


def in_vmem(value):
    return pltpu.with_memory_space_constraint(value, pltpu.VMEM)


def in_hbm(value):
    return pltpu.with_memory_space_constraint(value, pltpu.HBM)


def params(megabytes=32, **rest):
    return pltpu.CompilerParams(vmem_limit_bytes=megabytes << 20, **rest)


def body(layer_input, kv_weight, queries, kv_pool, lengths, block_table, new_table, migrations):
    replicas, count = lax.axis_size("replica"), lax.axis_size("mp")
    rows = lengths.shape[0]
    pool = kv_pool[0, 0]
    slots, page_size, width = pool.shape
    local_heads = queries.shape[2] // HD
    both = 2 * local_heads
    query_rows = both * rows
    depth = layer_input.shape[2]
    f32, bf16 = jnp.float32, jnp.bfloat16
    moves, old_table, table_after = migrations.T, block_table.T, new_table.T
    shape = jax.ShapeDtypeStruct

    message_rows = query_rows + 8 * rows
    movers = migrations.shape[0] // replicas
    inputs = layer_input.reshape(2 * rows, depth)
    leaving = pl.pallas_call(
        functools.partial(leave_kernel, rows),
        out_shape=[shape((page_size + EXTRA, width), bf16)] * (replicas - 1),
        in_specs=[HBM] * 5,
        out_specs=[VMEM] * (replicas - 1),
        scratch_shapes=[
            pltpu.SMEM(moves.shape, jnp.int32),
            pltpu.SMEM(old_table.shape, jnp.int32),
            pltpu.SMEM(lengths.shape, jnp.int32),
            pltpu.VMEM((2 * rows, depth), bf16),
            pltpu.SemaphoreType.DMA((4,)),
            pltpu.SemaphoreType.DMA((replicas - 1,)),
        ],
        compiler_params=params(),
        cost_estimate=cost(2.0),
        name="leave",
    )(*map(in_hbm, (moves, old_table, lengths, inputs, pool)))
    pages_in = exchange(leaving, "replica")

    weight_near, inputs_near, queries_near = map(in_vmem, (kv_weight, inputs, queries))
    sent = pl.pallas_call(
        functools.partial(open_kernel, count, local_heads),
        out_shape=[shape((message_rows, HD), bf16)] * count,
        in_specs=[VMEM] * 3,
        out_specs=[VMEM] * count,
        compiler_params=params(),
        cost_estimate=cost(1.2),
        name="open",
    )(inputs_near, queries_near, weight_near)
    sent, pages_in[0] = lax.optimization_barrier((list(sent), pages_in[0]))
    messages = [sent[0]] + exchange(sent[1:], "mp")

    pool_near = in_vmem(pool)
    pool_copy = pl.pallas_call(
        keep_kernel,
        out_shape=shape(pool.shape, bf16),
        in_specs=[VMEM],
        out_specs=ANY,
        scratch_shapes=[pltpu.SemaphoreType.DMA(())],
        compiler_params=params(),
        cost_estimate=cost(1.6),
        name="keep",
    )(pool_near)
    num, den = pl.pallas_call(
        functools.partial(attend_kernel, count, local_heads),
        out_shape=[shape((count, query_rows, HD), f32), shape((count, both, HD), f32)],
        in_specs=[SMEM, SMEM, VMEM] + [VMEM] * count,
        out_specs=[VMEM, VMEM],
        scratch_shapes=[pltpu.VMEM((count, query_rows, HD), f32)],
        compiler_params=params(),
        cost_estimate=cost(1.5),
        name="attend",
    )(old_table, lengths, pool_near, *messages[::-1])

    sum_rows = query_rows + -(-both // 16) * 16 + 4 * rows + 16 * movers
    *sums, num, den, kv, share = pl.pallas_call(
        functools.partial(arrive_kernel, count, replicas, local_heads, slots),
        out_shape=[shape((sum_rows, HD), SEND)] * (count - 1)
        + [shape((query_rows, HD), f32), shape((both, HD), f32)]
        + [shape((2, 2 * rows, HD), f32), shape((movers, 2 * KVH, HD), f32)],
        in_specs=[VMEM] * (replicas - 2)
        + [SMEM, SMEM, VMEM, VMEM]
        + [VMEM] * count
        + [VMEM] * 2,
        out_specs=[VMEM] * (count + 3),
        scratch_shapes=[
            pltpu.VMEM((count, query_rows, HD), f32),
            pltpu.VMEM((count, both, HD), f32),
            pltpu.VMEM((count, query_rows // 2, HD), f32),
        ],
        compiler_params=params(),
        cost_estimate=cost(1.2),
        name="arrive",
    )(*pages_in[1:], moves, table_after, weight_near, pages_in[0], *messages[::-1], num, den)
    sums_in = exchange(sums, "mp")

    first, second, pool_after = pl.pallas_call(
        functools.partial(finish_kernel, count, replicas, local_heads),
        out_shape=[
            shape((rows, local_heads * HD), bf16),
            shape((rows, local_heads * HD), bf16),
            shape(pool.shape, bf16),
        ],
        in_specs=[VMEM] * (replicas - 2) + [ANY] * 3 + [VMEM] * (6 + count - 1) + [VMEM, ANY],
        out_specs=[ANY] * 3,
        scratch_shapes=[
            pltpu.SMEM(moves.shape, jnp.int32),
            pltpu.SMEM(table_after.shape, jnp.int32),
            pltpu.SMEM(lengths.shape, jnp.int32),
            pltpu.VMEM((2, rows, HD), f32),
            pltpu.VMEM((KV_ROWS, width), f32),
            pltpu.VMEM((movers, 2 * KVH, HD), f32),
            pltpu.VMEM((rows + replicas - 1, WINDOW, width), bf16),
            pltpu.VMEM((2, rows, local_heads * HD), bf16),
            pltpu.SemaphoreType.DMA((3,)),
            pltpu.SemaphoreType.DMA((replicas - 1,)),
            pltpu.SemaphoreType.DMA((rows + replicas - 1,)),
            pltpu.SemaphoreType.DMA((2,)),
        ],
        input_output_aliases={8 + replicas - 1 + (count - 1) + 1: 2},
        compiler_params=params(),
        cost_estimate=cost(2.5),
        name="finish",
    )(
        *pages_in[1:],
        *(moves, table_after, lengths),
        *(kv, share, messages[0], num, den, pages_in[0]),
        *sums_in[::-1],
        *(pool_near, pool_copy),
    )
    return first, second, pool_after[None, None]


def solution(mesh):
    return jax.shard_map(
        body,
        mesh=mesh,
        in_specs=(
            P(None, ("groups", "replica"), "mp"),
            P("mp", None),
            P(None, ("groups", "replica"), "mp"),
            P(("groups", "replica"), "mp", None, None, None),
            P(("groups", "replica")),
            P(("groups", "replica"), None),
            P(("groups", "replica"), None),
            P("groups", None),
        ),
        out_specs=(
            P(("groups", "replica"), "mp"),
            P(("groups", "replica"), "mp"),
            P(("groups", "replica"), "mp", None, None, None),
        ),
        check_vma=False,
    )
```

```python
import functools
import math

import jax
import jax.numpy as jnp
from jax import lax
from jax.experimental import pallas as pl
from jax.experimental.pallas import tpu as pltpu
from jax.sharding import PartitionSpec as P

H = 32
KVH = 4
HD = 128
GROUP = H // KVH
CAP = 20.0
SCALE = 1.0 / math.sqrt(HD)
WINDOW = 32
KV_ROWS = 24
EXTRA = 8

SMEM = pl.BlockSpec(memory_space=pltpu.SMEM)
VMEM = pl.BlockSpec(memory_space=pltpu.VMEM)
ANY = pl.BlockSpec(memory_space=pl.ANY)
HBM = pl.BlockSpec(memory_space=pltpu.HBM)
SEND = jnp.bfloat16


def swap(value, axis, distance):
    size = lax.axis_size(axis)
    return lax.ppermute(value, axis, [(i, i ^ distance) for i in range(size)])


def exchange(messages, axis):
    received = [swap(messages[d], axis, d + 1) for d in reversed(range(len(messages)))]
    return received[::-1]


def start_order(count):
    return [count // 2] + [d for d in range(count - 1, 0, -1) if d != count // 2]


def by_start(values):
    own = len(values) & 1 ^ 1
    order = start_order(len(values) + 1 - own)
    return [values[d - 1 + own] for d in order] + list(values[:own])


def by_distance(values):
    own = len(values) & 1 ^ 1
    order = start_order(len(values) + 1 - own)
    return list(values[len(order) :]) + [values[order.index(d)] for d in range(1, len(order) + 1)]


def partner(axis, distance):
    return lax.axis_index(axis) ^ distance


def split(value, size):
    if size & (size - 1) == 0:
        return lax.shift_right_logical(value, size.bit_length() - 1), value & (size - 1)
    return lax.div(value, size), lax.rem(value, size)


def count_up(limit, step, state):
    if limit > 8:
        return lax.fori_loop(0, limit, step, state)
    for i in range(limit):
        state = step(i, state)
    return state


def locate(table, row, column, slots):
    def step(p, found):
        device, slot = split(table[p, row], slots)
        here = device == column
        return jnp.where(here, p, found[0]), jnp.where(here, slot, found[1])

    return count_up(table.shape[0], step, (jnp.int32(0), jnp.int32(0)))


def pair_row(moves, source, target, rows, side):
    def step(j, found):
        valid, row, order, number = found
        ends = [split(moves[i, j], rows) for i in range(2)]
        match = (ends[0][0] == source) & (ends[1][0] == target)
        return (
            jnp.where(match, jnp.int32(1), valid),
            jnp.where(match, ends[side][1], row),
            jnp.where(match, number, order),
            number + jnp.where(ends[side][0] == (source, target)[side], 1, 0),
        )

    return count_up(moves.shape[1], step, (jnp.int32(0),) * 4)[:3]


def head_columns(device, local_heads):
    return pl.ds(pl.multiple_of(split(device * local_heads, GROUP)[0] * HD, HD), HD)


def weight_of(score):
    return jnp.exp(CAP * jnp.tanh(score * (SCALE / CAP)))


def pieces_of(depth, width):
    return [slice(at, min(at + width, depth)) for at in range(0, depth, width)]


def start_copies(pairs, sems):
    copies = [pltpu.make_async_copy(*pair, sems.at[i]) for i, pair in enumerate(pairs)]
    for copy in copies:
        copy.start()
    return copies


def wait_for(copies):
    for copy in copies:
        copy.wait()


def leave_kernel(rows, moves_all, table_all, lengths_all, x_all, pool, *refs):
    pages, (moves, table, lengths, x, sems, page_sems) = refs[:-6], refs[-6:]
    me, column = lax.axis_index("replica"), lax.axis_index("mp")
    page_size, width = pool.shape[1:]
    depth = x.shape[1]
    rest = start_copies(
        ((moves_all, moves), (table_all, table), (lengths_all, lengths), (x_all, x)), sems
    )
    wait_for(rest[:2])
    found = [pair_row(moves, me, partner("replica", s + 1), rows, 0)[1] for s in range(len(pages))]
    copies = start_copies(
        [
            (pool.at[locate(table, row, column, pool.shape[0])[1]], page.at[pl.ds(0, page_size)])
            for row, page in zip(found, pages)
        ],
        page_sems,
    )
    wait_for(rest[2:])
    sublane = lax.broadcasted_iota(jnp.int32, (EXTRA, width), 0)
    first_rows = x[:rows, :].astype(jnp.float32)
    row_ids = lax.broadcasted_iota(jnp.int32, (rows, depth), 0)
    for row, page in zip(found, pages):
        high, low = split(lengths[row], 64)
        extra = jnp.where(sublane == 0, high, low).astype(jnp.float32)
        picked = jnp.sum(jnp.where(row_ids == row, first_rows, 0.0), axis=0, keepdims=True)
        for i, piece in enumerate(pieces_of(depth, width)):
            value = picked[:, piece]
            if value.shape[1] < width:
                value = jnp.concatenate([value, jnp.zeros((1, width - value.shape[1]), jnp.float32)], axis=1)
            extra = jnp.where(sublane == 2 + i, value, extra)
        page[page_size:, :] = extra.astype(jnp.bfloat16)
    wait_for(copies)


def open_kernel(count, local_heads, x, q, weight, *outs):
    rows = q.shape[1]
    wide = [q[i].astype(jnp.float32) for i in range(2)]
    blocks = [wide[i][:, h * HD : (h + 1) * HD] for i in range(2) for h in range(local_heads)]
    packed = jnp.concatenate(blocks, axis=0).astype(jnp.bfloat16)
    query_rows = packed.shape[0]
    for out in outs:
        out[:query_rows, :] = packed
    total = jnp.dot(x[...], weight[...], preferred_element_type=jnp.float32)
    for j in range(KVH):
        parts = []
        for half in range(2):
            start = (half * KVH + j) * HD
            part = total[:, start : start + HD]
            high = part.astype(jnp.bfloat16)
            parts += [high, (part - high.astype(jnp.float32)).astype(jnp.bfloat16)]
        parts = jnp.concatenate(parts, axis=0)
        for s, out in enumerate(outs):

            @pl.when(split(partner("mp", s) * local_heads, GROUP)[0] == j)
            def _(out=out, parts=parts):
                out[query_rows:, :] = parts


def keep_kernel(replicas, *refs):
    pages_in, (pool, moves_all, table_all, pool_out, moves, table, sems, page_sems) = (
        refs[: replicas - 1],
        refs[replicas - 1 :],
    )
    wait_for(start_copies(((moves_all, moves), (table_all, table)), sems))
    me, column = lax.axis_index("replica"), lax.axis_index("mp")
    rows = table.shape[1]
    slots, page_size, _ = pool.shape
    kept, copies = [jnp.bool_(True)] * rows, []
    for s, page in enumerate(pages_in):
        valid, row, _ = pair_row(moves, partner("replica", s + 1), me, rows, 1)
        kept = [stays & ~((valid == 1) & (row == r)) for r, stays in enumerate(kept)]
        copies.append((valid == 1, row, lambda slot, page=page: page.at[pl.ds(0, page_size)]))
    copies += [(stays, r, lambda slot: pool.at[slot]) for r, stays in enumerate(kept)]
    started = []
    for n, (active, row, source) in enumerate(copies):
        _, slot = locate(table, row, column, slots)
        copy = pltpu.make_async_copy(source(slot), pool_out.at[slot], page_sems.at[n])
        started.append((active, copy))
        pl.when(active)(copy.start)
    for active, copy in started:
        pl.when(active)(copy.wait)


def length_of(page, page_size):
    part = page[page_size:, :HD].astype(jnp.float32)
    return part[0:1] * 64.0 + part[1:2]


def own_tokens(messages, rows, query_rows, half):
    tokens = 2 * rows
    start = query_rows + 2 * half * tokens
    total = jnp.zeros((tokens, HD), jnp.float32)
    for message in messages:
        total += message[start : start + tokens, :].astype(jnp.float32)
        total += message[start + tokens : start + 2 * tokens, :].astype(jnp.float32)
    return total.astype(jnp.bfloat16).astype(jnp.float32)


def scores_of(q, keys):
    return lax.dot_general(q, keys, (((1,), (1,)), ((), ())), preferred_element_type=jnp.float32)


def attend_kernel(count, local_heads, table, lengths, pool, *refs):
    messages = by_distance(refs[:count])
    num, den, wide = refs[count:]
    column = lax.axis_index("mp")
    rows = lengths.shape[0]
    slots, page_size, width = pool.shape
    both = 2 * local_heads
    for s, message in enumerate(messages):
        wide[s] = message[: both * rows, :].astype(jnp.float32)
    lane = lax.broadcasted_iota(jnp.int32, (both, HD), 1)
    token = lax.broadcasted_iota(jnp.int32, (both, page_size), 1)
    places = [locate(table, r, column, slots) for r in range(rows)]
    columns = [head_columns(partner("mp", s), local_heads) for s in range(count)]
    keys = pool.at[:, :, pl.ds(0, width // 2)]
    values = pool.at[:, :, pl.ds(width // 2, width // 2)]
    cases = [(r, s) for r in range(rows) for s in range(count)]
    scores = {}
    for r, s in cases:
        q = wide[s, pl.ds(r, both, stride=rows), :].astype(jnp.bfloat16)
        scores[r, s] = scores_of(q, keys[places[r][1], :, columns[s]])
    weights = {}
    denominators = [jnp.zeros((both, HD), jnp.float32) for _ in range(count)]
    for r, s in cases:
        inside = token < lengths[r] - places[r][0] * page_size
        weight = jnp.where(inside, weight_of(scores[r, s]), 0.0)
        weights[r, s] = weight.astype(jnp.bfloat16)
        total = jnp.sum(weight, axis=1, keepdims=True)
        denominators[s] += jnp.where(lane == r, total, 0.0)
    for r, s in cases:
        num[s, pl.ds(r, both, stride=rows), :] = jnp.dot(
            weights[r, s], values[places[r][1], :, columns[s]], preferred_element_type=jnp.float32
        )
    for s in range(count):
        den[s] = denominators[s]


def arrive_kernel(count, replicas, local_heads, slots, *refs):
    refs = list(refs)
    take = lambda n: [refs.pop(0) for _ in range(n)]
    pages_in = take(replicas - 2)
    moves_all, table_all, projection = take(3)
    pages_in, messages = take(1) + pages_in, by_distance(take(count))
    num_in, den_in = take(2)
    outs = take(count - 1)
    own_num, own_den, own_kv, own_share, marks, num, den, wide, moves, table, sems = refs
    tables = start_copies(((moves_all, moves), (table_all, table)), sems)
    me, column = lax.axis_index("replica"), lax.axis_index("mp")
    rows = table.shape[1]
    page_size, width = pages_in[0].shape[0] - EXTRA, pages_in[0].shape[1]
    half_rows = local_heads * rows
    movers = moves.shape[1] // replicas

    depth = projection.shape[0]
    extra = [page[page_size:, :].astype(jnp.float32) for page in pages_in]
    inputs = [
        jnp.concatenate(
            [part[2 + i : 3 + i, : piece.stop - piece.start] for i, piece in enumerate(pieces_of(depth, width))],
            axis=1,
        )
        for part in extra
    ]
    inputs += [jnp.zeros((8 - len(inputs), depth), jnp.float32)]
    inputs = jnp.concatenate(inputs, axis=0).astype(jnp.bfloat16)
    share = jnp.dot(inputs, projection[...], preferred_element_type=jnp.float32)
    num[...] = num_in[...]
    den[...] = den_in[...]
    for s, message in enumerate(messages):
        wide[s] = message[half_rows : 2 * half_rows, :].astype(jnp.float32)
    lengths = [length_of(page, page_size) for page in pages_in]

    wait_for(tables)
    lane = lax.broadcasted_iota(jnp.int32, (local_heads, HD), 1)
    token = lax.broadcasted_iota(jnp.int32, (local_heads, page_size), 1)
    columns = [head_columns(partner("mp", s), local_heads) for s in range(count)]
    cases = [(d, s) for d in range(1, replicas) for s in range(count)]
    arrivals = [pair_row(moves, partner("replica", d), me, rows, 1) for d in range(1, replicas)]
    places = [locate(table, row, column, slots) for _, row, _ in arrivals]
    scores, weights, totals = {}, {}, {}
    for d, s in cases:
        row = arrivals[d - 1][1]
        q = wide[s, pl.ds(row, local_heads, stride=rows), :].astype(jnp.bfloat16)
        keys = pages_in[d - 1].at[pl.ds(0, page_size), pl.ds(0, width // 2)]
        scores[d, s] = scores_of(q, keys[:, columns[s]])
    for d, s in cases:
        inside = (token + places[d - 1][0] * page_size).astype(jnp.float32) < lengths[d - 1]
        weight = jnp.where(inside, weight_of(scores[d, s]), 0.0)
        weights[d, s] = weight.astype(jnp.bfloat16)
        totals[d, s] = jnp.sum(weight, axis=1, keepdims=True)
    for d, s in cases:
        values = pages_in[d - 1].at[pl.ds(0, page_size), pl.ds(width // 2, width // 2)]
        scores[d, s] = jnp.dot(weights[d, s], values[:, columns[s]], preferred_element_type=jnp.float32)
    for d, (valid, row, _) in enumerate(arrivals, 1):

        @pl.when(valid == 1)
        def _(d=d, row=row):
            for s in range(count):
                num[s, pl.ds(half_rows + row, local_heads, stride=rows), :] = scores[d, s]
                old = den[s, pl.ds(local_heads, local_heads), :]
                den[s, pl.ds(local_heads, local_heads), :] = jnp.where(lane == row, totals[d, s], old)

    arrived = []
    row_ids = lax.broadcasted_iota(jnp.int32, (rows, HD), 0)
    for number in range(movers):
        picked = jnp.zeros((1, width), jnp.float32)
        mark = jnp.zeros((rows, HD), jnp.float32)
        for d, (valid, row, order) in enumerate(arrivals):
            here = (valid == 1) & (order == number)
            picked = jnp.where(here, share[d : d + 1], picked)
            mark = jnp.where(here & (row_ids == row), 1.0, mark)
        part = jnp.concatenate([picked[:, j * HD : (j + 1) * HD] for j in range(2 * KVH)], axis=0)
        high = part.astype(jnp.bfloat16).astype(jnp.float32)
        arrived += [high, part - high]
        own_share[number] = part
        marks[number] = mark
    own_num[...] = num[0]
    own_den[...] = den[0]
    all_kv = []
    for half in range(2):
        own_kv[half] = own_tokens(messages, rows, 2 * half_rows, half)
        all_kv.append(own_kv[half])
    filler = [jnp.zeros((-2 * local_heads % 16, HD), jnp.float32)] if local_heads % 8 else []
    for s, out in enumerate(outs):
        at = s + 1
        parts = den[at]
        high = parts.astype(SEND).astype(jnp.float32)
        parts = high + pltpu.roll(parts - high, HD // 2, 1)
        out[...] = jnp.concatenate([num[at], parts] + filler + all_kv + arrived, axis=0).astype(SEND)


def finish_kernel(count, replicas, local_heads, *refs):
    refs = list(refs)
    take = lambda n: [refs.pop(0) for _ in range(n)]
    pages_in = take(replicas - 2)
    moves_all, table_all, lengths_all, kv, share, marks, q, num, den = take(9)
    pages_in, messages = take(1) + pages_in, by_distance(take(count - 1))
    pool_raw, _, first, second, pool = take(5)
    moves, table, lengths, full, arrived, windows, results, sems, write_sems, out_sems = refs
    tables = start_copies(((moves_all, moves), (table_all, table), (lengths_all, lengths)), sems)
    me, column = lax.axis_index("replica"), lax.axis_index("mp")
    rows = lengths.shape[0]
    slots, page_size, width = pool_raw.shape
    both = 2 * local_heads
    query_rows = both * rows
    movers = moves.shape[1] // replicas
    head = split(column * local_heads, GROUP)[0]

    kv_base = messages[0].shape[0] - 4 * rows - 16 * movers
    for s in range(count):
        device = partner("mp", s)
        for half in range(2):
            if s == 0:
                chunk = kv[half]
            else:
                start = kv_base + half * 2 * rows
                chunk = messages[s - 1][start : start + 2 * rows, :].astype(jnp.float32)

            def place(half=half, device=device, chunk=chunk):
                columns = head_columns(device, local_heads)
                full.at[pl.ds(0, 2 * rows), pl.ds(half * (width // 2), width // 2)][:, columns] = chunk

            if local_heads == GROUP:
                place()
            else:
                pl.when(split(device * local_heads, GROUP)[1] == 0)(place)
    for number in range(movers):
        total = share[number]
        for message in messages:
            start = kv_base + 4 * rows + 16 * number
            part = message[start : start + 16, :].astype(jnp.float32)
            total += part[: 2 * KVH] + part[2 * KVH :]
        total = total.astype(jnp.bfloat16).astype(jnp.float32)
        arrived[number] = total
        for j in range(2 * KVH):
            full[2 * rows + number : 2 * rows + number + 1, j * HD : (j + 1) * HD] = total[j : j + 1, :]
    sums = den[...]
    for message in messages:
        part = message[query_rows : query_rows + both, :].astype(jnp.float32)
        sums += part + pltpu.roll(part, HD // 2, 1)
    sums = jnp.transpose(sums)[:rows, :]

    held = []
    for half in range(2):
        value = kv[half, :rows, :]
        for number in range(movers):
            moved = arrived[number, pl.ds(head + half * KVH, 1), :]
            value = jnp.where(marks[number] > 0.5, moved, value)
        held.append(value)
    outs = []

    def finish_step(step, out):
        pieces = []
        for h in range(local_heads):
            at = (step * local_heads + h) * rows
            query = q[at : at + rows, :].astype(jnp.float32)
            numerator = num[at : at + rows, :]
            for message in messages:
                numerator += message[at : at + rows, :].astype(jnp.float32)
            denominator = sums[:, step * local_heads + h : step * local_heads + h + 1]
            extra = [(kv[0, :rows, :], kv[1, :rows, :])]
            if step == 1:
                extra = [held, (kv[0, rows:, :], kv[1, rows:, :])]
            for key, value in extra:
                weight = weight_of(jnp.sum(query * key, axis=1, keepdims=True))
                numerator += weight.astype(jnp.bfloat16).astype(jnp.float32) * value
                denominator += weight
            pieces.append(numerator / denominator)
        results[step] = jnp.concatenate(pieces, axis=1).astype(out.dtype)
        outs.append(pltpu.make_async_copy(results.at[step], out, out_sems.at[step]))
        outs[-1].start()

    finish_step(0, first)
    wait_for(tables)
    kept, plans = [jnp.bool_(True)] * rows, []

    def add_plan(active, row, length, first_token, source, r=None):
        index, slot = locate(table, row, column, slots)
        at = length - index * page_size
        touched = active & (at >= -1) & (at < page_size)
        start = jnp.clip(at, 0, page_size - WINDOW) & -16
        span = pl.ds(pl.multiple_of(start, 16), WINDOW)
        n = len(plans)
        source = source.at[slot] if r is not None else source
        write = pltpu.make_async_copy(windows.at[n], pool.at[slot, span], write_sems.at[n])
        plans.append((touched, source, span, write, first_token, rows + row, at - start))

    for s, page in enumerate(pages_in):
        valid, row, order = pair_row(moves, partner("replica", s + 1), me, rows, 1)
        valid = valid == 1
        length = jnp.max(length_of(page, page_size)).astype(jnp.int32)
        page = page.at[pl.ds(0, page_size)]
        add_plan(valid, row, length, 2 * rows + order, page)
        kept = [stays & ~(valid & (row == r)) for r, stays in enumerate(kept)]
    for r in range(rows):
        add_plan(kept[r], r, lengths[r], r, pool_raw, r)

    place_ids = lax.broadcasted_iota(jnp.int32, (WINDOW, width), 0)
    for n, (touched, source, span, write, token, next_token, offset) in enumerate(plans):

        @pl.when(touched)
        def _(n=n, source=source, span=span, write=write, token=token, next_token=next_token, offset=offset):
            old = source[span, :].astype(jnp.float32)
            new = jnp.where(place_ids == offset, full[pl.ds(token, 1), :], old)
            new = jnp.where(place_ids == offset + 1, full[pl.ds(next_token, 1), :], new)
            windows[n] = new.astype(jnp.bfloat16)
            write.start()

    finish_step(1, second)
    for plan in plans:
        pl.when(plan[0])(plan[3].wait)
    wait_for(outs)


def cost(microseconds):
    return pl.CostEstimate(flops=0, transcendentals=0, bytes_accessed=int(microseconds * 3.5e6))


def in_vmem(value):
    return pltpu.with_memory_space_constraint(value, pltpu.VMEM)


def in_hbm(value):
    return pltpu.with_memory_space_constraint(value, pltpu.HBM)


def params(megabytes=32, **rest):
    return pltpu.CompilerParams(vmem_limit_bytes=megabytes << 20, **rest)


def body(layer_input, kv_weight, queries, kv_pool, lengths, block_table, new_table, migrations):
    replicas, count = lax.axis_size("replica"), lax.axis_size("mp")
    rows = lengths.shape[0]
    pool = kv_pool[0, 0]
    slots, page_size, width = pool.shape
    local_heads = queries.shape[2] // HD
    both = 2 * local_heads
    query_rows = both * rows
    depth = layer_input.shape[2]
    f32, bf16 = jnp.float32, jnp.bfloat16
    moves, old_table, table_after = migrations.T, block_table.T, new_table.T
    shape = jax.ShapeDtypeStruct

    message_rows = query_rows + 8 * rows
    movers = migrations.shape[0] // replicas
    inputs = layer_input.reshape(2 * rows, depth)
    leaving = pl.pallas_call(
        functools.partial(leave_kernel, rows),
        out_shape=[shape((page_size + EXTRA, width), bf16)] * (replicas - 1),
        in_specs=[HBM] * 5,
        out_specs=[VMEM] * (replicas - 1),
        scratch_shapes=[
            pltpu.SMEM(moves.shape, jnp.int32),
            pltpu.SMEM(old_table.shape, jnp.int32),
            pltpu.SMEM(lengths.shape, jnp.int32),
            pltpu.VMEM((2 * rows, depth), bf16),
            pltpu.SemaphoreType.DMA((4,)),
            pltpu.SemaphoreType.DMA((replicas - 1,)),
        ],
        compiler_params=params(),
        cost_estimate=cost(2.0),
        name="leave",
    )(*map(in_hbm, (moves, old_table, lengths, inputs, pool)))
    pages_in = exchange(leaving, "replica")

    weight_near, inputs_near, queries_near = map(in_vmem, (kv_weight, inputs, queries))
    sent = pl.pallas_call(
        functools.partial(open_kernel, count, local_heads),
        out_shape=[shape((message_rows, HD), bf16)] * count,
        in_specs=[VMEM] * 3,
        out_specs=[VMEM] * count,
        compiler_params=params(),
        cost_estimate=cost(1.2),
        name="open",
    )(inputs_near, queries_near, weight_near)
    sent, pages_in[0] = lax.optimization_barrier((list(sent), pages_in[0]))
    messages = [sent[0]] + exchange(sent[1:], "mp")

    pool_near = in_vmem(pool)
    num, den = pl.pallas_call(
        functools.partial(attend_kernel, count, local_heads),
        out_shape=[shape((count, query_rows, HD), f32), shape((count, both, HD), f32)],
        in_specs=[SMEM, SMEM, VMEM] + [VMEM] * count,
        out_specs=[VMEM, VMEM],
        scratch_shapes=[pltpu.VMEM((count, query_rows, HD), f32)],
        compiler_params=params(),
        cost_estimate=cost(1.5),
        name="attend",
    )(old_table, lengths, pool_near, *by_start(messages))

    sum_rows = query_rows + -(-both // 16) * 16 + 4 * rows + 16 * movers
    *sums, num, den, kv, share, marks = pl.pallas_call(
        functools.partial(arrive_kernel, count, replicas, local_heads, slots),
        out_shape=[shape((sum_rows, HD), SEND)] * (count - 1)
        + [shape((query_rows, HD), f32), shape((both, HD), f32)]
        + [shape((2, 2 * rows, HD), f32), shape((movers, 2 * KVH, HD), f32)]
        + [shape((movers, rows, HD), f32)],
        in_specs=[VMEM] * (replicas - 2)
        + [ANY, ANY, VMEM, VMEM]
        + [VMEM] * count
        + [VMEM] * 2,
        out_specs=[VMEM] * (count + 4),
        scratch_shapes=[
            pltpu.VMEM((count, query_rows, HD), f32),
            pltpu.VMEM((count, both, HD), f32),
            pltpu.VMEM((count, query_rows // 2, HD), f32),
            pltpu.SMEM(moves.shape, jnp.int32),
            pltpu.SMEM(table_after.shape, jnp.int32),
            pltpu.SemaphoreType.DMA((2,)),
        ],
        compiler_params=params(),
        cost_estimate=cost(1.2),
        name="arrive",
    )(*pages_in[1:], moves, table_after, weight_near, pages_in[0], *by_start(messages), num, den)
    sums_in = exchange(sums, "mp")

    moves_then, _ = lax.optimization_barrier((moves, marks))

    pool_copy = pl.pallas_call(
        functools.partial(keep_kernel, replicas),
        out_shape=shape(pool.shape, bf16),
        in_specs=[VMEM] * replicas + [ANY] * 2,
        out_specs=ANY,
        scratch_shapes=[
            pltpu.SMEM(moves.shape, jnp.int32),
            pltpu.SMEM(table_after.shape, jnp.int32),
            pltpu.SemaphoreType.DMA((2,)),
            pltpu.SemaphoreType.DMA((rows + replicas - 1,)),
        ],
        compiler_params=params(),
        cost_estimate=cost(1.6),
        name="keep",
    )(*pages_in, pool_near, moves_then, table_after)

    first, second, pool_after = pl.pallas_call(
        functools.partial(finish_kernel, count, replicas, local_heads),
        out_shape=[
            shape((rows, local_heads * HD), bf16),
            shape((rows, local_heads * HD), bf16),
            shape(pool.shape, bf16),
        ],
        in_specs=[VMEM] * (replicas - 2) + [ANY] * 3 + [VMEM] * (7 + count - 1) + [VMEM, ANY],
        out_specs=[ANY] * 3,
        scratch_shapes=[
            pltpu.SMEM(moves.shape, jnp.int32),
            pltpu.SMEM(table_after.shape, jnp.int32),
            pltpu.SMEM(lengths.shape, jnp.int32),
            pltpu.VMEM((KV_ROWS, width), f32),
            pltpu.VMEM((movers, 2 * KVH, HD), f32),
            pltpu.VMEM((rows + replicas - 1, WINDOW, width), bf16),
            pltpu.VMEM((2, rows, local_heads * HD), bf16),
            pltpu.SemaphoreType.DMA((3,)),
            pltpu.SemaphoreType.DMA((rows + replicas - 1,)),
            pltpu.SemaphoreType.DMA((2,)),
        ],
        input_output_aliases={9 + replicas - 1 + (count - 1) + 1: 2},
        compiler_params=params(),
        cost_estimate=cost(2.5),
        name="finish",
    )(
        *pages_in[1:],
        *(moves, table_after, lengths),
        *(kv, share, marks, messages[0], num, den, pages_in[0]),
        *by_start(sums_in),
        *(pool_near, pool_copy),
    )
    return first, second, pool_after[None, None]


def solution(mesh):
    return jax.shard_map(
        body,
        mesh=mesh,
        in_specs=(
            P(None, ("groups", "replica"), "mp"),
            P("mp", None),
            P(None, ("groups", "replica"), "mp"),
            P(("groups", "replica"), "mp", None, None, None),
            P(("groups", "replica")),
            P(("groups", "replica"), None),
            P(("groups", "replica"), None),
            P("groups", None),
        ),
        out_specs=(
            P(("groups", "replica"), "mp"),
            P(("groups", "replica"), "mp"),
            P(("groups", "replica"), "mp", None, None, None),
        ),
        check_vma=False,
    )
```

```python
import functools
import math

import jax
import jax.numpy as jnp
from jax import lax
from jax.experimental import pallas as pl
from jax.experimental.pallas import tpu as pltpu
from jax.sharding import PartitionSpec as P

H = 32
KVH = 4
HD = 128
GROUP = H // KVH
CAP = 20.0
SCALE = 1.0 / math.sqrt(HD)
WINDOW = 32
KV_ROWS = 24
EXTRA = 8

SMEM = pl.BlockSpec(memory_space=pltpu.SMEM)
VMEM = pl.BlockSpec(memory_space=pltpu.VMEM)
ANY = pl.BlockSpec(memory_space=pl.ANY)
HBM = pl.BlockSpec(memory_space=pltpu.HBM)
SEND = jnp.bfloat16


def swap(value, axis, distance):
    size = lax.axis_size(axis)
    return lax.ppermute(value, axis, [(i, i ^ distance) for i in range(size)])


def exchange(messages, axis):
    received = [swap(messages[d], axis, d + 1) for d in reversed(range(len(messages)))]
    return received[::-1]


def start_order(count):
    return [count // 2] + [d for d in range(count - 1, 0, -1) if d != count // 2]


def by_start(values):
    own = len(values) & 1 ^ 1
    order = start_order(len(values) + 1 - own)
    return [values[d - 1 + own] for d in order] + list(values[:own])


def by_distance(values):
    own = len(values) & 1 ^ 1
    order = start_order(len(values) + 1 - own)
    return list(values[len(order) :]) + [values[order.index(d)] for d in range(1, len(order) + 1)]


def partner(axis, distance):
    return lax.axis_index(axis) ^ distance


def split(value, size):
    if size & (size - 1) == 0:
        return lax.shift_right_logical(value, size.bit_length() - 1), value & (size - 1)
    return lax.div(value, size), lax.rem(value, size)


def count_up(limit, step, state):
    if limit > 8:
        return lax.fori_loop(0, limit, step, state)
    for i in range(limit):
        state = step(i, state)
    return state


def locate(table, row, column, slots):
    def step(p, found):
        device, slot = split(table[p, row], slots)
        here = device == column
        return jnp.where(here, p, found[0]), jnp.where(here, slot, found[1])

    return count_up(table.shape[0], step, (jnp.int32(0), jnp.int32(0)))


def pair_row(moves, source, target, rows, side):
    def step(j, found):
        valid, row, order, number = found
        ends = [split(moves[i, j], rows) for i in range(2)]
        match = (ends[0][0] == source) & (ends[1][0] == target)
        return (
            jnp.where(match, jnp.int32(1), valid),
            jnp.where(match, ends[side][1], row),
            jnp.where(match, number, order),
            number + jnp.where(ends[side][0] == (source, target)[side], 1, 0),
        )

    return count_up(moves.shape[1], step, (jnp.int32(0),) * 4)[:3]


def head_columns(device, local_heads):
    return pl.ds(pl.multiple_of(split(device * local_heads, GROUP)[0] * HD, HD), HD)


def weight_of(score):
    return jnp.exp(CAP * jnp.tanh(score * (SCALE / CAP)))


def pieces_of(depth, width):
    return [slice(at, min(at + width, depth)) for at in range(0, depth, width)]


def start_copies(pairs, sems):
    copies = [pltpu.make_async_copy(*pair, sems.at[i]) for i, pair in enumerate(pairs)]
    for copy in copies:
        copy.start()
    return copies


def wait_for(copies):
    for copy in copies:
        copy.wait()


def leave_kernel(rows, moves_all, table_all, lengths_all, x_all, pool, *refs):
    held, pages, (moves, table, lengths, x, sems, pool_sems) = refs[0], refs[1:-6], refs[-6:]
    me, column = lax.axis_index("replica"), lax.axis_index("mp")
    page_size, width = pool.shape[1:]
    depth = x.shape[1]
    rest = start_copies(
        ((moves_all, moves), (table_all, table), (lengths_all, lengths), (x_all, x)), sems
    )
    copies = start_copies([(pool.at[i], held.at[i]) for i in range(pool.shape[0])], pool_sems)
    wait_for(rest[:2])
    found = [pair_row(moves, me, partner("replica", s + 1), rows, 0)[1] for s in range(len(pages))]
    picks = [locate(table, row, column, pool.shape[0])[1] for row in found]
    wait_for(rest[2:])
    sublane = lax.broadcasted_iota(jnp.int32, (EXTRA, width), 0)
    first_rows = x[:rows, :].astype(jnp.float32)
    row_ids = lax.broadcasted_iota(jnp.int32, (rows, depth), 0)
    for row, page in zip(found, pages):
        high, low = split(lengths[row], 64)
        extra = jnp.where(sublane == 0, high, low).astype(jnp.float32)
        picked = jnp.sum(jnp.where(row_ids == row, first_rows, 0.0), axis=0, keepdims=True)
        for i, piece in enumerate(pieces_of(depth, width)):
            value = picked[:, piece]
            if value.shape[1] < width:
                value = jnp.concatenate([value, jnp.zeros((1, width - value.shape[1]), jnp.float32)], axis=1)
            extra = jnp.where(sublane == 2 + i, value, extra)
        page[page_size:, :] = extra.astype(jnp.bfloat16)
    wait_for(copies)
    for slot, page in zip(picks, pages):
        page[:page_size, :] = held[slot]


def open_kernel(count, local_heads, x, q, weight, *refs):
    outs, (held, weight_sems) = refs[:-2], refs[-2:]
    depth, chunks = weight.shape[0], weight_sems.shape[0]
    spans = [pl.ds(c * (depth // chunks), depth // chunks) for c in range(chunks)]
    loads = start_copies([(weight.at[span], held.at[span]) for span in spans], weight_sems)
    rows = q.shape[1]
    wide = [q[i].astype(jnp.float32) for i in range(2)]
    blocks = [wide[i][:, h * HD : (h + 1) * HD] for i in range(2) for h in range(local_heads)]
    packed = jnp.concatenate(blocks, axis=0).astype(jnp.bfloat16)
    query_rows = packed.shape[0]
    for out in outs:
        out[:query_rows, :] = packed
    total = jnp.zeros((x.shape[0], weight.shape[1]), jnp.float32)
    for span, load in zip(spans, loads):
        load.wait()
        total += jnp.dot(x[:, span], held[span, :], preferred_element_type=jnp.float32)
    for j in range(KVH):
        parts = []
        for half in range(2):
            start = (half * KVH + j) * HD
            part = total[:, start : start + HD]
            high = part.astype(jnp.bfloat16)
            parts += [high, (part - high.astype(jnp.float32)).astype(jnp.bfloat16)]
        parts = jnp.concatenate(parts, axis=0)
        for s, out in enumerate(outs):

            @pl.when(split(partner("mp", s) * local_heads, GROUP)[0] == j)
            def _(out=out, parts=parts):
                out[query_rows:, :] = parts


def keep_kernel(replicas, *refs):
    pages_in, (pool, moves_all, table_all, pool_out, moves, table, sems, page_sems) = (
        refs[: replicas - 1],
        refs[replicas - 1 :],
    )
    wait_for(start_copies(((moves_all, moves), (table_all, table)), sems))
    me, column = lax.axis_index("replica"), lax.axis_index("mp")
    rows = table.shape[1]
    slots, page_size, _ = pool.shape
    kept, copies = [jnp.bool_(True)] * rows, []
    for s, page in enumerate(pages_in):
        valid, row, _ = pair_row(moves, partner("replica", s + 1), me, rows, 1)
        kept = [stays & ~((valid == 1) & (row == r)) for r, stays in enumerate(kept)]
        copies.append((valid == 1, row, lambda slot, page=page: page.at[pl.ds(0, page_size)]))
    copies += [(stays, r, lambda slot: pool.at[slot]) for r, stays in enumerate(kept)]
    started = []
    for n, (active, row, source) in enumerate(copies):
        _, slot = locate(table, row, column, slots)
        copy = pltpu.make_async_copy(source(slot), pool_out.at[slot], page_sems.at[n])
        started.append((active, copy))
        pl.when(active)(copy.start)
    for active, copy in started:
        pl.when(active)(copy.wait)


def length_of(page, page_size):
    part = page[page_size:, :HD].astype(jnp.float32)
    return part[0:1] * 64.0 + part[1:2]


def own_tokens(messages, rows, query_rows, half):
    tokens = 2 * rows
    start = query_rows + 2 * half * tokens
    total = jnp.zeros((tokens, HD), jnp.float32)
    for message in messages:
        total += message[start : start + tokens, :].astype(jnp.float32)
        total += message[start + tokens : start + 2 * tokens, :].astype(jnp.float32)
    return total.astype(jnp.bfloat16).astype(jnp.float32)


def scores_of(q, keys):
    return lax.dot_general(q, keys, (((1,), (1,)), ((), ())), preferred_element_type=jnp.float32)


def attend_kernel(count, local_heads, table, lengths, pool, *refs):
    messages = by_distance(refs[:count])
    num, den, wide = refs[count:]
    column = lax.axis_index("mp")
    rows = lengths.shape[0]
    slots, page_size, width = pool.shape
    both = 2 * local_heads
    for s, message in enumerate(messages):
        wide[s] = message[: both * rows, :].astype(jnp.float32)
    lane = lax.broadcasted_iota(jnp.int32, (both, HD), 1)
    token = lax.broadcasted_iota(jnp.int32, (both, page_size), 1)
    places = [locate(table, r, column, slots) for r in range(rows)]
    columns = [head_columns(partner("mp", s), local_heads) for s in range(count)]
    keys = pool.at[:, :, pl.ds(0, width // 2)]
    values = pool.at[:, :, pl.ds(width // 2, width // 2)]
    cases = [(r, s) for r in range(rows) for s in range(count)]
    scores = {}
    for r, s in cases:
        q = wide[s, pl.ds(r, both, stride=rows), :].astype(jnp.bfloat16)
        scores[r, s] = scores_of(q, keys[places[r][1], :, columns[s]])
    weights = {}
    denominators = [jnp.zeros((both, HD), jnp.float32) for _ in range(count)]
    for r, s in cases:
        inside = token < lengths[r] - places[r][0] * page_size
        weight = jnp.where(inside, weight_of(scores[r, s]), 0.0)
        weights[r, s] = weight.astype(jnp.bfloat16)
        total = jnp.sum(weight, axis=1, keepdims=True)
        denominators[s] += jnp.where(lane == r, total, 0.0)
    for r, s in cases:
        num[s, pl.ds(r, both, stride=rows), :] = jnp.dot(
            weights[r, s], values[places[r][1], :, columns[s]], preferred_element_type=jnp.float32
        )
    for s in range(count):
        den[s] = denominators[s]


def arrive_kernel(count, replicas, local_heads, slots, *refs):
    refs = list(refs)
    take = lambda n: [refs.pop(0) for _ in range(n)]
    pages_in = take(replicas - 2)
    moves_all, table_all, projection = take(3)
    pages_in, messages = take(1) + pages_in, by_distance(take(count))
    num_in, den_in = take(2)
    outs = take(count - 1)
    own_num, own_den, own_kv, own_share, marks, num, den, wide, moves, table, sems = refs
    tables = start_copies(((moves_all, moves), (table_all, table)), sems)
    me, column = lax.axis_index("replica"), lax.axis_index("mp")
    rows = table.shape[1]
    page_size, width = pages_in[0].shape[0] - EXTRA, pages_in[0].shape[1]
    half_rows = local_heads * rows
    movers = moves.shape[1] // replicas

    depth = projection.shape[0]
    extra = [page[page_size:, :].astype(jnp.float32) for page in pages_in]
    inputs = [
        jnp.concatenate(
            [part[2 + i : 3 + i, : piece.stop - piece.start] for i, piece in enumerate(pieces_of(depth, width))],
            axis=1,
        )
        for part in extra
    ]
    inputs += [jnp.zeros((8 - len(inputs), depth), jnp.float32)]
    inputs = jnp.concatenate(inputs, axis=0).astype(jnp.bfloat16)
    share = jnp.dot(inputs, projection[...], preferred_element_type=jnp.float32)
    num[...] = num_in[...]
    den[...] = den_in[...]
    for s, message in enumerate(messages):
        wide[s] = message[half_rows : 2 * half_rows, :].astype(jnp.float32)
    lengths = [length_of(page, page_size) for page in pages_in]

    wait_for(tables)
    lane = lax.broadcasted_iota(jnp.int32, (local_heads, HD), 1)
    token = lax.broadcasted_iota(jnp.int32, (local_heads, page_size), 1)
    columns = [head_columns(partner("mp", s), local_heads) for s in range(count)]
    cases = [(d, s) for d in range(1, replicas) for s in range(count)]
    arrivals = [pair_row(moves, partner("replica", d), me, rows, 1) for d in range(1, replicas)]
    places = [locate(table, row, column, slots) for _, row, _ in arrivals]
    scores, weights, totals = {}, {}, {}
    for d, s in cases:
        row = arrivals[d - 1][1]
        q = wide[s, pl.ds(row, local_heads, stride=rows), :].astype(jnp.bfloat16)
        keys = pages_in[d - 1].at[pl.ds(0, page_size), pl.ds(0, width // 2)]
        scores[d, s] = scores_of(q, keys[:, columns[s]])
    for d, s in cases:
        inside = (token + places[d - 1][0] * page_size).astype(jnp.float32) < lengths[d - 1]
        weight = jnp.where(inside, weight_of(scores[d, s]), 0.0)
        weights[d, s] = weight.astype(jnp.bfloat16)
        totals[d, s] = jnp.sum(weight, axis=1, keepdims=True)
    for d, s in cases:
        values = pages_in[d - 1].at[pl.ds(0, page_size), pl.ds(width // 2, width // 2)]
        scores[d, s] = jnp.dot(weights[d, s], values[:, columns[s]], preferred_element_type=jnp.float32)
    for d, (valid, row, _) in enumerate(arrivals, 1):

        @pl.when(valid == 1)
        def _(d=d, row=row):
            for s in range(count):
                num[s, pl.ds(half_rows + row, local_heads, stride=rows), :] = scores[d, s]
                old = den[s, pl.ds(local_heads, local_heads), :]
                den[s, pl.ds(local_heads, local_heads), :] = jnp.where(lane == row, totals[d, s], old)

    arrived = []
    row_ids = lax.broadcasted_iota(jnp.int32, (rows, HD), 0)
    for number in range(movers):
        picked = jnp.zeros((1, width), jnp.float32)
        mark = jnp.zeros((rows, HD), jnp.float32)
        for d, (valid, row, order) in enumerate(arrivals):
            here = (valid == 1) & (order == number)
            picked = jnp.where(here, share[d : d + 1], picked)
            mark = jnp.where(here & (row_ids == row), 1.0, mark)
        part = jnp.concatenate([picked[:, j * HD : (j + 1) * HD] for j in range(2 * KVH)], axis=0)
        high = part.astype(jnp.bfloat16).astype(jnp.float32)
        arrived += [high, part - high]
        own_share[number] = part
        marks[number] = mark
    own_num[...] = num[0]
    own_den[...] = den[0]
    all_kv = []
    for half in range(2):
        own_kv[half] = own_tokens(messages, rows, 2 * half_rows, half)
        all_kv.append(own_kv[half])
    filler = [jnp.zeros((-2 * local_heads % 16, HD), jnp.float32)] if local_heads % 8 else []
    for s, out in enumerate(outs):
        at = s + 1
        parts = den[at]
        high = parts.astype(SEND).astype(jnp.float32)
        parts = high + pltpu.roll(parts - high, HD // 2, 1)
        out[...] = jnp.concatenate([num[at], parts] + filler + all_kv + arrived, axis=0).astype(SEND)


def finish_kernel(count, replicas, local_heads, *refs):
    refs = list(refs)
    take = lambda n: [refs.pop(0) for _ in range(n)]
    pages_in = take(replicas - 2)
    moves_all, table_all, lengths_all, kv, share, marks, q, num, den = take(9)
    pages_in, messages = take(1) + pages_in, by_distance(take(count - 1))
    pool_raw, _, first, second, pool = take(5)
    moves, table, lengths, full, arrived, windows, results, sems, write_sems, out_sems = refs
    tables = start_copies(((moves_all, moves), (table_all, table), (lengths_all, lengths)), sems)
    me, column = lax.axis_index("replica"), lax.axis_index("mp")
    rows = lengths.shape[0]
    slots, page_size, width = pool_raw.shape
    both = 2 * local_heads
    query_rows = both * rows
    movers = moves.shape[1] // replicas
    head = split(column * local_heads, GROUP)[0]

    kv_base = messages[0].shape[0] - 4 * rows - 16 * movers
    for s in range(count):
        device = partner("mp", s)
        for half in range(2):
            if s == 0:
                chunk = kv[half]
            else:
                start = kv_base + half * 2 * rows
                chunk = messages[s - 1][start : start + 2 * rows, :].astype(jnp.float32)

            def place(half=half, device=device, chunk=chunk):
                columns = head_columns(device, local_heads)
                full.at[pl.ds(0, 2 * rows), pl.ds(half * (width // 2), width // 2)][:, columns] = chunk

            if local_heads == GROUP:
                place()
            else:
                pl.when(split(device * local_heads, GROUP)[1] == 0)(place)
    for number in range(movers):
        total = share[number]
        for message in messages:
            start = kv_base + 4 * rows + 16 * number
            part = message[start : start + 16, :].astype(jnp.float32)
            total += part[: 2 * KVH] + part[2 * KVH :]
        total = total.astype(jnp.bfloat16).astype(jnp.float32)
        arrived[number] = total
        for j in range(2 * KVH):
            full[2 * rows + number : 2 * rows + number + 1, j * HD : (j + 1) * HD] = total[j : j + 1, :]
    sums = den[...]
    for message in messages:
        part = message[query_rows : query_rows + both, :].astype(jnp.float32)
        sums += part + pltpu.roll(part, HD // 2, 1)
    sums = jnp.transpose(sums)[:rows, :]

    held = []
    for half in range(2):
        value = kv[half, :rows, :]
        for number in range(movers):
            moved = arrived[number, pl.ds(head + half * KVH, 1), :]
            value = jnp.where(marks[number] > 0.5, moved, value)
        held.append(value)
    outs = []

    def finish_step(step, out):
        pieces = []
        for h in range(local_heads):
            at = (step * local_heads + h) * rows
            query = q[at : at + rows, :].astype(jnp.float32)
            numerator = num[at : at + rows, :]
            for message in messages:
                numerator += message[at : at + rows, :].astype(jnp.float32)
            denominator = sums[:, step * local_heads + h : step * local_heads + h + 1]
            extra = [(kv[0, :rows, :], kv[1, :rows, :])]
            if step == 1:
                extra = [held, (kv[0, rows:, :], kv[1, rows:, :])]
            for key, value in extra:
                weight = weight_of(jnp.sum(query * key, axis=1, keepdims=True))
                numerator += weight.astype(jnp.bfloat16).astype(jnp.float32) * value
                denominator += weight
            pieces.append(numerator / denominator)
        results[step] = jnp.concatenate(pieces, axis=1).astype(out.dtype)
        outs.append(pltpu.make_async_copy(results.at[step], out, out_sems.at[step]))
        outs[-1].start()

    finish_step(0, first)
    wait_for(tables)
    kept, plans = [jnp.bool_(True)] * rows, []

    def add_plan(active, row, length, first_token, source, r=None):
        index, slot = locate(table, row, column, slots)
        at = length - index * page_size
        touched = active & (at >= -1) & (at < page_size)
        start = jnp.clip(at, 0, page_size - WINDOW) & -16
        span = pl.ds(pl.multiple_of(start, 16), WINDOW)
        n = len(plans)
        source = source.at[slot] if r is not None else source
        write = pltpu.make_async_copy(windows.at[n], pool.at[slot, span], write_sems.at[n])
        plans.append((touched, source, span, write, first_token, rows + row, at - start))

    for s, page in enumerate(pages_in):
        valid, row, order = pair_row(moves, partner("replica", s + 1), me, rows, 1)
        valid = valid == 1
        length = jnp.max(length_of(page, page_size)).astype(jnp.int32)
        page = page.at[pl.ds(0, page_size)]
        add_plan(valid, row, length, 2 * rows + order, page)
        kept = [stays & ~(valid & (row == r)) for r, stays in enumerate(kept)]
    for r in range(rows):
        add_plan(kept[r], r, lengths[r], r, pool_raw, r)

    place_ids = lax.broadcasted_iota(jnp.int32, (WINDOW, width), 0)
    for n, (touched, source, span, write, token, next_token, offset) in enumerate(plans):

        @pl.when(touched)
        def _(n=n, source=source, span=span, write=write, token=token, next_token=next_token, offset=offset):
            old = source[span, :].astype(jnp.float32)
            new = jnp.where(place_ids == offset, full[pl.ds(token, 1), :], old)
            new = jnp.where(place_ids == offset + 1, full[pl.ds(next_token, 1), :], new)
            windows[n] = new.astype(jnp.bfloat16)
            write.start()

    finish_step(1, second)
    for plan in plans:
        pl.when(plan[0])(plan[3].wait)
    wait_for(outs)


def cost(microseconds):
    return pl.CostEstimate(flops=0, transcendentals=0, bytes_accessed=int(microseconds * 3.5e6))


def in_vmem(value):
    return pltpu.with_memory_space_constraint(value, pltpu.VMEM)


def in_hbm(value):
    return pltpu.with_memory_space_constraint(value, pltpu.HBM)


def params(megabytes=32, **rest):
    return pltpu.CompilerParams(vmem_limit_bytes=megabytes << 20, **rest)


def body(layer_input, kv_weight, queries, kv_pool, lengths, block_table, new_table, migrations):
    replicas, count = lax.axis_size("replica"), lax.axis_size("mp")
    rows = lengths.shape[0]
    pool = kv_pool[0, 0]
    slots, page_size, width = pool.shape
    local_heads = queries.shape[2] // HD
    both = 2 * local_heads
    query_rows = both * rows
    depth = layer_input.shape[2]
    f32, bf16 = jnp.float32, jnp.bfloat16
    moves, old_table, table_after = migrations.T, block_table.T, new_table.T
    shape = jax.ShapeDtypeStruct

    message_rows = query_rows + 8 * rows
    movers = migrations.shape[0] // replicas
    inputs = layer_input.reshape(2 * rows, depth)
    pool_near, *leaving = pl.pallas_call(
        functools.partial(leave_kernel, rows),
        out_shape=[shape(pool.shape, bf16)] + [shape((page_size + EXTRA, width), bf16)] * (replicas - 1),
        in_specs=[HBM] * 5,
        out_specs=[VMEM] * replicas,
        scratch_shapes=[
            pltpu.SMEM(moves.shape, jnp.int32),
            pltpu.SMEM(old_table.shape, jnp.int32),
            pltpu.SMEM(lengths.shape, jnp.int32),
            pltpu.VMEM((2 * rows, depth), bf16),
            pltpu.SemaphoreType.DMA((4,)),
            pltpu.SemaphoreType.DMA((slots,)),
        ],
        compiler_params=params(),
        cost_estimate=cost(1.8),
        name="leave",
    )(*map(in_hbm, (moves, old_table, lengths, inputs, pool)))
    pages_in = exchange(leaving, "replica")

    weight_near, inputs_near, queries_near = map(in_vmem, (kv_weight, inputs, queries))
    sent = pl.pallas_call(
        functools.partial(open_kernel, count, local_heads),
        out_shape=[shape((message_rows, HD), bf16)] * count,
        in_specs=[VMEM] * 2 + [HBM],
        out_specs=[VMEM] * count,
        scratch_shapes=[pltpu.VMEM((depth, width), bf16), pltpu.SemaphoreType.DMA((8,))],
        compiler_params=params(),
        cost_estimate=cost(1.2),
        name="open",
    )(inputs_near, queries_near, in_hbm(kv_weight))
    sent, pages_in[0] = lax.optimization_barrier((list(sent), pages_in[0]))
    messages = [sent[0]] + exchange(sent[1:], "mp")

    num, den = pl.pallas_call(
        functools.partial(attend_kernel, count, local_heads),
        out_shape=[shape((count, query_rows, HD), f32), shape((count, both, HD), f32)],
        in_specs=[SMEM, SMEM, VMEM] + [VMEM] * count,
        out_specs=[VMEM, VMEM],
        scratch_shapes=[pltpu.VMEM((count, query_rows, HD), f32)],
        compiler_params=params(),
        cost_estimate=cost(1.5),
        name="attend",
    )(old_table, lengths, pool_near, *by_start(messages))

    sum_rows = query_rows + -(-both // 16) * 16 + 4 * rows + 16 * movers
    *sums, num, den, kv, share, marks = pl.pallas_call(
        functools.partial(arrive_kernel, count, replicas, local_heads, slots),
        out_shape=[shape((sum_rows, HD), SEND)] * (count - 1)
        + [shape((query_rows, HD), f32), shape((both, HD), f32)]
        + [shape((2, 2 * rows, HD), f32), shape((movers, 2 * KVH, HD), f32)]
        + [shape((movers, rows, HD), f32)],
        in_specs=[VMEM] * (replicas - 2)
        + [ANY, ANY, VMEM, VMEM]
        + [VMEM] * count
        + [VMEM] * 2,
        out_specs=[VMEM] * (count + 4),
        scratch_shapes=[
            pltpu.VMEM((count, query_rows, HD), f32),
            pltpu.VMEM((count, both, HD), f32),
            pltpu.VMEM((count, query_rows // 2, HD), f32),
            pltpu.SMEM(moves.shape, jnp.int32),
            pltpu.SMEM(table_after.shape, jnp.int32),
            pltpu.SemaphoreType.DMA((2,)),
        ],
        compiler_params=params(),
        cost_estimate=cost(1.2),
        name="arrive",
    )(*pages_in[1:], moves, table_after, weight_near, pages_in[0], *by_start(messages), num, den)
    sums_in = exchange(sums, "mp")

    moves_then, _ = lax.optimization_barrier((moves, marks))

    pool_copy = pl.pallas_call(
        functools.partial(keep_kernel, replicas),
        out_shape=shape(pool.shape, bf16),
        in_specs=[VMEM] * replicas + [ANY] * 2,
        out_specs=ANY,
        scratch_shapes=[
            pltpu.SMEM(moves.shape, jnp.int32),
            pltpu.SMEM(table_after.shape, jnp.int32),
            pltpu.SemaphoreType.DMA((2,)),
            pltpu.SemaphoreType.DMA((rows + replicas - 1,)),
        ],
        compiler_params=params(),
        cost_estimate=cost(1.6),
        name="keep",
    )(*pages_in, pool_near, moves_then, table_after)

    first, second, pool_after = pl.pallas_call(
        functools.partial(finish_kernel, count, replicas, local_heads),
        out_shape=[
            shape((rows, local_heads * HD), bf16),
            shape((rows, local_heads * HD), bf16),
            shape(pool.shape, bf16),
        ],
        in_specs=[VMEM] * (replicas - 2) + [ANY] * 3 + [VMEM] * (7 + count - 1) + [VMEM, ANY],
        out_specs=[ANY] * 3,
        scratch_shapes=[
            pltpu.SMEM(moves.shape, jnp.int32),
            pltpu.SMEM(table_after.shape, jnp.int32),
            pltpu.SMEM(lengths.shape, jnp.int32),
            pltpu.VMEM((KV_ROWS, width), f32),
            pltpu.VMEM((movers, 2 * KVH, HD), f32),
            pltpu.VMEM((rows + replicas - 1, WINDOW, width), bf16),
            pltpu.VMEM((2, rows, local_heads * HD), bf16),
            pltpu.SemaphoreType.DMA((3,)),
            pltpu.SemaphoreType.DMA((rows + replicas - 1,)),
            pltpu.SemaphoreType.DMA((2,)),
        ],
        input_output_aliases={9 + replicas - 1 + (count - 1) + 1: 2},
        compiler_params=params(),
        cost_estimate=cost(2.5),
        name="finish",
    )(
        *pages_in[1:],
        *(moves, table_after, lengths),
        *(kv, share, marks, messages[0], num, den, pages_in[0]),
        *by_start(sums_in),
        *(pool_near, pool_copy),
    )
    return first, second, pool_after[None, None]


def solution(mesh):
    return jax.shard_map(
        body,
        mesh=mesh,
        in_specs=(
            P(None, ("groups", "replica"), "mp"),
            P("mp", None),
            P(None, ("groups", "replica"), "mp"),
            P(("groups", "replica"), "mp", None, None, None),
            P(("groups", "replica")),
            P(("groups", "replica"), None),
            P(("groups", "replica"), None),
            P("groups", None),
        ),
        out_specs=(
            P(("groups", "replica"), "mp"),
            P(("groups", "replica"), "mp"),
            P(("groups", "replica"), "mp", None, None, None),
        ),
        check_vma=False,
    )
```

```python
import functools
import math

import jax
import jax.numpy as jnp
from jax import lax
from jax.experimental import pallas as pl
from jax.experimental.pallas import tpu as pltpu
from jax.sharding import PartitionSpec as P

H = 32
KVH = 4
HD = 128
GROUP = H // KVH
CAP = 20.0
SCALE = 1.0 / math.sqrt(HD)
WINDOW = 32
KV_ROWS = 24

SMEM = pl.BlockSpec(memory_space=pltpu.SMEM)
VMEM = pl.BlockSpec(memory_space=pltpu.VMEM)
ANY = pl.BlockSpec(memory_space=pl.ANY)
HBM = pl.BlockSpec(memory_space=pltpu.HBM)
SEND = jnp.bfloat16


def swap(value, axis, distance):
    size = lax.axis_size(axis)
    return lax.ppermute(value, axis, [(i, i ^ distance) for i in range(size)])


def exchange(messages, axis):
    received = [swap(messages[d], axis, d + 1) for d in reversed(range(len(messages)))]
    return received[::-1]


def start_order(count):
    return [count // 2] + [d for d in range(count - 1, 0, -1) if d != count // 2]


def by_start(values):
    own = len(values) & 1 ^ 1
    order = start_order(len(values) + 1 - own)
    return [values[d - 1 + own] for d in order] + list(values[:own])


def by_distance(values):
    own = len(values) & 1 ^ 1
    order = start_order(len(values) + 1 - own)
    return list(values[len(order) :]) + [values[order.index(d)] for d in range(1, len(order) + 1)]


def partner(axis, distance):
    return lax.axis_index(axis) ^ distance


def split(value, size):
    if size & (size - 1) == 0:
        return lax.shift_right_logical(value, size.bit_length() - 1), value & (size - 1)
    return lax.div(value, size), lax.rem(value, size)


def count_up(limit, step, state):
    if limit > 8:
        return lax.fori_loop(0, limit, step, state)
    for i in range(limit):
        state = step(i, state)
    return state


def locate(table, row, column, slots):
    def step(p, found):
        device, slot = split(table[p, row], slots)
        here = device == column
        return jnp.where(here, p, found[0]), jnp.where(here, slot, found[1])

    return count_up(table.shape[0], step, (jnp.int32(0), jnp.int32(0)))


def pair_row(moves, source, target, rows, side):
    def step(j, found):
        valid, row, order, number = found
        ends = [split(moves[i, j], rows) for i in range(2)]
        match = (ends[0][0] == source) & (ends[1][0] == target)
        return (
            jnp.where(match, jnp.int32(1), valid),
            jnp.where(match, ends[side][1], row),
            jnp.where(match, number, order),
            number + jnp.where(ends[side][0] == (source, target)[side], 1, 0),
        )

    return count_up(moves.shape[1], step, (jnp.int32(0),) * 4)[:3]


def head_columns(device, local_heads):
    return pl.ds(pl.multiple_of(split(device * local_heads, GROUP)[0] * HD, HD), HD)


def weight_of(score):
    return jnp.exp(CAP * jnp.tanh(score * (SCALE / CAP)))


def pieces_of(width):
    return [slice(at, at + HD) for at in range(0, width, HD)]


def page_lines(width, page_size):
    return [j * page_size for j in range(width // HD)]


def extra_lines(depth):
    return -(-(2 + depth // HD) // 8) * 8


def start_copies(pairs, sems):
    copies = [pltpu.make_async_copy(*pair, sems.at[i]) for i, pair in enumerate(pairs)]
    for copy in copies:
        copy.start()
    return copies


def wait_for(copies):
    for copy in copies:
        copy.wait()


def leave_kernel(rows, moves_all, table_all, lengths_all, x_all, pool, *refs):
    held, pages, (moves, table, lengths, x, sems, pool_sems) = refs[0], refs[1:-6], refs[-6:]
    me, column = lax.axis_index("replica"), lax.axis_index("mp")
    page_size, width = pool.shape[1:]
    depth = x.shape[1]
    rest = start_copies(
        ((moves_all, moves), (table_all, table), (lengths_all, lengths), (x_all, x)), sems
    )
    copies = start_copies([(pool.at[i], held.at[i]) for i in range(pool.shape[0])], pool_sems)
    wait_for(rest[:2])
    found = [pair_row(moves, me, partner("replica", s + 1), rows, 0)[1] for s in range(len(pages))]
    picks = [locate(table, row, column, pool.shape[0])[1] for row in found]
    wait_for(rest[2:])
    lines = extra_lines(depth)
    sublane = lax.broadcasted_iota(jnp.int32, (lines, HD), 0)
    first_rows = x[:rows, :].astype(jnp.float32)
    row_ids = lax.broadcasted_iota(jnp.int32, (rows, depth), 0)
    for row, page in zip(found, pages):
        high, low = split(lengths[row], 64)
        picked = jnp.sum(jnp.where(row_ids == row, first_rows, 0.0), axis=0, keepdims=True)
        parts = [jnp.zeros((2, HD), jnp.float32)] + [picked[:, piece] for piece in pieces_of(depth)]
        spare = lines - 2 - depth // HD
        parts += [jnp.zeros((spare, HD), jnp.float32)] if spare else []
        extra = jnp.concatenate(parts, axis=0)
        extra = jnp.where(sublane == 0, high.astype(jnp.float32), extra)
        extra = jnp.where(sublane == 1, low.astype(jnp.float32), extra)
        page[page_size * width // HD :, :] = extra.astype(jnp.bfloat16)
    wait_for(copies)
    for slot, page in zip(picks, pages):
        for line, piece in zip(page_lines(width, page_size), pieces_of(width)):
            page[line : line + page_size, :] = held[slot, :, piece]


def open_kernel(count, local_heads, x, q, weight, *refs):
    outs, (held, weight_sems) = refs[:-2], refs[-2:]
    depth, chunks = weight.shape[0], weight_sems.shape[0]
    spans = [pl.ds(c * (depth // chunks), depth // chunks) for c in range(chunks)]
    loads = start_copies([(weight.at[span], held.at[span]) for span in spans], weight_sems)
    rows = q.shape[1]
    wide = [q[i].astype(jnp.float32) for i in range(2)]
    blocks = [wide[i][:, h * HD : (h + 1) * HD] for i in range(2) for h in range(local_heads)]
    packed = jnp.concatenate(blocks, axis=0).astype(jnp.bfloat16)
    query_rows = packed.shape[0]
    for out in outs:
        out[:query_rows, :] = packed
    total = jnp.zeros((x.shape[0], weight.shape[1]), jnp.float32)
    for span, load in zip(spans, loads):
        load.wait()
        total += jnp.dot(x[:, span], held[span, :], preferred_element_type=jnp.float32)
    for j in range(KVH):
        parts = []
        for half in range(2):
            start = (half * KVH + j) * HD
            part = total[:, start : start + HD]
            high = part.astype(jnp.bfloat16)
            parts += [high, (part - high.astype(jnp.float32)).astype(jnp.bfloat16)]
        parts = jnp.concatenate(parts, axis=0)
        for s, out in enumerate(outs):

            @pl.when(split(partner("mp", s) * local_heads, GROUP)[0] == j)
            def _(out=out, parts=parts):
                out[query_rows:, :] = parts


def keep_kernel(replicas, *refs):
    pages_in, (pool, moves_all, table_all, pool_out, moves, table, sems, page_sems) = (
        refs[: replicas - 1],
        refs[replicas - 1 :],
    )
    wait_for(start_copies(((moves_all, moves), (table_all, table)), sems))
    me, column = lax.axis_index("replica"), lax.axis_index("mp")
    rows = table.shape[1]
    slots, page_size, width = pool.shape
    kept, copies = [jnp.bool_(True)] * rows, []
    for s, page in enumerate(pages_in):
        valid, row, _ = pair_row(moves, partner("replica", s + 1), me, rows, 1)
        kept = [stays & ~((valid == 1) & (row == r)) for r, stays in enumerate(kept)]
        copies.append((valid == 1, row, page))
    copies += [(stays, r, None) for r, stays in enumerate(kept)]
    started = []
    for n, (active, row, page) in enumerate(copies):
        _, slot = locate(table, row, column, slots)
        pairs = [(pool.at[slot], pool_out.at[slot])]
        if page is not None:
            pairs = [
                (page.at[pl.ds(line, page_size)], pool_out.at[slot, :, piece])
                for line, piece in zip(page_lines(width, page_size), pieces_of(width))
            ]
        parts = [pltpu.make_async_copy(*pair, page_sems.at[n, i]) for i, pair in enumerate(pairs)]
        started.append((active, parts))

        @pl.when(active)
        def _(parts=parts):
            for copy in parts:
                copy.start()

    for active, parts in started:
        pl.when(active)(functools.partial(wait_for, parts))


def extra_of(page, page_size, width):
    return page[page_size * width // HD :, :].astype(jnp.float32)


def length_of(extra):
    return extra[0:1] * 64.0 + extra[1:2]


def own_tokens(messages, rows, query_rows, half):
    tokens = 2 * rows
    start = query_rows + 2 * half * tokens
    total = jnp.zeros((tokens, HD), jnp.float32)
    for message in messages:
        total += message[start : start + tokens, :].astype(jnp.float32)
        total += message[start + tokens : start + 2 * tokens, :].astype(jnp.float32)
    return total.astype(jnp.bfloat16).astype(jnp.float32)


def scores_of(q, keys):
    return lax.dot_general(q, keys, (((1,), (1,)), ((), ())), preferred_element_type=jnp.float32)


def attend_kernel(count, local_heads, table, lengths, pool, *refs):
    messages = by_distance(refs[:count])
    num, den, wide = refs[count:]
    column = lax.axis_index("mp")
    rows = lengths.shape[0]
    slots, page_size, width = pool.shape
    both = 2 * local_heads
    for s, message in enumerate(messages):
        wide[s] = message[: both * rows, :].astype(jnp.float32)
    lane = lax.broadcasted_iota(jnp.int32, (both, HD), 1)
    token = lax.broadcasted_iota(jnp.int32, (both, page_size), 1)
    places = [locate(table, r, column, slots) for r in range(rows)]
    columns = [head_columns(partner("mp", s), local_heads) for s in range(count)]
    keys = pool.at[:, :, pl.ds(0, width // 2)]
    values = pool.at[:, :, pl.ds(width // 2, width // 2)]
    cases = [(r, s) for r in range(rows) for s in range(count)]
    scores = {}
    for r, s in cases:
        q = wide[s, pl.ds(r, both, stride=rows), :].astype(jnp.bfloat16)
        scores[r, s] = scores_of(q, keys[places[r][1], :, columns[s]])
    weights = {}
    denominators = [jnp.zeros((both, HD), jnp.float32) for _ in range(count)]
    for r, s in cases:
        inside = token < lengths[r] - places[r][0] * page_size
        weight = jnp.where(inside, weight_of(scores[r, s]), 0.0)
        weights[r, s] = weight.astype(jnp.bfloat16)
        total = jnp.sum(weight, axis=1, keepdims=True)
        denominators[s] += jnp.where(lane == r, total, 0.0)
    for r, s in cases:
        num[s, pl.ds(r, both, stride=rows), :] = jnp.dot(
            weights[r, s], values[places[r][1], :, columns[s]], preferred_element_type=jnp.float32
        )
    for s in range(count):
        den[s] = denominators[s]


def arrive_kernel(count, replicas, local_heads, slots, page_size, *refs):
    refs = list(refs)
    take = lambda n: [refs.pop(0) for _ in range(n)]
    pages_in = take(replicas - 2)
    moves_all, table_all, projection = take(3)
    pages_in, messages = take(1) + pages_in, by_distance(take(count))
    num_in, den_in = take(2)
    outs = take(count - 1)
    own_num, own_den, own_kv, own_share, marks, num, den, wide, moves, table, sems = refs
    tables = start_copies(((moves_all, moves), (table_all, table)), sems)
    me, column = lax.axis_index("replica"), lax.axis_index("mp")
    rows = table.shape[1]
    depth, width = projection.shape
    half_rows = local_heads * rows
    movers = moves.shape[1] // replicas

    extra = [extra_of(page, page_size, width) for page in pages_in]
    inputs = [
        jnp.concatenate([part[2 + i : 3 + i] for i in range(depth // HD)], axis=1) for part in extra
    ]
    inputs += [jnp.zeros((8 - len(inputs), depth), jnp.float32)]
    inputs = jnp.concatenate(inputs, axis=0).astype(jnp.bfloat16)
    share = jnp.dot(inputs, projection[...], preferred_element_type=jnp.float32)
    num[...] = num_in[...]
    den[...] = den_in[...]
    for s, message in enumerate(messages):
        wide[s] = message[half_rows : 2 * half_rows, :].astype(jnp.float32)
    lengths = [length_of(part) for part in extra]

    wait_for(tables)
    lane = lax.broadcasted_iota(jnp.int32, (local_heads, HD), 1)
    token = lax.broadcasted_iota(jnp.int32, (local_heads, page_size), 1)
    lines = [
        pl.multiple_of(split(partner("mp", s) * local_heads, GROUP)[0] * page_size, page_size) for s in range(count)
    ]
    cases = [(d, s) for d in range(1, replicas) for s in range(count)]
    arrivals = [pair_row(moves, partner("replica", d), me, rows, 1) for d in range(1, replicas)]
    places = [locate(table, row, column, slots) for _, row, _ in arrivals]
    scores, weights, totals = {}, {}, {}
    for d, s in cases:
        row = arrivals[d - 1][1]
        q = wide[s, pl.ds(row, local_heads, stride=rows), :].astype(jnp.bfloat16)
        scores[d, s] = scores_of(q, pages_in[d - 1][pl.ds(lines[s], page_size), :])
    for d, s in cases:
        inside = (token + places[d - 1][0] * page_size).astype(jnp.float32) < lengths[d - 1]
        weight = jnp.where(inside, weight_of(scores[d, s]), 0.0)
        weights[d, s] = weight.astype(jnp.bfloat16)
        totals[d, s] = jnp.sum(weight, axis=1, keepdims=True)
    for d, s in cases:
        values = pages_in[d - 1][pl.ds(lines[s] + KVH * page_size, page_size), :]
        scores[d, s] = jnp.dot(weights[d, s], values, preferred_element_type=jnp.float32)
    for d, (valid, row, _) in enumerate(arrivals, 1):

        @pl.when(valid == 1)
        def _(d=d, row=row):
            for s in range(count):
                num[s, pl.ds(half_rows + row, local_heads, stride=rows), :] = scores[d, s]
                old = den[s, pl.ds(local_heads, local_heads), :]
                den[s, pl.ds(local_heads, local_heads), :] = jnp.where(lane == row, totals[d, s], old)

    arrived = []
    row_ids = lax.broadcasted_iota(jnp.int32, (rows, HD), 0)
    for number in range(movers):
        picked = jnp.zeros((1, width), jnp.float32)
        mark = jnp.zeros((rows, HD), jnp.float32)
        for d, (valid, row, order) in enumerate(arrivals):
            here = (valid == 1) & (order == number)
            picked = jnp.where(here, share[d : d + 1], picked)
            mark = jnp.where(here & (row_ids == row), 1.0, mark)
        part = jnp.concatenate([picked[:, j * HD : (j + 1) * HD] for j in range(2 * KVH)], axis=0)
        high = part.astype(jnp.bfloat16).astype(jnp.float32)
        arrived += [high, part - high]
        own_share[number] = part
        marks[number] = mark
    own_num[...] = num[0]
    own_den[...] = den[0]
    all_kv = []
    for half in range(2):
        own_kv[half] = own_tokens(messages, rows, 2 * half_rows, half)
        all_kv.append(own_kv[half])
    filler = [jnp.zeros((-2 * local_heads % 16, HD), jnp.float32)] if local_heads % 8 else []
    for s, out in enumerate(outs):
        at = s + 1
        parts = den[at]
        high = parts.astype(SEND).astype(jnp.float32)
        parts = high + pltpu.roll(parts - high, HD // 2, 1)
        out[...] = jnp.concatenate([num[at], parts] + filler + all_kv + arrived, axis=0).astype(SEND)


def finish_kernel(count, replicas, local_heads, *refs):
    refs = list(refs)
    take = lambda n: [refs.pop(0) for _ in range(n)]
    pages_in = take(replicas - 2)
    moves_all, table_all, lengths_all, kv, share, marks, q, num, den = take(9)
    pages_in, messages = take(1) + pages_in, by_distance(take(count - 1))
    pool_raw, _, first, second, pool = take(5)
    moves, table, lengths, full, arrived, windows, results, sems, write_sems, out_sems = refs
    tables = start_copies(((moves_all, moves), (table_all, table), (lengths_all, lengths)), sems)
    me, column = lax.axis_index("replica"), lax.axis_index("mp")
    rows = lengths.shape[0]
    slots, page_size, width = pool_raw.shape
    both = 2 * local_heads
    query_rows = both * rows
    movers = moves.shape[1] // replicas
    head = split(column * local_heads, GROUP)[0]

    kv_base = messages[0].shape[0] - 4 * rows - 16 * movers
    for s in range(count):
        device = partner("mp", s)
        for half in range(2):
            if s == 0:
                chunk = kv[half]
            else:
                start = kv_base + half * 2 * rows
                chunk = messages[s - 1][start : start + 2 * rows, :].astype(jnp.float32)

            def place(half=half, device=device, chunk=chunk):
                columns = head_columns(device, local_heads)
                full.at[pl.ds(0, 2 * rows), pl.ds(half * (width // 2), width // 2)][:, columns] = chunk

            if local_heads == GROUP:
                place()
            else:
                pl.when(split(device * local_heads, GROUP)[1] == 0)(place)
    for number in range(movers):
        total = share[number]
        for message in messages:
            start = kv_base + 4 * rows + 16 * number
            part = message[start : start + 16, :].astype(jnp.float32)
            total += part[: 2 * KVH] + part[2 * KVH :]
        total = total.astype(jnp.bfloat16).astype(jnp.float32)
        arrived[number] = total
        for j in range(2 * KVH):
            full[2 * rows + number : 2 * rows + number + 1, j * HD : (j + 1) * HD] = total[j : j + 1, :]
    sums = den[...]
    for message in messages:
        part = message[query_rows : query_rows + both, :].astype(jnp.float32)
        sums += part + pltpu.roll(part, HD // 2, 1)
    sums = jnp.transpose(sums)[:rows, :]

    held = []
    for half in range(2):
        value = kv[half, :rows, :]
        for number in range(movers):
            moved = arrived[number, pl.ds(head + half * KVH, 1), :]
            value = jnp.where(marks[number] > 0.5, moved, value)
        held.append(value)
    outs = []

    def finish_step(step, out):
        pieces = []
        for h in range(local_heads):
            at = (step * local_heads + h) * rows
            query = q[at : at + rows, :].astype(jnp.float32)
            numerator = num[at : at + rows, :]
            for message in messages:
                numerator += message[at : at + rows, :].astype(jnp.float32)
            denominator = sums[:, step * local_heads + h : step * local_heads + h + 1]
            extra = [(kv[0, :rows, :], kv[1, :rows, :])]
            if step == 1:
                extra = [held, (kv[0, rows:, :], kv[1, rows:, :])]
            for key, value in extra:
                weight = weight_of(jnp.sum(query * key, axis=1, keepdims=True))
                numerator += weight.astype(jnp.bfloat16).astype(jnp.float32) * value
                denominator += weight
            pieces.append(numerator / denominator)
        results[step] = jnp.concatenate(pieces, axis=1).astype(out.dtype)
        outs.append(pltpu.make_async_copy(results.at[step], out, out_sems.at[step]))
        outs[-1].start()

    finish_step(0, first)
    wait_for(tables)
    kept, plans = [jnp.bool_(True)] * rows, []

    def add_plan(active, row, length, first_token, source, r=None):
        index, slot = locate(table, row, column, slots)
        at = length - index * page_size
        touched = active & (at >= -1) & (at < page_size)
        start = jnp.clip(at, 0, page_size - WINDOW) & -16
        span = pl.ds(pl.multiple_of(start, 16), WINDOW)
        n = len(plans)
        if r is None:
            read = lambda: jnp.concatenate(
                [source[pl.ds(pl.multiple_of(line + start, 16), WINDOW), :] for line in page_lines(width, page_size)],
                axis=1,
            )
        else:
            read = lambda: source[slot, span, :]
        write = pltpu.make_async_copy(windows.at[n], pool.at[slot, span], write_sems.at[n])
        plans.append((touched, read, write, first_token, rows + row, at - start))

    for s, page in enumerate(pages_in):
        valid, row, order = pair_row(moves, partner("replica", s + 1), me, rows, 1)
        valid = valid == 1
        length = jnp.max(length_of(extra_of(page, page_size, width))).astype(jnp.int32)
        add_plan(valid, row, length, 2 * rows + order, page)
        kept = [stays & ~(valid & (row == r)) for r, stays in enumerate(kept)]
    for r in range(rows):
        add_plan(kept[r], r, lengths[r], r, pool_raw, r)

    place_ids = lax.broadcasted_iota(jnp.int32, (WINDOW, width), 0)
    for n, (touched, read, write, token, next_token, offset) in enumerate(plans):

        @pl.when(touched)
        def _(n=n, read=read, write=write, token=token, next_token=next_token, offset=offset):
            old = read().astype(jnp.float32)
            new = jnp.where(place_ids == offset, full[pl.ds(token, 1), :], old)
            new = jnp.where(place_ids == offset + 1, full[pl.ds(next_token, 1), :], new)
            windows[n] = new.astype(jnp.bfloat16)
            write.start()

    finish_step(1, second)
    for plan in plans:
        pl.when(plan[0])(plan[2].wait)
    wait_for(outs)


def cost(microseconds):
    return pl.CostEstimate(flops=0, transcendentals=0, bytes_accessed=int(microseconds * 3.5e6))


def in_vmem(value):
    return pltpu.with_memory_space_constraint(value, pltpu.VMEM)


def in_hbm(value):
    return pltpu.with_memory_space_constraint(value, pltpu.HBM)


def params(megabytes=32, **rest):
    return pltpu.CompilerParams(vmem_limit_bytes=megabytes << 20, **rest)


def body(layer_input, kv_weight, queries, kv_pool, lengths, block_table, new_table, migrations):
    replicas, count = lax.axis_size("replica"), lax.axis_size("mp")
    rows = lengths.shape[0]
    pool = kv_pool[0, 0]
    slots, page_size, width = pool.shape
    local_heads = queries.shape[2] // HD
    both = 2 * local_heads
    query_rows = both * rows
    depth = layer_input.shape[2]
    f32, bf16 = jnp.float32, jnp.bfloat16
    moves, old_table, table_after = migrations.T, block_table.T, new_table.T
    shape = jax.ShapeDtypeStruct

    message_rows = query_rows + 8 * rows
    movers = migrations.shape[0] // replicas
    inputs = layer_input.reshape(2 * rows, depth)
    pool_near, *leaving = pl.pallas_call(
        functools.partial(leave_kernel, rows),
        out_shape=[shape(pool.shape, bf16)] + [shape((page_size * width // HD + extra_lines(depth), HD), bf16)] * (replicas - 1),
        in_specs=[HBM] * 5,
        out_specs=[VMEM] * replicas,
        scratch_shapes=[
            pltpu.SMEM(moves.shape, jnp.int32),
            pltpu.SMEM(old_table.shape, jnp.int32),
            pltpu.SMEM(lengths.shape, jnp.int32),
            pltpu.VMEM((2 * rows, depth), bf16),
            pltpu.SemaphoreType.DMA((4,)),
            pltpu.SemaphoreType.DMA((slots,)),
        ],
        compiler_params=params(),
        cost_estimate=cost(1.8),
        name="leave",
    )(*map(in_hbm, (moves, old_table, lengths, inputs, pool)))
    pages_in = exchange(leaving, "replica")

    weight_near, inputs_near, queries_near = map(in_vmem, (kv_weight, inputs, queries))
    sent = pl.pallas_call(
        functools.partial(open_kernel, count, local_heads),
        out_shape=[shape((message_rows, HD), bf16)] * count,
        in_specs=[VMEM] * 2 + [HBM],
        out_specs=[VMEM] * count,
        scratch_shapes=[pltpu.VMEM((depth, width), bf16), pltpu.SemaphoreType.DMA((8,))],
        compiler_params=params(),
        cost_estimate=cost(1.2),
        name="open",
    )(inputs_near, queries_near, in_hbm(kv_weight))
    sent, pages_in[0] = lax.optimization_barrier((list(sent), pages_in[0]))
    messages = [sent[0]] + exchange(sent[1:], "mp")

    num, den = pl.pallas_call(
        functools.partial(attend_kernel, count, local_heads),
        out_shape=[shape((count, query_rows, HD), f32), shape((count, both, HD), f32)],
        in_specs=[SMEM, SMEM, VMEM] + [VMEM] * count,
        out_specs=[VMEM, VMEM],
        scratch_shapes=[pltpu.VMEM((count, query_rows, HD), f32)],
        compiler_params=params(),
        cost_estimate=cost(1.5),
        name="attend",
    )(old_table, lengths, pool_near, *by_start(messages))

    sum_rows = query_rows + -(-both // 16) * 16 + 4 * rows + 16 * movers
    *sums, num, den, kv, share, marks = pl.pallas_call(
        functools.partial(arrive_kernel, count, replicas, local_heads, slots, page_size),
        out_shape=[shape((sum_rows, HD), SEND)] * (count - 1)
        + [shape((query_rows, HD), f32), shape((both, HD), f32)]
        + [shape((2, 2 * rows, HD), f32), shape((movers, 2 * KVH, HD), f32)]
        + [shape((movers, rows, HD), f32)],
        in_specs=[VMEM] * (replicas - 2)
        + [ANY, ANY, VMEM, VMEM]
        + [VMEM] * count
        + [VMEM] * 2,
        out_specs=[VMEM] * (count + 4),
        scratch_shapes=[
            pltpu.VMEM((count, query_rows, HD), f32),
            pltpu.VMEM((count, both, HD), f32),
            pltpu.VMEM((count, query_rows // 2, HD), f32),
            pltpu.SMEM(moves.shape, jnp.int32),
            pltpu.SMEM(table_after.shape, jnp.int32),
            pltpu.SemaphoreType.DMA((2,)),
        ],
        compiler_params=params(),
        cost_estimate=cost(1.2),
        name="arrive",
    )(*pages_in[1:], moves, table_after, weight_near, pages_in[0], *by_start(messages), num, den)
    sums_in = exchange(sums, "mp")

    moves_then, _ = lax.optimization_barrier((moves, marks))

    pool_copy = pl.pallas_call(
        functools.partial(keep_kernel, replicas),
        out_shape=shape(pool.shape, bf16),
        in_specs=[VMEM] * replicas + [ANY] * 2,
        out_specs=ANY,
        scratch_shapes=[
            pltpu.SMEM(moves.shape, jnp.int32),
            pltpu.SMEM(table_after.shape, jnp.int32),
            pltpu.SemaphoreType.DMA((2,)),
            pltpu.SemaphoreType.DMA((rows + replicas - 1, width // HD)),
        ],
        compiler_params=params(),
        cost_estimate=cost(1.6),
        name="keep",
    )(*pages_in, pool_near, moves_then, table_after)

    first, second, pool_after = pl.pallas_call(
        functools.partial(finish_kernel, count, replicas, local_heads),
        out_shape=[
            shape((rows, local_heads * HD), bf16),
            shape((rows, local_heads * HD), bf16),
            shape(pool.shape, bf16),
        ],
        in_specs=[VMEM] * (replicas - 2) + [ANY] * 3 + [VMEM] * (7 + count - 1) + [VMEM, ANY],
        out_specs=[ANY] * 3,
        scratch_shapes=[
            pltpu.SMEM(moves.shape, jnp.int32),
            pltpu.SMEM(table_after.shape, jnp.int32),
            pltpu.SMEM(lengths.shape, jnp.int32),
            pltpu.VMEM((KV_ROWS, width), f32),
            pltpu.VMEM((movers, 2 * KVH, HD), f32),
            pltpu.VMEM((rows + replicas - 1, WINDOW, width), bf16),
            pltpu.VMEM((2, rows, local_heads * HD), bf16),
            pltpu.SemaphoreType.DMA((3,)),
            pltpu.SemaphoreType.DMA((rows + replicas - 1,)),
            pltpu.SemaphoreType.DMA((2,)),
        ],
        input_output_aliases={9 + replicas - 1 + (count - 1) + 1: 2},
        compiler_params=params(),
        cost_estimate=cost(2.5),
        name="finish",
    )(
        *pages_in[1:],
        *(moves, table_after, lengths),
        *(kv, share, marks, messages[0], num, den, pages_in[0]),
        *by_start(sums_in),
        *(pool_near, pool_copy),
    )
    return first, second, pool_after[None, None]


def solution(mesh):
    return jax.shard_map(
        body,
        mesh=mesh,
        in_specs=(
            P(None, ("groups", "replica"), "mp"),
            P("mp", None),
            P(None, ("groups", "replica"), "mp"),
            P(("groups", "replica"), "mp", None, None, None),
            P(("groups", "replica")),
            P(("groups", "replica"), None),
            P(("groups", "replica"), None),
            P("groups", None),
        ),
        out_specs=(
            P(("groups", "replica"), "mp"),
            P(("groups", "replica"), "mp"),
            P(("groups", "replica"), "mp", None, None, None),
        ),
        check_vma=False,
    )
```

```python
import functools
import math

import jax
import jax.numpy as jnp
from jax import lax
from jax.experimental import pallas as pl
from jax.experimental.pallas import tpu as pltpu
from jax.sharding import PartitionSpec as P

H = 32
KVH = 4
HD = 128
GROUP = H // KVH
CAP = 20.0
SCALE = 1.0 / math.sqrt(HD)
WINDOW = 32
KV_ROWS = 24

SMEM = pl.BlockSpec(memory_space=pltpu.SMEM)
VMEM = pl.BlockSpec(memory_space=pltpu.VMEM)
ANY = pl.BlockSpec(memory_space=pl.ANY)
HBM = pl.BlockSpec(memory_space=pltpu.HBM)
SEND = jnp.bfloat16


def swap(value, axis, distance):
    size = lax.axis_size(axis)
    return lax.ppermute(value, axis, [(i, i ^ distance) for i in range(size)])


def exchange(messages, axis):
    received = [swap(messages[d], axis, d + 1) for d in reversed(range(len(messages)))]
    return received[::-1]


def start_order(count):
    return [count // 2] + [d for d in range(count - 1, 0, -1) if d != count // 2]


def by_start(values):
    own = len(values) & 1 ^ 1
    order = start_order(len(values) + 1 - own)
    return [values[d - 1 + own] for d in order] + list(values[:own])


def by_distance(values):
    own = len(values) & 1 ^ 1
    order = start_order(len(values) + 1 - own)
    return list(values[len(order) :]) + [values[order.index(d)] for d in range(1, len(order) + 1)]


def partner(axis, distance):
    return lax.axis_index(axis) ^ distance


def split(value, size):
    if size & (size - 1) == 0:
        return lax.shift_right_logical(value, size.bit_length() - 1), value & (size - 1)
    return lax.div(value, size), lax.rem(value, size)


def count_up(limit, step, state):
    if limit > 8:
        return lax.fori_loop(0, limit, step, state)
    for i in range(limit):
        state = step(i, state)
    return state


def locate(table, row, column, slots):
    def step(p, found):
        device, slot = split(table[p, row], slots)
        here = device == column
        return jnp.where(here, p, found[0]), jnp.where(here, slot, found[1])

    return count_up(table.shape[0], step, (jnp.int32(0), jnp.int32(0)))


def pair_row(moves, source, target, rows, side):
    def step(j, found):
        valid, row, order, number = found
        ends = [split(moves[i, j], rows) for i in range(2)]
        match = (ends[0][0] == source) & (ends[1][0] == target)
        return (
            jnp.where(match, jnp.int32(1), valid),
            jnp.where(match, ends[side][1], row),
            jnp.where(match, number, order),
            number + jnp.where(ends[side][0] == (source, target)[side], 1, 0),
        )

    return count_up(moves.shape[1], step, (jnp.int32(0),) * 4)[:3]


def head_columns(device, local_heads):
    return pl.ds(pl.multiple_of(split(device * local_heads, GROUP)[0] * HD, HD), HD)


def weight_of(score):
    return jnp.exp(CAP * jnp.tanh(score * (SCALE / CAP)))


def pieces_of(width):
    return [slice(at, at + HD) for at in range(0, width, HD)]


def page_lines(width, page_size):
    return [j * page_size for j in range(width // HD)]


def extra_lines(depth):
    return -(-(2 + depth // HD) // 8) * 8


def start_copies(pairs, sems):
    copies = [pltpu.make_async_copy(*pair, sems.at[i]) for i, pair in enumerate(pairs)]
    for copy in copies:
        copy.start()
    return copies


def wait_for(copies):
    for copy in copies:
        copy.wait()


def leave_kernel(rows, moves_all, table_all, lengths_all, x_all, pool, *refs):
    held, pages, (moves, table, lengths, x, sems, pool_sems) = refs[0], refs[1:-6], refs[-6:]
    me, column = lax.axis_index("replica"), lax.axis_index("mp")
    page_size, width = pool.shape[1:]
    depth = x.shape[1]
    rest = start_copies(
        ((moves_all, moves), (table_all, table), (lengths_all, lengths), (x_all, x)), sems
    )
    copies = start_copies([(pool.at[i], held.at[i]) for i in range(pool.shape[0])], pool_sems)
    wait_for(rest[:2])
    found = [pair_row(moves, me, partner("replica", s + 1), rows, 0)[1] for s in range(len(pages))]
    picks = [locate(table, row, column, pool.shape[0])[1] for row in found]
    wait_for(rest[2:])
    lines = extra_lines(depth)
    sublane = lax.broadcasted_iota(jnp.int32, (lines, HD), 0)
    first_rows = x[:rows, :].astype(jnp.float32)
    row_ids = lax.broadcasted_iota(jnp.int32, (rows, depth), 0)
    for row, page in zip(found, pages):
        high, low = split(lengths[row], 64)
        picked = jnp.sum(jnp.where(row_ids == row, first_rows, 0.0), axis=0, keepdims=True)
        parts = [jnp.zeros((2, HD), jnp.float32)] + [picked[:, piece] for piece in pieces_of(depth)]
        spare = lines - 2 - depth // HD
        parts += [jnp.zeros((spare, HD), jnp.float32)] if spare else []
        extra = jnp.concatenate(parts, axis=0)
        extra = jnp.where(sublane == 0, high.astype(jnp.float32), extra)
        extra = jnp.where(sublane == 1, low.astype(jnp.float32), extra)
        page[page_size * width // HD :, :] = extra.astype(jnp.bfloat16)
    wait_for(copies)
    for slot, page in zip(picks, pages):
        for line, piece in zip(page_lines(width, page_size), pieces_of(width)):
            page[line : line + page_size, :] = held[slot, :, piece]


def open_kernel(count, local_heads, x, q, weight, *refs):
    outs, (held, weight_sems) = refs[:-2], refs[-2:]
    depth, chunks = weight.shape[0], weight_sems.shape[0]
    spans = [pl.ds(c * (depth // chunks), depth // chunks) for c in range(chunks)]
    loads = start_copies([(weight.at[span], held.at[span]) for span in spans], weight_sems)
    rows = q.shape[1]
    wide = [q[i].astype(jnp.float32) for i in range(2)]
    blocks = [wide[i][:, h * HD : (h + 1) * HD] for i in range(2) for h in range(local_heads)]
    packed = jnp.concatenate(blocks, axis=0).astype(jnp.bfloat16)
    query_rows = packed.shape[0]
    for out in outs:
        out[:query_rows, :] = packed
    total = jnp.zeros((x.shape[0], weight.shape[1]), jnp.float32)
    for span, load in zip(spans, loads):
        load.wait()
        total += jnp.dot(x[:, span], held[span, :], preferred_element_type=jnp.float32)
    for j in range(KVH):
        parts = []
        for half in range(2):
            start = (half * KVH + j) * HD
            part = total[:, start : start + HD]
            high = part.astype(jnp.bfloat16)
            parts += [high, (part - high.astype(jnp.float32)).astype(jnp.bfloat16)]
        parts = jnp.concatenate(parts, axis=0)
        for s, out in enumerate(outs):

            @pl.when(split(partner("mp", s) * local_heads, GROUP)[0] == j)
            def _(out=out, parts=parts):
                out[query_rows:, :] = parts


def keep_kernel(replicas, *refs):
    pages_in, (pool, moves_all, table_all, pool_out, moves, table, sems, page_sems) = (
        refs[: replicas - 1],
        refs[replicas - 1 :],
    )
    wait_for(start_copies(((moves_all, moves), (table_all, table)), sems))
    me, column = lax.axis_index("replica"), lax.axis_index("mp")
    rows = table.shape[1]
    slots, page_size, width = pool.shape
    kept, copies = [jnp.bool_(True)] * rows, []
    for s, page in enumerate(pages_in):
        valid, row, _ = pair_row(moves, partner("replica", s + 1), me, rows, 1)
        kept = [stays & ~((valid == 1) & (row == r)) for r, stays in enumerate(kept)]
        copies.append((valid == 1, row, page))
    copies += [(stays, r, None) for r, stays in enumerate(kept)]
    started = []
    for n, (active, row, page) in enumerate(copies):
        _, slot = locate(table, row, column, slots)
        pairs = [(pool.at[slot], pool_out.at[slot])]
        if page is not None:
            pairs = [
                (page.at[pl.ds(line, page_size)], pool_out.at[slot, :, piece])
                for line, piece in zip(page_lines(width, page_size), pieces_of(width))
            ]
        parts = [pltpu.make_async_copy(*pair, page_sems.at[n, i]) for i, pair in enumerate(pairs)]
        started.append((active, parts))

        @pl.when(active)
        def _(parts=parts):
            for copy in parts:
                copy.start()

    for active, parts in started:
        pl.when(active)(functools.partial(wait_for, parts))


def extra_of(page, page_size, width):
    return page[page_size * width // HD :, :].astype(jnp.float32)


def length_of(extra):
    return extra[0:1] * 64.0 + extra[1:2]


def own_tokens(messages, rows, query_rows, half):
    tokens = 2 * rows
    start = query_rows + 2 * half * tokens
    total = jnp.zeros((tokens, HD), jnp.float32)
    for message in messages:
        total += message[start : start + tokens, :].astype(jnp.float32)
        total += message[start + tokens : start + 2 * tokens, :].astype(jnp.float32)
    return total.astype(jnp.bfloat16).astype(jnp.float32)


def scores_of(q, keys):
    return lax.dot_general(q, keys, (((1,), (1,)), ((), ())), preferred_element_type=jnp.float32)


def attend_kernel(count, local_heads, table, lengths, pool, *refs):
    messages = by_distance(refs[:count])
    num, den, wide = refs[count:]
    column = lax.axis_index("mp")
    rows = lengths.shape[0]
    slots, page_size, width = pool.shape
    both = 2 * local_heads
    for s, message in enumerate(messages):
        wide[s] = message[: both * rows, :].astype(jnp.float32)
    lane = lax.broadcasted_iota(jnp.int32, (both, HD), 1)
    token = lax.broadcasted_iota(jnp.int32, (both, page_size), 1)
    places = [locate(table, r, column, slots) for r in range(rows)]
    columns = [head_columns(partner("mp", s), local_heads) for s in range(count)]
    keys = pool.at[:, :, pl.ds(0, width // 2)]
    values = pool.at[:, :, pl.ds(width // 2, width // 2)]
    cases = [(r, s) for r in range(rows) for s in range(count)]
    scores = {}
    for r, s in cases:
        q = wide[s, pl.ds(r, both, stride=rows), :].astype(jnp.bfloat16)
        scores[r, s] = scores_of(q, keys[places[r][1], :, columns[s]])
    weights = {}
    denominators = [jnp.zeros((both, HD), jnp.float32) for _ in range(count)]
    for r, s in cases:
        inside = token < lengths[r] - places[r][0] * page_size
        weight = jnp.where(inside, weight_of(scores[r, s]), 0.0)
        weights[r, s] = weight.astype(jnp.bfloat16)
        total = jnp.sum(weight, axis=1, keepdims=True)
        denominators[s] += jnp.where(lane == r, total, 0.0)
    for r, s in cases:
        num[s, pl.ds(r, both, stride=rows), :] = jnp.dot(
            weights[r, s], values[places[r][1], :, columns[s]], preferred_element_type=jnp.float32
        )
    for s in range(count):
        den[s] = denominators[s]


def arrive_kernel(count, replicas, local_heads, slots, page_size, *refs):
    refs = list(refs)
    take = lambda n: [refs.pop(0) for _ in range(n)]
    pages_in = take(replicas - 2)
    moves_all, table_all, projection = take(3)
    pages_in, messages = take(1) + pages_in, by_distance(take(count))
    num_in, den_in = take(2)
    outs = take(count - 1)
    own_num, own_den, own_kv, own_share, marks, num, den, wide, moves, table, sems = refs
    tables = start_copies(((moves_all, moves), (table_all, table)), sems)
    me, column = lax.axis_index("replica"), lax.axis_index("mp")
    rows = table.shape[1]
    depth, width = projection.shape
    half_rows = local_heads * rows
    movers = moves.shape[1] // replicas

    extra = [extra_of(page, page_size, width) for page in pages_in]
    inputs = [
        jnp.concatenate([part[2 + i : 3 + i] for i in range(depth // HD)], axis=1) for part in extra
    ]
    inputs += [jnp.zeros((8 - len(inputs), depth), jnp.float32)]
    inputs = jnp.concatenate(inputs, axis=0).astype(jnp.bfloat16)
    share = jnp.dot(inputs, projection[...], preferred_element_type=jnp.float32)
    num[:, : 2 * half_rows, :] = num_in[...]
    den[...] = den_in[...]
    for s, message in enumerate(messages):
        wide[s, :half_rows, :] = message[half_rows : 2 * half_rows, :].astype(jnp.float32)
    lengths = [length_of(part) for part in extra]

    wait_for(tables)
    lane = lax.broadcasted_iota(jnp.int32, (local_heads, HD), 1)
    token = lax.broadcasted_iota(jnp.int32, (local_heads, page_size), 1)
    lines = [
        pl.multiple_of(split(partner("mp", s) * local_heads, GROUP)[0] * page_size, page_size) for s in range(count)
    ]
    cases = [(d, s) for d in range(1, replicas) for s in range(count)]
    arrivals = [pair_row(moves, partner("replica", d), me, rows, 1) for d in range(1, replicas)]
    places = [locate(table, row, column, slots) for _, row, _ in arrivals]
    scores, weights, totals = {}, {}, {}
    for d, s in cases:
        row = arrivals[d - 1][1]
        q = wide[s, pl.ds(row, local_heads, stride=rows), :].astype(jnp.bfloat16)
        scores[d, s] = scores_of(q, pages_in[d - 1][pl.ds(lines[s], page_size), :])
    for d, s in cases:
        inside = (token + places[d - 1][0] * page_size).astype(jnp.float32) < lengths[d - 1]
        weight = jnp.where(inside, weight_of(scores[d, s]), 0.0)
        weights[d, s] = weight.astype(jnp.bfloat16)
        totals[d, s] = jnp.sum(weight, axis=1, keepdims=True)
    for d, s in cases:
        values = pages_in[d - 1][pl.ds(lines[s] + KVH * page_size, page_size), :]
        scores[d, s] = jnp.dot(weights[d, s], values, preferred_element_type=jnp.float32)
    for d, (valid, row, _) in enumerate(arrivals, 1):

        @pl.when(valid == 1)
        def _(d=d, row=row):
            for s in range(count):
                num[s, pl.ds(half_rows + row, local_heads, stride=rows), :] = scores[d, s]
                old = den[s, pl.ds(local_heads, local_heads), :]
                den[s, pl.ds(local_heads, local_heads), :] = jnp.where(lane == row, totals[d, s], old)

    arrived = []
    row_ids = lax.broadcasted_iota(jnp.int32, (rows, HD), 0)
    for number in range(movers):
        picked = jnp.zeros((1, width), jnp.float32)
        mark = jnp.zeros((rows, HD), jnp.float32)
        for d, (valid, row, order) in enumerate(arrivals):
            here = (valid == 1) & (order == number)
            picked = jnp.where(here, share[d : d + 1], picked)
            mark = jnp.where(here & (row_ids == row), 1.0, mark)
        part = jnp.concatenate([picked[:, j * HD : (j + 1) * HD] for j in range(2 * KVH)], axis=0)
        high = part.astype(jnp.bfloat16).astype(jnp.float32)
        arrived += [high, part - high]
        own_share[number] = part
        marks[number] = mark
    own_num[...] = num[0, : 2 * half_rows, :]
    own_den[...] = den[0]
    all_kv = []
    for half in range(2):
        own_kv[half] = own_tokens(messages, rows, 2 * half_rows, half)
        all_kv.append(own_kv[half])
    filler = [jnp.zeros((-2 * local_heads % 16, HD), jnp.float32)] if local_heads % 8 else []
    for s, out in enumerate(outs):
        at = s + 1
        parts = den[at]
        high = parts.astype(SEND).astype(jnp.float32)
        parts = high + pltpu.roll(parts - high, HD // 2, 1)
        out[...] = jnp.concatenate([num[at, : 2 * half_rows, :], parts] + filler + all_kv + arrived, axis=0).astype(SEND)


def finish_kernel(count, replicas, local_heads, *refs):
    refs = list(refs)
    take = lambda n: [refs.pop(0) for _ in range(n)]
    pages_in = take(replicas - 2)
    moves_all, table_all, lengths_all, kv, share, marks, q, num, den = take(9)
    pages_in, messages = take(1) + pages_in, by_distance(take(count - 1))
    pool_raw, _, first, second, pool = take(5)
    moves, table, lengths, full, arrived, windows, results, sems, write_sems, out_sems = refs
    tables = start_copies(((moves_all, moves), (table_all, table), (lengths_all, lengths)), sems)
    me, column = lax.axis_index("replica"), lax.axis_index("mp")
    rows = lengths.shape[0]
    slots, page_size, width = pool_raw.shape
    both = 2 * local_heads
    query_rows = both * rows
    movers = moves.shape[1] // replicas
    head = split(column * local_heads, GROUP)[0]

    kv_base = messages[0].shape[0] - 4 * rows - 16 * movers
    for s in range(count):
        device = partner("mp", s)
        for half in range(2):
            if s == 0:
                chunk = kv[half]
            else:
                start = kv_base + half * 2 * rows
                chunk = messages[s - 1][start : start + 2 * rows, :].astype(jnp.float32)

            def place(half=half, device=device, chunk=chunk):
                columns = head_columns(device, local_heads)
                full.at[pl.ds(0, 2 * rows), pl.ds(half * (width // 2), width // 2)][:, columns] = chunk

            if local_heads == GROUP:
                place()
            else:
                pl.when(split(device * local_heads, GROUP)[1] == 0)(place)
    for number in range(movers):
        total = share[number]
        for message in messages:
            start = kv_base + 4 * rows + 16 * number
            part = message[start : start + 16, :].astype(jnp.float32)
            total += part[: 2 * KVH] + part[2 * KVH :]
        total = total.astype(jnp.bfloat16).astype(jnp.float32)
        arrived[number] = total
        for j in range(2 * KVH):
            full[2 * rows + number : 2 * rows + number + 1, j * HD : (j + 1) * HD] = total[j : j + 1, :]
    sums = den[...]
    for message in messages:
        part = message[query_rows : query_rows + both, :].astype(jnp.float32)
        sums += part + pltpu.roll(part, HD // 2, 1)
    sums = jnp.transpose(sums)[:rows, :]

    held = []
    for half in range(2):
        value = kv[half, :rows, :]
        for number in range(movers):
            moved = arrived[number, pl.ds(head + half * KVH, 1), :]
            value = jnp.where(marks[number] > 0.5, moved, value)
        held.append(value)
    outs = []

    def finish_step(step, out):
        pieces = []
        for h in range(local_heads):
            at = (step * local_heads + h) * rows
            query = q[at : at + rows, :].astype(jnp.float32)
            numerator = num[at : at + rows, :]
            for message in messages:
                numerator += message[at : at + rows, :].astype(jnp.float32)
            denominator = sums[:, step * local_heads + h : step * local_heads + h + 1]
            extra = [(kv[0, :rows, :], kv[1, :rows, :])]
            if step == 1:
                extra = [held, (kv[0, rows:, :], kv[1, rows:, :])]
            for key, value in extra:
                weight = weight_of(jnp.sum(query * key, axis=1, keepdims=True))
                numerator += weight.astype(jnp.bfloat16).astype(jnp.float32) * value
                denominator += weight
            pieces.append(numerator / denominator)
        results[step] = jnp.concatenate(pieces, axis=1).astype(out.dtype)
        outs.append(pltpu.make_async_copy(results.at[step], out, out_sems.at[step]))
        outs[-1].start()

    finish_step(0, first)
    wait_for(tables)
    kept, plans = [jnp.bool_(True)] * rows, []

    def add_plan(active, row, length, first_token, source, r=None):
        index, slot = locate(table, row, column, slots)
        at = length - index * page_size
        touched = active & (at >= -1) & (at < page_size)
        start = jnp.clip(at, 0, page_size - WINDOW) & -16
        span = pl.ds(pl.multiple_of(start, 16), WINDOW)
        n = len(plans)
        if r is None:
            read = lambda: jnp.concatenate(
                [source[pl.ds(pl.multiple_of(line + start, 16), WINDOW), :] for line in page_lines(width, page_size)],
                axis=1,
            )
        else:
            read = lambda: source[slot, span, :]
        write = pltpu.make_async_copy(windows.at[n], pool.at[slot, span], write_sems.at[n])
        plans.append((touched, read, write, first_token, rows + row, at - start))

    for s, page in enumerate(pages_in):
        valid, row, order = pair_row(moves, partner("replica", s + 1), me, rows, 1)
        valid = valid == 1
        length = jnp.max(length_of(extra_of(page, page_size, width))).astype(jnp.int32)
        add_plan(valid, row, length, 2 * rows + order, page)
        kept = [stays & ~(valid & (row == r)) for r, stays in enumerate(kept)]
    for r in range(rows):
        add_plan(kept[r], r, lengths[r], r, pool_raw, r)

    place_ids = lax.broadcasted_iota(jnp.int32, (WINDOW, width), 0)
    for n, (touched, read, write, token, next_token, offset) in enumerate(plans):

        @pl.when(touched)
        def _(n=n, read=read, write=write, token=token, next_token=next_token, offset=offset):
            old = read().astype(jnp.float32)
            new = jnp.where(place_ids == offset, full[pl.ds(token, 1), :], old)
            new = jnp.where(place_ids == offset + 1, full[pl.ds(next_token, 1), :], new)
            windows[n] = new.astype(jnp.bfloat16)
            write.start()

    finish_step(1, second)
    for plan in plans:
        pl.when(plan[0])(plan[2].wait)
    wait_for(outs)


def cost(microseconds):
    return pl.CostEstimate(flops=0, transcendentals=0, bytes_accessed=int(microseconds * 3.5e6))


def in_vmem(value):
    return pltpu.with_memory_space_constraint(value, pltpu.VMEM)


def in_hbm(value):
    return pltpu.with_memory_space_constraint(value, pltpu.HBM)


def params(megabytes=32, **rest):
    return pltpu.CompilerParams(vmem_limit_bytes=megabytes << 20, **rest)


def body(layer_input, kv_weight, queries, kv_pool, lengths, block_table, new_table, migrations):
    replicas, count = lax.axis_size("replica"), lax.axis_size("mp")
    rows = lengths.shape[0]
    pool = kv_pool[0, 0]
    slots, page_size, width = pool.shape
    local_heads = queries.shape[2] // HD
    both = 2 * local_heads
    query_rows = both * rows
    depth = layer_input.shape[2]
    f32, bf16 = jnp.float32, jnp.bfloat16
    moves, old_table, table_after = migrations.T, block_table.T, new_table.T
    shape = jax.ShapeDtypeStruct

    message_rows = query_rows + 8 * rows
    movers = migrations.shape[0] // replicas
    inputs = layer_input.reshape(2 * rows, depth)
    pool_near, *leaving = pl.pallas_call(
        functools.partial(leave_kernel, rows),
        out_shape=[shape(pool.shape, bf16)] + [shape((page_size * width // HD + extra_lines(depth), HD), bf16)] * (replicas - 1),
        in_specs=[HBM] * 5,
        out_specs=[VMEM] * replicas,
        scratch_shapes=[
            pltpu.SMEM(moves.shape, jnp.int32),
            pltpu.SMEM(old_table.shape, jnp.int32),
            pltpu.SMEM(lengths.shape, jnp.int32),
            pltpu.VMEM((2 * rows, depth), bf16),
            pltpu.SemaphoreType.DMA((4,)),
            pltpu.SemaphoreType.DMA((slots,)),
        ],
        compiler_params=params(),
        cost_estimate=cost(1.8),
        name="leave",
    )(*map(in_hbm, (moves, old_table, lengths, inputs, pool)))
    pages_in = exchange(leaving, "replica")

    weight_near, inputs_near, queries_near = map(in_vmem, (kv_weight, inputs, queries))
    sent = pl.pallas_call(
        functools.partial(open_kernel, count, local_heads),
        out_shape=[shape((message_rows, HD), bf16)] * count,
        in_specs=[VMEM] * 2 + [HBM],
        out_specs=[VMEM] * count,
        scratch_shapes=[pltpu.VMEM((depth, width), bf16), pltpu.SemaphoreType.DMA((8,))],
        compiler_params=params(),
        cost_estimate=cost(1.2),
        name="open",
    )(inputs_near, queries_near, in_hbm(kv_weight))
    sent, pages_in[0] = lax.optimization_barrier((list(sent), pages_in[0]))
    messages = [sent[0]] + exchange(sent[1:], "mp")

    num, den = pl.pallas_call(
        functools.partial(attend_kernel, count, local_heads),
        out_shape=[shape((count, query_rows, HD), f32), shape((count, both, HD), f32)],
        in_specs=[SMEM, SMEM, VMEM] + [VMEM] * count,
        out_specs=[VMEM, VMEM],
        scratch_shapes=[pltpu.VMEM((count, query_rows, HD), f32)],
        compiler_params=params(),
        cost_estimate=cost(1.5),
        name="attend",
    )(old_table, lengths, pool_near, *by_start(messages))

    sum_rows = query_rows + -(-both // 16) * 16 + 4 * rows + 16 * movers
    *sums, num, den, kv, share, marks = pl.pallas_call(
        functools.partial(arrive_kernel, count, replicas, local_heads, slots, page_size),
        out_shape=[shape((sum_rows, HD), SEND)] * (count - 1)
        + [shape((query_rows, HD), f32), shape((both, HD), f32)]
        + [shape((2, 2 * rows, HD), f32), shape((movers, 2 * KVH, HD), f32)]
        + [shape((movers, rows, HD), f32)],
        in_specs=[VMEM] * (replicas - 2)
        + [ANY, ANY, VMEM, VMEM]
        + [VMEM] * count
        + [VMEM] * 2,
        out_specs=[VMEM] * (count + 4),
        scratch_shapes=[
            pltpu.VMEM((count, query_rows + rows, HD), f32),
            pltpu.VMEM((count, both, HD), f32),
            pltpu.VMEM((count, query_rows // 2 + rows, HD), f32),
            pltpu.SMEM(moves.shape, jnp.int32),
            pltpu.SMEM(table_after.shape, jnp.int32),
            pltpu.SemaphoreType.DMA((2,)),
        ],
        compiler_params=params(),
        cost_estimate=cost(1.2),
        name="arrive",
    )(*pages_in[1:], moves, table_after, weight_near, pages_in[0], *by_start(messages), num, den)
    sums_in = exchange(sums, "mp")

    moves_then, _ = lax.optimization_barrier((moves, marks))

    pool_copy = pl.pallas_call(
        functools.partial(keep_kernel, replicas),
        out_shape=shape(pool.shape, bf16),
        in_specs=[VMEM] * replicas + [ANY] * 2,
        out_specs=ANY,
        scratch_shapes=[
            pltpu.SMEM(moves.shape, jnp.int32),
            pltpu.SMEM(table_after.shape, jnp.int32),
            pltpu.SemaphoreType.DMA((2,)),
            pltpu.SemaphoreType.DMA((rows + replicas - 1, width // HD)),
        ],
        compiler_params=params(),
        cost_estimate=cost(1.6),
        name="keep",
    )(*pages_in, pool_near, moves_then, table_after)

    first, second, pool_after = pl.pallas_call(
        functools.partial(finish_kernel, count, replicas, local_heads),
        out_shape=[
            shape((rows, local_heads * HD), bf16),
            shape((rows, local_heads * HD), bf16),
            shape(pool.shape, bf16),
        ],
        in_specs=[VMEM] * (replicas - 2) + [ANY] * 3 + [VMEM] * (7 + count - 1) + [VMEM, ANY],
        out_specs=[ANY] * 3,
        scratch_shapes=[
            pltpu.SMEM(moves.shape, jnp.int32),
            pltpu.SMEM(table_after.shape, jnp.int32),
            pltpu.SMEM(lengths.shape, jnp.int32),
            pltpu.VMEM((KV_ROWS, width), f32),
            pltpu.VMEM((movers, 2 * KVH, HD), f32),
            pltpu.VMEM((rows + replicas - 1, WINDOW, width), bf16),
            pltpu.VMEM((2, rows, local_heads * HD), bf16),
            pltpu.SemaphoreType.DMA((3,)),
            pltpu.SemaphoreType.DMA((rows + replicas - 1,)),
            pltpu.SemaphoreType.DMA((2,)),
        ],
        input_output_aliases={9 + replicas - 1 + (count - 1) + 1: 2},
        compiler_params=params(),
        cost_estimate=cost(2.5),
        name="finish",
    )(
        *pages_in[1:],
        *(moves, table_after, lengths),
        *(kv, share, marks, messages[0], num, den, pages_in[0]),
        *by_start(sums_in),
        *(pool_near, pool_copy),
    )
    return first, second, pool_after[None, None]


def solution(mesh):
    return jax.shard_map(
        body,
        mesh=mesh,
        in_specs=(
            P(None, ("groups", "replica"), "mp"),
            P("mp", None),
            P(None, ("groups", "replica"), "mp"),
            P(("groups", "replica"), "mp", None, None, None),
            P(("groups", "replica")),
            P(("groups", "replica"), None),
            P(("groups", "replica"), None),
            P("groups", None),
        ),
        out_specs=(
            P(("groups", "replica"), "mp"),
            P(("groups", "replica"), "mp"),
            P(("groups", "replica"), "mp", None, None, None),
        ),
        check_vma=False,
    )
```

```python
import functools
import math

import jax
import jax.numpy as jnp
from jax import lax
from jax.experimental import pallas as pl
from jax.experimental.pallas import tpu as pltpu
from jax.sharding import PartitionSpec as P

H = 32
KVH = 4
HD = 128
GROUP = H // KVH
CAP = 20.0
SCALE = 1.0 / math.sqrt(HD)
WINDOW = 32
KV_ROWS = 24

SMEM = pl.BlockSpec(memory_space=pltpu.SMEM)
VMEM = pl.BlockSpec(memory_space=pltpu.VMEM)
ANY = pl.BlockSpec(memory_space=pl.ANY)
HBM = pl.BlockSpec(memory_space=pltpu.HBM)
SEND = jnp.bfloat16


def swap(value, axis, distance):
    size = lax.axis_size(axis)
    return lax.ppermute(value, axis, [(i, i ^ distance) for i in range(size)])


def exchange(messages, axis):
    received = [swap(messages[d], axis, d + 1) for d in reversed(range(len(messages)))]
    return received[::-1]


def turns(size):
    if size == 4:
        return [[1, 3, 0, 2], [3, 2, 1, 0], [2, 0, 3, 1]]
    return [[(i + s) % size for i in range(size)] for s in range(1, size)]


def rotate(messages, axis):
    steps = turns(lax.axis_size(axis))
    return [lax.ppermute(message, axis, list(enumerate(step))) for message, step in zip(messages, steps)]


def pick(values, index):
    found = jnp.int32(values[0])
    for i, value in enumerate(values[1:], 1):
        found = jnp.where(index == i, value, found)
    return found


def turn_target(axis, k):
    return pick(turns(lax.axis_size(axis))[k - 1], lax.axis_index(axis))


def turn_source(axis, k):
    if k == 0:
        return lax.axis_index(axis)
    step = turns(lax.axis_size(axis))[k - 1]
    return pick([step.index(i) for i in range(len(step))], lax.axis_index(axis))


def start_order(count):
    return [count // 2] + [d for d in range(count - 1, 0, -1) if d != count // 2]


def by_start(values):
    own = len(values) & 1 ^ 1
    order = start_order(len(values)) if own else range(1, len(values) + 1)
    return [values[d - 1 + own] for d in order] + list(values[:own])


def by_distance(values):
    own = len(values) & 1 ^ 1
    order = start_order(len(values)) if own else range(1, len(values) + 1)
    return list(values[len(order) :]) + [values[list(order).index(d)] for d in range(1, len(order) + 1)]


def partner(axis, distance):
    return lax.axis_index(axis) ^ distance


def split(value, size):
    if size & (size - 1) == 0:
        return lax.shift_right_logical(value, size.bit_length() - 1), value & (size - 1)
    return lax.div(value, size), lax.rem(value, size)


def count_up(limit, step, state):
    if limit > 8:
        return lax.fori_loop(0, limit, step, state)
    for i in range(limit):
        state = step(i, state)
    return state


def locate(table, row, column, slots):
    def step(p, found):
        device, slot = split(table[p, row], slots)
        here = device == column
        return jnp.where(here, p, found[0]), jnp.where(here, slot, found[1])

    return count_up(table.shape[0], step, (jnp.int32(0), jnp.int32(0)))


def pair_row(moves, source, target, rows, side):
    def step(j, found):
        valid, row, order, number = found
        ends = [split(moves[i, j], rows) for i in range(2)]
        match = (ends[0][0] == source) & (ends[1][0] == target)
        return (
            jnp.where(match, jnp.int32(1), valid),
            jnp.where(match, ends[side][1], row),
            jnp.where(match, number, order),
            number + jnp.where(ends[side][0] == (source, target)[side], 1, 0),
        )

    return count_up(moves.shape[1], step, (jnp.int32(0),) * 4)[:3]


def head_columns(device, local_heads):
    return pl.ds(pl.multiple_of(split(device * local_heads, GROUP)[0] * HD, HD), HD)


def weight_of(score):
    return jnp.exp(CAP * jnp.tanh(score * (SCALE / CAP)))


def pieces_of(width):
    return [slice(at, at + HD) for at in range(0, width, HD)]


def page_lines(width, page_size):
    return [j * page_size for j in range(width // HD)]


def extra_lines(depth):
    return -(-(2 + depth // HD) // 8) * 8


def start_copies(pairs, sems):
    copies = [pltpu.make_async_copy(*pair, sems.at[i]) for i, pair in enumerate(pairs)]
    for copy in copies:
        copy.start()
    return copies


def wait_for(copies):
    for copy in copies:
        copy.wait()


def leave_kernel(rows, moves_all, table_all, lengths_all, x_all, pool, *refs):
    held, pages, (moves, table, lengths, x, sems, pool_sems) = refs[0], refs[1:-6], refs[-6:]
    me, column = lax.axis_index("replica"), lax.axis_index("mp")
    page_size, width = pool.shape[1:]
    depth = x.shape[1]
    rest = start_copies(
        ((moves_all, moves), (table_all, table), (lengths_all, lengths), (x_all, x)), sems
    )
    copies = start_copies([(pool.at[i], held.at[i]) for i in range(pool.shape[0])], pool_sems)
    wait_for(rest[:2])
    found = [pair_row(moves, me, partner("replica", s + 1), rows, 0)[1] for s in range(len(pages))]
    picks = [locate(table, row, column, pool.shape[0])[1] for row in found]
    wait_for(rest[2:])
    lines = extra_lines(depth)
    sublane = lax.broadcasted_iota(jnp.int32, (lines, HD), 0)
    first_rows = x[:rows, :].astype(jnp.float32)
    row_ids = lax.broadcasted_iota(jnp.int32, (rows, depth), 0)
    for row, page in zip(found, pages):
        high, low = split(lengths[row], 64)
        picked = jnp.sum(jnp.where(row_ids == row, first_rows, 0.0), axis=0, keepdims=True)
        parts = [jnp.zeros((2, HD), jnp.float32)] + [picked[:, piece] for piece in pieces_of(depth)]
        spare = lines - 2 - depth // HD
        parts += [jnp.zeros((spare, HD), jnp.float32)] if spare else []
        extra = jnp.concatenate(parts, axis=0)
        extra = jnp.where(sublane == 0, high.astype(jnp.float32), extra)
        extra = jnp.where(sublane == 1, low.astype(jnp.float32), extra)
        page[page_size * width // HD :, :] = extra.astype(jnp.bfloat16)
    wait_for(copies)
    for slot, page in zip(picks, pages):
        for line, piece in zip(page_lines(width, page_size), pieces_of(width)):
            page[line : line + page_size, :] = held[slot, :, piece]


def open_kernel(count, local_heads, x, q, weight, *refs):
    outs, (held, weight_sems) = refs[:-2], refs[-2:]
    depth, chunks = weight.shape[0], weight_sems.shape[0]
    spans = [pl.ds(c * (depth // chunks), depth // chunks) for c in range(chunks)]
    loads = start_copies([(weight.at[span], held.at[span]) for span in spans], weight_sems)
    rows = q.shape[1]
    wide = [q[i].astype(jnp.float32) for i in range(2)]
    blocks = [wide[i][:, h * HD : (h + 1) * HD] for i in range(2) for h in range(local_heads)]
    packed = jnp.concatenate(blocks, axis=0).astype(jnp.bfloat16)
    query_rows = packed.shape[0]
    for out in outs:
        out[:query_rows, :] = packed
    total = jnp.zeros((x.shape[0], weight.shape[1]), jnp.float32)
    for span, load in zip(spans, loads):
        load.wait()
        total += jnp.dot(x[:, span], held[span, :], preferred_element_type=jnp.float32)
    for j in range(KVH):
        parts = []
        for half in range(2):
            start = (half * KVH + j) * HD
            part = total[:, start : start + HD]
            high = part.astype(jnp.bfloat16)
            parts += [high, (part - high.astype(jnp.float32)).astype(jnp.bfloat16)]
        parts = jnp.concatenate(parts, axis=0)
        for s, out in enumerate(outs):

            @pl.when(split(partner("mp", s) * local_heads, GROUP)[0] == j)
            def _(out=out, parts=parts):
                out[query_rows:, :] = parts


def keep_kernel(replicas, *refs):
    pages_in, (pool, moves_all, table_all, pool_out, moves, table, sems, page_sems) = (
        refs[: replicas - 1],
        refs[replicas - 1 :],
    )
    wait_for(start_copies(((moves_all, moves), (table_all, table)), sems))
    me, column = lax.axis_index("replica"), lax.axis_index("mp")
    rows = table.shape[1]
    slots, page_size, width = pool.shape
    kept, copies = [jnp.bool_(True)] * rows, []
    for s, page in enumerate(pages_in):
        valid, row, _ = pair_row(moves, partner("replica", s + 1), me, rows, 1)
        kept = [stays & ~((valid == 1) & (row == r)) for r, stays in enumerate(kept)]
        copies.append((valid == 1, row, page))
    copies += [(stays, r, None) for r, stays in enumerate(kept)]
    started = []
    for n, (active, row, page) in enumerate(copies):
        _, slot = locate(table, row, column, slots)
        pairs = [(pool.at[slot], pool_out.at[slot])]
        if page is not None:
            pairs = [
                (page.at[pl.ds(line, page_size)], pool_out.at[slot, :, piece])
                for line, piece in zip(page_lines(width, page_size), pieces_of(width))
            ]
        parts = [pltpu.make_async_copy(*pair, page_sems.at[n, i]) for i, pair in enumerate(pairs)]
        started.append((active, parts))

        @pl.when(active)
        def _(parts=parts):
            for copy in parts:
                copy.start()

    for active, parts in started:
        pl.when(active)(functools.partial(wait_for, parts))


def extra_of(page, page_size, width):
    return page[page_size * width // HD :, :].astype(jnp.float32)


def length_of(extra):
    return extra[0:1] * 64.0 + extra[1:2]


def own_tokens(messages, rows, query_rows, half):
    tokens = 2 * rows
    start = query_rows + 2 * half * tokens
    total = jnp.zeros((tokens, HD), jnp.float32)
    for message in messages:
        total += message[start : start + tokens, :].astype(jnp.float32)
        total += message[start + tokens : start + 2 * tokens, :].astype(jnp.float32)
    return total.astype(jnp.bfloat16).astype(jnp.float32)


def scores_of(q, keys):
    return lax.dot_general(q, keys, (((1,), (1,)), ((), ())), preferred_element_type=jnp.float32)


def attend_kernel(count, local_heads, table, lengths, pool, *refs):
    messages = by_distance(refs[:count])
    num, den, wide = refs[count:]
    column = lax.axis_index("mp")
    rows = lengths.shape[0]
    slots, page_size, width = pool.shape
    both = 2 * local_heads
    for s, message in enumerate(messages):
        wide[s] = message[: both * rows, :].astype(jnp.float32)
    lane = lax.broadcasted_iota(jnp.int32, (both, HD), 1)
    token = lax.broadcasted_iota(jnp.int32, (both, page_size), 1)
    places = [locate(table, r, column, slots) for r in range(rows)]
    columns = [head_columns(partner("mp", s), local_heads) for s in range(count)]
    keys = pool.at[:, :, pl.ds(0, width // 2)]
    values = pool.at[:, :, pl.ds(width // 2, width // 2)]
    cases = [(r, s) for r in range(rows) for s in range(count)]
    scores = {}
    for r, s in cases:
        q = wide[s, pl.ds(r, both, stride=rows), :].astype(jnp.bfloat16)
        scores[r, s] = scores_of(q, keys[places[r][1], :, columns[s]])
    weights = {}
    denominators = [jnp.zeros((both, HD), jnp.float32) for _ in range(count)]
    for r, s in cases:
        inside = token < lengths[r] - places[r][0] * page_size
        weight = jnp.where(inside, weight_of(scores[r, s]), 0.0)
        weights[r, s] = weight.astype(jnp.bfloat16)
        total = jnp.sum(weight, axis=1, keepdims=True)
        denominators[s] += jnp.where(lane == r, total, 0.0)
    for r, s in cases:
        num[s, pl.ds(r, both, stride=rows), :] = jnp.dot(
            weights[r, s], values[places[r][1], :, columns[s]], preferred_element_type=jnp.float32
        )
    for s in range(count):
        den[s] = denominators[s]


def arrive_kernel(count, replicas, local_heads, slots, page_size, *refs):
    refs = list(refs)
    take = lambda n: [refs.pop(0) for _ in range(n)]
    pages_in = take(replicas - 2)
    moves_all, table_all, projection = take(3)
    pages_in, messages = take(1) + pages_in, by_distance(take(count))
    num_in, den_in = take(2)
    outs = take(count - 1)
    own_num, own_den, own_kv, own_share, marks, num, den, wide, moves, table, sems = refs
    tables = start_copies(((moves_all, moves), (table_all, table)), sems)
    me, column = lax.axis_index("replica"), lax.axis_index("mp")
    rows = table.shape[1]
    depth, width = projection.shape
    half_rows = local_heads * rows
    movers = moves.shape[1] // replicas

    extra = [extra_of(page, page_size, width) for page in pages_in]
    inputs = [
        jnp.concatenate([part[2 + i : 3 + i] for i in range(depth // HD)], axis=1) for part in extra
    ]
    inputs += [jnp.zeros((8 - len(inputs), depth), jnp.float32)]
    inputs = jnp.concatenate(inputs, axis=0).astype(jnp.bfloat16)
    share = jnp.dot(inputs, projection[...], preferred_element_type=jnp.float32)
    num[:, : 2 * half_rows, :] = num_in[...]
    den[...] = den_in[...]
    for s, message in enumerate(messages):
        wide[s, :half_rows, :] = message[half_rows : 2 * half_rows, :].astype(jnp.float32)
    lengths = [length_of(part) for part in extra]

    wait_for(tables)
    lane = lax.broadcasted_iota(jnp.int32, (local_heads, HD), 1)
    token = lax.broadcasted_iota(jnp.int32, (local_heads, page_size), 1)
    lines = [
        pl.multiple_of(split(partner("mp", s) * local_heads, GROUP)[0] * page_size, page_size) for s in range(count)
    ]
    cases = [(d, s) for d in range(1, replicas) for s in range(count)]
    arrivals = [pair_row(moves, partner("replica", d), me, rows, 1) for d in range(1, replicas)]
    places = [locate(table, row, column, slots) for _, row, _ in arrivals]
    scores, weights, totals = {}, {}, {}
    for d, s in cases:
        row = arrivals[d - 1][1]
        q = wide[s, pl.ds(row, local_heads, stride=rows), :].astype(jnp.bfloat16)
        scores[d, s] = scores_of(q, pages_in[d - 1][pl.ds(lines[s], page_size), :])
    for d, s in cases:
        inside = (token + places[d - 1][0] * page_size).astype(jnp.float32) < lengths[d - 1]
        weight = jnp.where(inside, weight_of(scores[d, s]), 0.0)
        weights[d, s] = weight.astype(jnp.bfloat16)
        totals[d, s] = jnp.sum(weight, axis=1, keepdims=True)
    for d, s in cases:
        values = pages_in[d - 1][pl.ds(lines[s] + KVH * page_size, page_size), :]
        scores[d, s] = jnp.dot(weights[d, s], values, preferred_element_type=jnp.float32)
    for d, (valid, row, _) in enumerate(arrivals, 1):

        @pl.when(valid == 1)
        def _(d=d, row=row):
            for s in range(count):
                num[s, pl.ds(half_rows + row, local_heads, stride=rows), :] = scores[d, s]
                old = den[s, pl.ds(local_heads, local_heads), :]
                den[s, pl.ds(local_heads, local_heads), :] = jnp.where(lane == row, totals[d, s], old)

    arrived = []
    row_ids = lax.broadcasted_iota(jnp.int32, (rows, HD), 0)
    for number in range(movers):
        picked = jnp.zeros((1, width), jnp.float32)
        mark = jnp.zeros((rows, HD), jnp.float32)
        for d, (valid, row, order) in enumerate(arrivals):
            here = (valid == 1) & (order == number)
            picked = jnp.where(here, share[d : d + 1], picked)
            mark = jnp.where(here & (row_ids == row), 1.0, mark)
        part = jnp.concatenate([picked[:, j * HD : (j + 1) * HD] for j in range(2 * KVH)], axis=0)
        high = part.astype(jnp.bfloat16).astype(jnp.float32)
        arrived += [high, part - high]
        own_share[number] = part
        marks[number] = mark
    own_num[...] = num[0, : 2 * half_rows, :]
    own_den[...] = den[0]
    all_kv = []
    for half in range(2):
        own_kv[half] = own_tokens(messages, rows, 2 * half_rows, half)
        all_kv.append(own_kv[half])
    filler = [jnp.zeros((-2 * local_heads % 16, HD), jnp.float32)] if local_heads % 8 else []
    for s, out in enumerate(outs):
        at = lax.axis_index("mp") ^ turn_target("mp", s + 1)
        parts = den[at]
        high = parts.astype(SEND).astype(jnp.float32)
        parts = high + pltpu.roll(parts - high, HD // 2, 1)
        out[...] = jnp.concatenate([num[at, : 2 * half_rows, :], parts] + filler + all_kv + arrived, axis=0).astype(SEND)


def finish_kernel(count, replicas, local_heads, *refs):
    refs = list(refs)
    take = lambda n: [refs.pop(0) for _ in range(n)]
    pages_in = take(replicas - 2)
    moves_all, table_all, lengths_all, kv, share, marks, q, num, den = take(9)
    pages_in, messages = take(1) + pages_in, by_distance(take(count - 1))
    pool_raw, _, first, second, pool = take(5)
    moves, table, lengths, full, arrived, windows, results, sems, write_sems, out_sems = refs
    tables = start_copies(((moves_all, moves), (table_all, table), (lengths_all, lengths)), sems)
    me, column = lax.axis_index("replica"), lax.axis_index("mp")
    rows = lengths.shape[0]
    slots, page_size, width = pool_raw.shape
    both = 2 * local_heads
    query_rows = both * rows
    movers = moves.shape[1] // replicas
    head = split(column * local_heads, GROUP)[0]

    kv_base = messages[0].shape[0] - 4 * rows - 16 * movers
    for s in range(count):
        device = turn_source("mp", s)
        for half in range(2):
            if s == 0:
                chunk = kv[half]
            else:
                start = kv_base + half * 2 * rows
                chunk = messages[s - 1][start : start + 2 * rows, :].astype(jnp.float32)

            def place(half=half, device=device, chunk=chunk):
                columns = head_columns(device, local_heads)
                full.at[pl.ds(0, 2 * rows), pl.ds(half * (width // 2), width // 2)][:, columns] = chunk

            if local_heads == GROUP:
                place()
            else:
                pl.when(split(device * local_heads, GROUP)[1] == 0)(place)
    for number in range(movers):
        total = share[number]
        for message in messages:
            start = kv_base + 4 * rows + 16 * number
            part = message[start : start + 16, :].astype(jnp.float32)
            total += part[: 2 * KVH] + part[2 * KVH :]
        total = total.astype(jnp.bfloat16).astype(jnp.float32)
        arrived[number] = total
        for j in range(2 * KVH):
            full[2 * rows + number : 2 * rows + number + 1, j * HD : (j + 1) * HD] = total[j : j + 1, :]
    sums = den[...]
    for message in messages:
        part = message[query_rows : query_rows + both, :].astype(jnp.float32)
        sums += part + pltpu.roll(part, HD // 2, 1)
    sums = jnp.transpose(sums)[:rows, :]

    held = []
    for half in range(2):
        value = kv[half, :rows, :]
        for number in range(movers):
            moved = arrived[number, pl.ds(head + half * KVH, 1), :]
            value = jnp.where(marks[number] > 0.5, moved, value)
        held.append(value)
    outs = []

    def finish_step(step, out):
        pieces = []
        for h in range(local_heads):
            at = (step * local_heads + h) * rows
            query = q[at : at + rows, :].astype(jnp.float32)
            numerator = num[at : at + rows, :]
            for message in messages:
                numerator += message[at : at + rows, :].astype(jnp.float32)
            denominator = sums[:, step * local_heads + h : step * local_heads + h + 1]
            extra = [(kv[0, :rows, :], kv[1, :rows, :])]
            if step == 1:
                extra = [held, (kv[0, rows:, :], kv[1, rows:, :])]
            for key, value in extra:
                weight = weight_of(jnp.sum(query * key, axis=1, keepdims=True))
                numerator += weight.astype(jnp.bfloat16).astype(jnp.float32) * value
                denominator += weight
            pieces.append(numerator / denominator)
        results[step] = jnp.concatenate(pieces, axis=1).astype(out.dtype)
        outs.append(pltpu.make_async_copy(results.at[step], out, out_sems.at[step]))
        outs[-1].start()

    finish_step(0, first)
    wait_for(tables)
    kept, plans = [jnp.bool_(True)] * rows, []

    def add_plan(active, row, length, first_token, source, r=None):
        index, slot = locate(table, row, column, slots)
        at = length - index * page_size
        touched = active & (at >= -1) & (at < page_size)
        start = jnp.clip(at, 0, page_size - WINDOW) & -16
        span = pl.ds(pl.multiple_of(start, 16), WINDOW)
        n = len(plans)
        if r is None:
            read = lambda: jnp.concatenate(
                [source[pl.ds(pl.multiple_of(line + start, 16), WINDOW), :] for line in page_lines(width, page_size)],
                axis=1,
            )
        else:
            read = lambda: source[slot, span, :]
        write = pltpu.make_async_copy(windows.at[n], pool.at[slot, span], write_sems.at[n])
        plans.append((touched, read, write, first_token, rows + row, at - start))

    for s, page in enumerate(pages_in):
        valid, row, order = pair_row(moves, partner("replica", s + 1), me, rows, 1)
        valid = valid == 1
        length = jnp.max(length_of(extra_of(page, page_size, width))).astype(jnp.int32)
        add_plan(valid, row, length, 2 * rows + order, page)
        kept = [stays & ~(valid & (row == r)) for r, stays in enumerate(kept)]
    for r in range(rows):
        add_plan(kept[r], r, lengths[r], r, pool_raw, r)

    place_ids = lax.broadcasted_iota(jnp.int32, (WINDOW, width), 0)
    for n, (touched, read, write, token, next_token, offset) in enumerate(plans):

        @pl.when(touched)
        def _(n=n, read=read, write=write, token=token, next_token=next_token, offset=offset):
            old = read().astype(jnp.float32)
            new = jnp.where(place_ids == offset, full[pl.ds(token, 1), :], old)
            new = jnp.where(place_ids == offset + 1, full[pl.ds(next_token, 1), :], new)
            windows[n] = new.astype(jnp.bfloat16)
            write.start()

    finish_step(1, second)
    for plan in plans:
        pl.when(plan[0])(plan[2].wait)
    wait_for(outs)


def cost(microseconds):
    return pl.CostEstimate(flops=0, transcendentals=0, bytes_accessed=int(microseconds * 3.5e6))


def in_vmem(value):
    return pltpu.with_memory_space_constraint(value, pltpu.VMEM)


def in_hbm(value):
    return pltpu.with_memory_space_constraint(value, pltpu.HBM)


def params(megabytes=32, **rest):
    return pltpu.CompilerParams(vmem_limit_bytes=megabytes << 20, **rest)


def body(layer_input, kv_weight, queries, kv_pool, lengths, block_table, new_table, migrations):
    replicas, count = lax.axis_size("replica"), lax.axis_size("mp")
    rows = lengths.shape[0]
    pool = kv_pool[0, 0]
    slots, page_size, width = pool.shape
    local_heads = queries.shape[2] // HD
    both = 2 * local_heads
    query_rows = both * rows
    depth = layer_input.shape[2]
    f32, bf16 = jnp.float32, jnp.bfloat16
    moves, old_table, table_after = migrations.T, block_table.T, new_table.T
    shape = jax.ShapeDtypeStruct

    message_rows = query_rows + 8 * rows
    movers = migrations.shape[0] // replicas
    inputs = layer_input.reshape(2 * rows, depth)
    pool_near, *leaving = pl.pallas_call(
        functools.partial(leave_kernel, rows),
        out_shape=[shape(pool.shape, bf16)] + [shape((page_size * width // HD + extra_lines(depth), HD), bf16)] * (replicas - 1),
        in_specs=[HBM] * 5,
        out_specs=[VMEM] * replicas,
        scratch_shapes=[
            pltpu.SMEM(moves.shape, jnp.int32),
            pltpu.SMEM(old_table.shape, jnp.int32),
            pltpu.SMEM(lengths.shape, jnp.int32),
            pltpu.VMEM((2 * rows, depth), bf16),
            pltpu.SemaphoreType.DMA((4,)),
            pltpu.SemaphoreType.DMA((slots,)),
        ],
        compiler_params=params(),
        cost_estimate=cost(1.8),
        name="leave",
    )(*map(in_hbm, (moves, old_table, lengths, inputs, pool)))
    pages_in = exchange(leaving, "replica")

    weight_near, inputs_near, queries_near = map(in_vmem, (kv_weight, inputs, queries))
    sent = pl.pallas_call(
        functools.partial(open_kernel, count, local_heads),
        out_shape=[shape((message_rows, HD), bf16)] * count,
        in_specs=[VMEM] * 2 + [HBM],
        out_specs=[VMEM] * count,
        scratch_shapes=[pltpu.VMEM((depth, width), bf16), pltpu.SemaphoreType.DMA((8,))],
        compiler_params=params(),
        cost_estimate=cost(1.2),
        name="open",
    )(inputs_near, queries_near, in_hbm(kv_weight))
    sent, pages_in[0] = lax.optimization_barrier((list(sent), pages_in[0]))
    messages = [sent[0]] + exchange(sent[1:], "mp")

    num, den = pl.pallas_call(
        functools.partial(attend_kernel, count, local_heads),
        out_shape=[shape((count, query_rows, HD), f32), shape((count, both, HD), f32)],
        in_specs=[SMEM, SMEM, VMEM] + [VMEM] * count,
        out_specs=[VMEM, VMEM],
        scratch_shapes=[pltpu.VMEM((count, query_rows, HD), f32)],
        compiler_params=params(),
        cost_estimate=cost(1.5),
        name="attend",
    )(old_table, lengths, pool_near, *by_start(messages))

    sum_rows = query_rows + -(-both // 16) * 16 + 4 * rows + 16 * movers
    *sums, num, den, kv, share, marks = pl.pallas_call(
        functools.partial(arrive_kernel, count, replicas, local_heads, slots, page_size),
        out_shape=[shape((sum_rows, HD), SEND)] * (count - 1)
        + [shape((query_rows, HD), f32), shape((both, HD), f32)]
        + [shape((2, 2 * rows, HD), f32), shape((movers, 2 * KVH, HD), f32)]
        + [shape((movers, rows, HD), f32)],
        in_specs=[VMEM] * (replicas - 2)
        + [ANY, ANY, VMEM, VMEM]
        + [VMEM] * count
        + [VMEM] * 2,
        out_specs=[VMEM] * (count + 4),
        scratch_shapes=[
            pltpu.VMEM((count, query_rows + rows, HD), f32),
            pltpu.VMEM((count, both, HD), f32),
            pltpu.VMEM((count, query_rows // 2 + rows, HD), f32),
            pltpu.SMEM(moves.shape, jnp.int32),
            pltpu.SMEM(table_after.shape, jnp.int32),
            pltpu.SemaphoreType.DMA((2,)),
        ],
        compiler_params=params(),
        cost_estimate=cost(1.2),
        name="arrive",
    )(*pages_in[1:], moves, table_after, weight_near, pages_in[0], *by_start(messages), num, den)
    sums_in = rotate(sums, "mp")

    moves_then, _ = lax.optimization_barrier((moves, marks))

    pool_copy = pl.pallas_call(
        functools.partial(keep_kernel, replicas),
        out_shape=shape(pool.shape, bf16),
        in_specs=[VMEM] * replicas + [ANY] * 2,
        out_specs=ANY,
        scratch_shapes=[
            pltpu.SMEM(moves.shape, jnp.int32),
            pltpu.SMEM(table_after.shape, jnp.int32),
            pltpu.SemaphoreType.DMA((2,)),
            pltpu.SemaphoreType.DMA((rows + replicas - 1, width // HD)),
        ],
        compiler_params=params(),
        cost_estimate=cost(1.6),
        name="keep",
    )(*pages_in, pool_near, moves_then, table_after)

    first, second, pool_after = pl.pallas_call(
        functools.partial(finish_kernel, count, replicas, local_heads),
        out_shape=[
            shape((rows, local_heads * HD), bf16),
            shape((rows, local_heads * HD), bf16),
            shape(pool.shape, bf16),
        ],
        in_specs=[VMEM] * (replicas - 2) + [ANY] * 3 + [VMEM] * (7 + count - 1) + [VMEM, ANY],
        out_specs=[ANY] * 3,
        scratch_shapes=[
            pltpu.SMEM(moves.shape, jnp.int32),
            pltpu.SMEM(table_after.shape, jnp.int32),
            pltpu.SMEM(lengths.shape, jnp.int32),
            pltpu.VMEM((KV_ROWS, width), f32),
            pltpu.VMEM((movers, 2 * KVH, HD), f32),
            pltpu.VMEM((rows + replicas - 1, WINDOW, width), bf16),
            pltpu.VMEM((2, rows, local_heads * HD), bf16),
            pltpu.SemaphoreType.DMA((3,)),
            pltpu.SemaphoreType.DMA((rows + replicas - 1,)),
            pltpu.SemaphoreType.DMA((2,)),
        ],
        input_output_aliases={9 + replicas - 1 + (count - 1) + 1: 2},
        compiler_params=params(),
        cost_estimate=cost(2.5),
        name="finish",
    )(
        *pages_in[1:],
        *(moves, table_after, lengths),
        *(kv, share, marks, messages[0], num, den, pages_in[0]),
        *by_start(sums_in),
        *(pool_near, pool_copy),
    )
    return first, second, pool_after[None, None]


def solution(mesh):
    return jax.shard_map(
        body,
        mesh=mesh,
        in_specs=(
            P(None, ("groups", "replica"), "mp"),
            P("mp", None),
            P(None, ("groups", "replica"), "mp"),
            P(("groups", "replica"), "mp", None, None, None),
            P(("groups", "replica")),
            P(("groups", "replica"), None),
            P(("groups", "replica"), None),
            P("groups", None),
        ),
        out_specs=(
            P(("groups", "replica"), "mp"),
            P(("groups", "replica"), "mp"),
            P(("groups", "replica"), "mp", None, None, None),
        ),
        check_vma=False,
    )
```

```python
import functools
import math

import jax
import jax.numpy as jnp
from jax import lax
from jax.experimental import pallas as pl
from jax.experimental.pallas import tpu as pltpu
from jax.sharding import PartitionSpec as P

H = 32
KVH = 4
HD = 128
GROUP = H // KVH
CAP = 20.0
SCALE = 1.0 / math.sqrt(HD)
WINDOW = 32
KV_ROWS = 24

SMEM = pl.BlockSpec(memory_space=pltpu.SMEM)
VMEM = pl.BlockSpec(memory_space=pltpu.VMEM)
ANY = pl.BlockSpec(memory_space=pl.ANY)
HBM = pl.BlockSpec(memory_space=pltpu.HBM)
SEND = jnp.bfloat16


def swap(value, axis, distance):
    size = lax.axis_size(axis)
    return lax.ppermute(value, axis, [(i, i ^ distance) for i in range(size)])


def exchange(messages, axis):
    received = [swap(messages[d], axis, d + 1) for d in reversed(range(len(messages)))]
    return received[::-1]


def turns(size):
    if size == 4:
        return [[1, 3, 0, 2], [3, 2, 1, 0], [2, 0, 3, 1]]
    return [[(i + s) % size for i in range(size)] for s in range(1, size)]


def rotate(messages, axis):
    steps = turns(lax.axis_size(axis))
    return [lax.ppermute(message, axis, list(enumerate(step))) for message, step in zip(messages, steps)]


def pick(values, index):
    found = jnp.int32(values[0])
    for i, value in enumerate(values[1:], 1):
        found = jnp.where(index == i, value, found)
    return found


def turn_target(axis, k):
    return pick(turns(lax.axis_size(axis))[k - 1], lax.axis_index(axis))


def turn_source(axis, k):
    if k == 0:
        return lax.axis_index(axis)
    step = turns(lax.axis_size(axis))[k - 1]
    return pick([step.index(i) for i in range(len(step))], lax.axis_index(axis))


def start_order(count):
    return [count // 2] + [d for d in range(count - 1, 0, -1) if d != count // 2]


def by_start(values):
    own = len(values) & 1 ^ 1
    order = start_order(len(values)) if own else range(1, len(values) + 1)
    return [values[d - 1 + own] for d in order] + list(values[:own])


def by_distance(values):
    own = len(values) & 1 ^ 1
    order = start_order(len(values)) if own else range(1, len(values) + 1)
    return list(values[len(order) :]) + [values[list(order).index(d)] for d in range(1, len(order) + 1)]


def partner(axis, distance):
    return lax.axis_index(axis) ^ distance


def split(value, size):
    if size & (size - 1) == 0:
        return lax.shift_right_logical(value, size.bit_length() - 1), value & (size - 1)
    return lax.div(value, size), lax.rem(value, size)


def count_up(limit, step, state):
    if limit > 8:
        return lax.fori_loop(0, limit, step, state)
    for i in range(limit):
        state = step(i, state)
    return state


def locate(table, row, column, slots):
    def step(p, found):
        device, slot = split(table[p, row], slots)
        here = device == column
        return jnp.where(here, p, found[0]), jnp.where(here, slot, found[1])

    return count_up(table.shape[0], step, (jnp.int32(0), jnp.int32(0)))


def pair_row(moves, source, target, rows, side):
    def step(j, found):
        valid, row, order, number = found
        ends = [split(moves[i, j], rows) for i in range(2)]
        match = (ends[0][0] == source) & (ends[1][0] == target)
        return (
            jnp.where(match, jnp.int32(1), valid),
            jnp.where(match, ends[side][1], row),
            jnp.where(match, number, order),
            number + jnp.where(ends[side][0] == (source, target)[side], 1, 0),
        )

    return count_up(moves.shape[1], step, (jnp.int32(0),) * 4)[:3]


def head_columns(device, local_heads):
    return pl.ds(pl.multiple_of(split(device * local_heads, GROUP)[0] * HD, HD), HD)


def weight_of(score):
    return jnp.exp(CAP * jnp.tanh(score * (SCALE / CAP)))


def pieces_of(width):
    return [slice(at, at + HD) for at in range(0, width, HD)]


def page_lines(width, page_size):
    return [j * page_size for j in range(width // HD)]


def extra_lines(depth):
    return -(-(2 + depth // HD) // 8) * 8


def start_copies(pairs, sems):
    copies = [pltpu.make_async_copy(*pair, sems.at[i]) for i, pair in enumerate(pairs)]
    for copy in copies:
        copy.start()
    return copies


def wait_for(copies):
    for copy in copies:
        copy.wait()


def leave_kernel(rows, moves_all, table_all, lengths_all, x_all, pool, *refs):
    held, pages, (moves, table, lengths, x, sems, pool_sems) = refs[0], refs[1:-6], refs[-6:]
    me, column = lax.axis_index("replica"), lax.axis_index("mp")
    page_size, width = pool.shape[1:]
    depth = x.shape[1]
    rest = start_copies(
        ((moves_all, moves), (table_all, table), (lengths_all, lengths), (x_all, x)), sems
    )
    copies = start_copies([(pool.at[i], held.at[i]) for i in range(pool.shape[0])], pool_sems)
    wait_for(rest[:2])
    found = [pair_row(moves, me, partner("replica", s + 1), rows, 0)[1] for s in range(len(pages))]
    picks = [locate(table, row, column, pool.shape[0])[1] for row in found]
    wait_for(rest[2:])
    lines = extra_lines(depth)
    sublane = lax.broadcasted_iota(jnp.int32, (lines, HD), 0)
    first_rows = x[:rows, :].astype(jnp.float32)
    row_ids = lax.broadcasted_iota(jnp.int32, (rows, depth), 0)
    for row, page in zip(found, pages):
        high, low = split(lengths[row], 64)
        picked = jnp.sum(jnp.where(row_ids == row, first_rows, 0.0), axis=0, keepdims=True)
        parts = [jnp.zeros((2, HD), jnp.float32)] + [picked[:, piece] for piece in pieces_of(depth)]
        spare = lines - 2 - depth // HD
        parts += [jnp.zeros((spare, HD), jnp.float32)] if spare else []
        extra = jnp.concatenate(parts, axis=0)
        extra = jnp.where(sublane == 0, high.astype(jnp.float32), extra)
        extra = jnp.where(sublane == 1, low.astype(jnp.float32), extra)
        page[page_size * width // HD :, :] = extra.astype(jnp.bfloat16)
    wait_for(copies)
    for slot, page in zip(picks, pages):
        for line, piece in zip(page_lines(width, page_size), pieces_of(width)):
            page[line : line + page_size, :] = held[slot, :, piece]


INDEX, SLOT, KEPT, VALID, ROW, ORDER, NEW_INDEX, NEW_SLOT = range(8)


def make_plan(plan, moves, old_table, new_table, replicas, slots):
    me, column = lax.axis_index("replica"), lax.axis_index("mp")
    rows = old_table.shape[1]
    kept = [jnp.int32(1)] * rows
    for s in range(replicas - 1):
        valid, row, order = pair_row(moves, partner("replica", s + 1), me, rows, 1)
        plan[VALID, s], plan[ROW, s], plan[ORDER, s] = valid, row, order
        plan[NEW_INDEX, s], plan[NEW_SLOT, s] = locate(new_table, row, column, slots)
        kept = [jnp.where((valid == 1) & (row == r), 0, stays) for r, stays in enumerate(kept)]
    for r in range(rows):
        plan[KEPT, r] = kept[r]
        plan[INDEX, r], plan[SLOT, r] = locate(old_table, r, column, slots)


def open_kernel(count, local_heads, replicas, slots, x, q, weight, moves_all, old_all, new_all, *refs):
    outs, (plan_out, held, plan, moves, old_table, new_table, weight_sems, sems) = refs[:-8], refs[-8:]
    tables = start_copies(((moves_all, moves), (old_all, old_table), (new_all, new_table)), sems)
    depth, chunks = weight.shape[0], weight_sems.shape[0]
    spans = [pl.ds(c * (depth // chunks), depth // chunks) for c in range(chunks)]
    loads = start_copies([(weight.at[span], held.at[span]) for span in spans], weight_sems)
    rows = q.shape[1]
    wide = [q[i].astype(jnp.float32) for i in range(2)]
    blocks = [wide[i][:, h * HD : (h + 1) * HD] for i in range(2) for h in range(local_heads)]
    packed = jnp.concatenate(blocks, axis=0).astype(jnp.bfloat16)
    query_rows = packed.shape[0]
    for out in outs:
        out[:query_rows, :] = packed
    wait_for(tables)
    make_plan(plan, moves, old_table, new_table, replicas, slots)
    plan_copy = pltpu.make_async_copy(plan, plan_out, sems.at[3])
    plan_copy.start()
    total = jnp.zeros((x.shape[0], weight.shape[1]), jnp.float32)
    for span, load in zip(spans, loads):
        load.wait()
        total += jnp.dot(x[:, span], held[span, :], preferred_element_type=jnp.float32)
    for j in range(KVH):
        parts = []
        for half in range(2):
            start = (half * KVH + j) * HD
            part = total[:, start : start + HD]
            high = part.astype(jnp.bfloat16)
            parts += [high, (part - high.astype(jnp.float32)).astype(jnp.bfloat16)]
        parts = jnp.concatenate(parts, axis=0)
        for s, out in enumerate(outs):

            @pl.when(split(partner("mp", s) * local_heads, GROUP)[0] == j)
            def _(out=out, parts=parts):
                out[query_rows:, :] = parts

    plan_copy.wait()


def keep_kernel(replicas, *refs):
    pages_in, (pool, plan_all, pool_out, plan, sem, page_sems) = refs[: replicas - 1], refs[replicas - 1 :]
    load = pltpu.make_async_copy(plan_all, plan, sem)
    load.start()
    load.wait()
    slots, page_size, width = pool.shape
    copies = [(plan[VALID, s] == 1, plan[NEW_SLOT, s], page) for s, page in enumerate(pages_in)]
    copies += [(plan[KEPT, r] == 1, plan[SLOT, r], None) for r in range(slots)]
    started = []
    for n, (active, slot, page) in enumerate(copies):
        pairs = [(pool.at[slot], pool_out.at[slot])]
        if page is not None:
            pairs = [
                (page.at[pl.ds(line, page_size)], pool_out.at[slot, :, piece])
                for line, piece in zip(page_lines(width, page_size), pieces_of(width))
            ]
        parts = [pltpu.make_async_copy(*pair, page_sems.at[n, i]) for i, pair in enumerate(pairs)]
        started.append((active, parts))

        @pl.when(active)
        def _(parts=parts):
            for copy in parts:
                copy.start()

    for active, parts in started:
        pl.when(active)(functools.partial(wait_for, parts))


def extra_of(page, page_size, width):
    return page[page_size * width // HD :, :].astype(jnp.float32)


def length_of(extra):
    return extra[0:1] * 64.0 + extra[1:2]


def own_tokens(messages, rows, query_rows, half):
    tokens = 2 * rows
    start = query_rows + 2 * half * tokens
    total = jnp.zeros((tokens, HD), jnp.float32)
    for message in messages:
        total += message[start : start + tokens, :].astype(jnp.float32)
        total += message[start + tokens : start + 2 * tokens, :].astype(jnp.float32)
    return total.astype(jnp.bfloat16).astype(jnp.float32)


def scores_of(q, keys):
    return lax.dot_general(q, keys, (((1,), (1,)), ((), ())), preferred_element_type=jnp.float32)


def attend_kernel(count, local_heads, plan_all, lengths_all, pool, *refs):
    messages = by_distance(refs[:count])
    num, den, wide, plan, lengths, sems = refs[count:]
    tables = start_copies(((plan_all, plan), (lengths_all, lengths)), sems)
    rows = lengths.shape[0]
    slots, page_size, width = pool.shape
    both = 2 * local_heads
    for s, message in enumerate(messages):
        wide[s] = message[: both * rows, :].astype(jnp.float32)
    lane = lax.broadcasted_iota(jnp.int32, (both, HD), 1)
    token = lax.broadcasted_iota(jnp.int32, (both, page_size), 1)
    wait_for(tables)
    places = [(plan[INDEX, r], plan[SLOT, r]) for r in range(rows)]
    columns = [head_columns(partner("mp", s), local_heads) for s in range(count)]
    keys = pool.at[:, :, pl.ds(0, width // 2)]
    values = pool.at[:, :, pl.ds(width // 2, width // 2)]
    cases = [(r, s) for r in range(rows) for s in range(count)]
    scores = {}
    for r, s in cases:
        q = wide[s, pl.ds(r, both, stride=rows), :].astype(jnp.bfloat16)
        scores[r, s] = scores_of(q, keys[places[r][1], :, columns[s]])
    weights = {}
    denominators = [jnp.zeros((both, HD), jnp.float32) for _ in range(count)]
    for r, s in cases:
        inside = token < lengths[r] - places[r][0] * page_size
        weight = jnp.where(inside, weight_of(scores[r, s]), 0.0)
        weights[r, s] = weight.astype(jnp.bfloat16)
        total = jnp.sum(weight, axis=1, keepdims=True)
        denominators[s] += jnp.where(lane == r, total, 0.0)
    for r, s in cases:
        num[s, pl.ds(r, both, stride=rows), :] = jnp.dot(
            weights[r, s], values[places[r][1], :, columns[s]], preferred_element_type=jnp.float32
        )
    for s in range(count):
        den[s] = denominators[s]


def arrive_kernel(count, replicas, local_heads, rows, movers, page_size, *refs):
    refs = list(refs)
    take = lambda n: [refs.pop(0) for _ in range(n)]
    pages_in = take(replicas - 2)
    plan_all, projection = take(2)
    pages_in, messages = take(1) + pages_in, by_distance(take(count))
    num_in, den_in = take(2)
    outs = take(count - 1)
    own_num, own_den, own_kv, own_share, marks, num, den, wide, plan, sem = refs
    load = pltpu.make_async_copy(plan_all, plan, sem)
    load.start()
    depth, width = projection.shape
    half_rows = local_heads * rows

    extra = [extra_of(page, page_size, width) for page in pages_in]
    inputs = [
        jnp.concatenate([part[2 + i : 3 + i] for i in range(depth // HD)], axis=1) for part in extra
    ]
    inputs += [jnp.zeros((8 - len(inputs), depth), jnp.float32)]
    inputs = jnp.concatenate(inputs, axis=0).astype(jnp.bfloat16)
    share = jnp.dot(inputs, projection[...], preferred_element_type=jnp.float32)
    num[:, : 2 * half_rows, :] = num_in[...]
    den[...] = den_in[...]
    for s, message in enumerate(messages):
        wide[s, :half_rows, :] = message[half_rows : 2 * half_rows, :].astype(jnp.float32)
    lengths = [length_of(part) for part in extra]

    load.wait()
    lane = lax.broadcasted_iota(jnp.int32, (local_heads, HD), 1)
    token = lax.broadcasted_iota(jnp.int32, (local_heads, page_size), 1)
    lines = [
        pl.multiple_of(split(partner("mp", s) * local_heads, GROUP)[0] * page_size, page_size) for s in range(count)
    ]
    cases = [(d, s) for d in range(1, replicas) for s in range(count)]
    arrivals = [(plan[VALID, d], plan[ROW, d], plan[ORDER, d]) for d in range(replicas - 1)]
    indices = [plan[NEW_INDEX, d] for d in range(replicas - 1)]
    scores, weights, totals = {}, {}, {}
    for d, s in cases:
        row = arrivals[d - 1][1]
        q = wide[s, pl.ds(row, local_heads, stride=rows), :].astype(jnp.bfloat16)
        scores[d, s] = scores_of(q, pages_in[d - 1][pl.ds(lines[s], page_size), :])
    for d, s in cases:
        inside = (token + indices[d - 1] * page_size).astype(jnp.float32) < lengths[d - 1]
        weight = jnp.where(inside, weight_of(scores[d, s]), 0.0)
        weights[d, s] = weight.astype(jnp.bfloat16)
        totals[d, s] = jnp.sum(weight, axis=1, keepdims=True)
    for d, s in cases:
        values = pages_in[d - 1][pl.ds(lines[s] + KVH * page_size, page_size), :]
        scores[d, s] = jnp.dot(weights[d, s], values, preferred_element_type=jnp.float32)
    for d, (valid, row, _) in enumerate(arrivals, 1):

        @pl.when(valid == 1)
        def _(d=d, row=row):
            for s in range(count):
                num[s, pl.ds(half_rows + row, local_heads, stride=rows), :] = scores[d, s]
                old = den[s, pl.ds(local_heads, local_heads), :]
                den[s, pl.ds(local_heads, local_heads), :] = jnp.where(lane == row, totals[d, s], old)

    arrived = []
    row_ids = lax.broadcasted_iota(jnp.int32, (rows, HD), 0)
    for number in range(movers):
        picked = jnp.zeros((1, width), jnp.float32)
        mark = jnp.zeros((rows, HD), jnp.float32)
        for d, (valid, row, order) in enumerate(arrivals):
            here = (valid == 1) & (order == number)
            picked = jnp.where(here, share[d : d + 1], picked)
            mark = jnp.where(here & (row_ids == row), 1.0, mark)
        part = jnp.concatenate([picked[:, j * HD : (j + 1) * HD] for j in range(2 * KVH)], axis=0)
        high = part.astype(jnp.bfloat16).astype(jnp.float32)
        arrived += [high, part - high]
        own_share[number] = part
        marks[number] = mark
    own_num[...] = num[0, : 2 * half_rows, :]
    own_den[...] = den[0]
    all_kv = []
    for half in range(2):
        own_kv[half] = own_tokens(messages, rows, 2 * half_rows, half)
        all_kv.append(own_kv[half])
    filler = [jnp.zeros((-2 * local_heads % 16, HD), jnp.float32)] if local_heads % 8 else []
    for s, out in enumerate(outs):
        at = lax.axis_index("mp") ^ turn_target("mp", s + 1)
        parts = den[at]
        high = parts.astype(SEND).astype(jnp.float32)
        parts = high + pltpu.roll(parts - high, HD // 2, 1)
        out[...] = jnp.concatenate([num[at, : 2 * half_rows, :], parts] + filler + all_kv + arrived, axis=0).astype(SEND)


def finish_kernel(count, replicas, local_heads, movers, *refs):
    refs = list(refs)
    take = lambda n: [refs.pop(0) for _ in range(n)]
    pages_in = take(replicas - 2)
    plan_all, lengths_all, kv, share, marks, q, num, den = take(8)
    pages_in, messages = take(1) + pages_in, by_distance(take(count - 1))
    pool_raw, _, first, second, pool = take(5)
    plan, lengths, full, arrived, windows, results, sems, write_sems, out_sems = refs
    tables = start_copies(((plan_all, plan), (lengths_all, lengths)), sems)
    column = lax.axis_index("mp")
    rows = lengths.shape[0]
    slots, page_size, width = pool_raw.shape
    both = 2 * local_heads
    query_rows = both * rows
    head = split(column * local_heads, GROUP)[0]

    kv_base = messages[0].shape[0] - 4 * rows - 16 * movers
    for s in range(count):
        device = turn_source("mp", s)
        for half in range(2):
            if s == 0:
                chunk = kv[half]
            else:
                start = kv_base + half * 2 * rows
                chunk = messages[s - 1][start : start + 2 * rows, :].astype(jnp.float32)

            def place(half=half, device=device, chunk=chunk):
                columns = head_columns(device, local_heads)
                full.at[pl.ds(0, 2 * rows), pl.ds(half * (width // 2), width // 2)][:, columns] = chunk

            if local_heads == GROUP:
                place()
            else:
                pl.when(split(device * local_heads, GROUP)[1] == 0)(place)
    for number in range(movers):
        total = share[number]
        for message in messages:
            start = kv_base + 4 * rows + 16 * number
            part = message[start : start + 16, :].astype(jnp.float32)
            total += part[: 2 * KVH] + part[2 * KVH :]
        total = total.astype(jnp.bfloat16).astype(jnp.float32)
        arrived[number] = total
        for j in range(2 * KVH):
            full[2 * rows + number : 2 * rows + number + 1, j * HD : (j + 1) * HD] = total[j : j + 1, :]
    sums = den[...]
    for message in messages:
        part = message[query_rows : query_rows + both, :].astype(jnp.float32)
        sums += part + pltpu.roll(part, HD // 2, 1)
    sums = jnp.transpose(sums)[:rows, :]

    held = []
    for half in range(2):
        value = kv[half, :rows, :]
        for number in range(movers):
            moved = arrived[number, pl.ds(head + half * KVH, 1), :]
            value = jnp.where(marks[number] > 0.5, moved, value)
        held.append(value)
    outs = []

    def finish_step(step, out):
        pieces = []
        for h in range(local_heads):
            at = (step * local_heads + h) * rows
            query = q[at : at + rows, :].astype(jnp.float32)
            numerator = num[at : at + rows, :]
            for message in messages:
                numerator += message[at : at + rows, :].astype(jnp.float32)
            denominator = sums[:, step * local_heads + h : step * local_heads + h + 1]
            extra = [(kv[0, :rows, :], kv[1, :rows, :])]
            if step == 1:
                extra = [held, (kv[0, rows:, :], kv[1, rows:, :])]
            for key, value in extra:
                weight = weight_of(jnp.sum(query * key, axis=1, keepdims=True))
                numerator += weight.astype(jnp.bfloat16).astype(jnp.float32) * value
                denominator += weight
            pieces.append(numerator / denominator)
        results[step] = jnp.concatenate(pieces, axis=1).astype(out.dtype)
        outs.append(pltpu.make_async_copy(results.at[step], out, out_sems.at[step]))
        outs[-1].start()

    finish_step(0, first)
    wait_for(tables)
    plans = []

    def add_plan(active, index, slot, row, length, first_token, source, r=None):
        at = length - index * page_size
        touched = active & (at >= -1) & (at < page_size)
        start = jnp.clip(at, 0, page_size - WINDOW) & -16
        span = pl.ds(pl.multiple_of(start, 16), WINDOW)
        n = len(plans)
        if r is None:
            read = lambda: jnp.concatenate(
                [source[pl.ds(pl.multiple_of(line + start, 16), WINDOW), :] for line in page_lines(width, page_size)],
                axis=1,
            )
        else:
            read = lambda: source[slot, span, :]
        write = pltpu.make_async_copy(windows.at[n], pool.at[slot, span], write_sems.at[n])
        plans.append((touched, read, write, first_token, rows + row, at - start))

    for s, page in enumerate(pages_in):
        length = jnp.max(length_of(extra_of(page, page_size, width))).astype(jnp.int32)
        place = plan[NEW_INDEX, s], plan[NEW_SLOT, s]
        add_plan(plan[VALID, s] == 1, *place, plan[ROW, s], length, 2 * rows + plan[ORDER, s], page)
    for r in range(rows):
        add_plan(plan[KEPT, r] == 1, plan[INDEX, r], plan[SLOT, r], r, lengths[r], r, pool_raw, r)

    place_ids = lax.broadcasted_iota(jnp.int32, (WINDOW, width), 0)
    for n, (touched, read, write, token, next_token, offset) in enumerate(plans):

        @pl.when(touched)
        def _(n=n, read=read, write=write, token=token, next_token=next_token, offset=offset):
            old = read().astype(jnp.float32)
            new = jnp.where(place_ids == offset, full[pl.ds(token, 1), :], old)
            new = jnp.where(place_ids == offset + 1, full[pl.ds(next_token, 1), :], new)
            windows[n] = new.astype(jnp.bfloat16)
            write.start()

    finish_step(1, second)
    for plan in plans:
        pl.when(plan[0])(plan[2].wait)
    wait_for(outs)


def cost(microseconds):
    return pl.CostEstimate(flops=0, transcendentals=0, bytes_accessed=int(microseconds * 3.5e6))


def in_vmem(value):
    return pltpu.with_memory_space_constraint(value, pltpu.VMEM)


def in_hbm(value):
    return pltpu.with_memory_space_constraint(value, pltpu.HBM)


def params(megabytes=32, **rest):
    return pltpu.CompilerParams(vmem_limit_bytes=megabytes << 20, **rest)


def body(layer_input, kv_weight, queries, kv_pool, lengths, block_table, new_table, migrations):
    replicas, count = lax.axis_size("replica"), lax.axis_size("mp")
    rows = lengths.shape[0]
    pool = kv_pool[0, 0]
    slots, page_size, width = pool.shape
    local_heads = queries.shape[2] // HD
    both = 2 * local_heads
    query_rows = both * rows
    depth = layer_input.shape[2]
    f32, bf16 = jnp.float32, jnp.bfloat16
    moves, old_table, table_after = migrations.T, block_table.T, new_table.T
    shape = jax.ShapeDtypeStruct

    message_rows = query_rows + 8 * rows
    movers = migrations.shape[0] // replicas
    inputs = layer_input.reshape(2 * rows, depth)
    pool_near, *leaving = pl.pallas_call(
        functools.partial(leave_kernel, rows),
        out_shape=[shape(pool.shape, bf16)] + [shape((page_size * width // HD + extra_lines(depth), HD), bf16)] * (replicas - 1),
        in_specs=[HBM] * 5,
        out_specs=[VMEM] * replicas,
        scratch_shapes=[
            pltpu.SMEM(moves.shape, jnp.int32),
            pltpu.SMEM(old_table.shape, jnp.int32),
            pltpu.SMEM(lengths.shape, jnp.int32),
            pltpu.VMEM((2 * rows, depth), bf16),
            pltpu.SemaphoreType.DMA((4,)),
            pltpu.SemaphoreType.DMA((slots,)),
        ],
        compiler_params=params(),
        cost_estimate=cost(1.8),
        name="leave",
    )(*map(in_hbm, (moves, old_table, lengths, inputs, pool)))
    pages_in = exchange(leaving, "replica")

    weight_near, inputs_near, queries_near = map(in_vmem, (kv_weight, inputs, queries))
    *sent, plan = pl.pallas_call(
        functools.partial(open_kernel, count, local_heads, replicas, slots),
        out_shape=[shape((message_rows, HD), bf16)] * count + [shape((8, 128), jnp.int32)],
        in_specs=[VMEM] * 2 + [HBM] + [ANY] * 3,
        out_specs=[VMEM] * count + [ANY],
        scratch_shapes=[
            pltpu.VMEM((depth, width), bf16),
            pltpu.SMEM((8, 128), jnp.int32),
            pltpu.SMEM(moves.shape, jnp.int32),
            pltpu.SMEM(old_table.shape, jnp.int32),
            pltpu.SMEM(table_after.shape, jnp.int32),
            pltpu.SemaphoreType.DMA((8,)),
            pltpu.SemaphoreType.DMA((4,)),
        ],
        compiler_params=params(),
        cost_estimate=cost(1.2),
        name="open",
    )(inputs_near, queries_near, in_hbm(kv_weight), moves, old_table, table_after)
    sent, pages_in[0] = lax.optimization_barrier((list(sent), pages_in[0]))
    messages = [sent[0]] + exchange(sent[1:], "mp")

    num, den = pl.pallas_call(
        functools.partial(attend_kernel, count, local_heads),
        out_shape=[shape((count, query_rows, HD), f32), shape((count, both, HD), f32)],
        in_specs=[ANY, ANY, VMEM] + [VMEM] * count,
        out_specs=[VMEM, VMEM],
        scratch_shapes=[
            pltpu.VMEM((count, query_rows, HD), f32),
            pltpu.SMEM(plan.shape, jnp.int32),
            pltpu.SMEM(lengths.shape, jnp.int32),
            pltpu.SemaphoreType.DMA((2,)),
        ],
        compiler_params=params(),
        cost_estimate=cost(1.5),
        name="attend",
    )(plan, lengths, pool_near, *by_start(messages))

    sum_rows = query_rows + -(-both // 16) * 16 + 4 * rows + 16 * movers
    *sums, num, den, kv, share, marks = pl.pallas_call(
        functools.partial(arrive_kernel, count, replicas, local_heads, rows, movers, page_size),
        out_shape=[shape((sum_rows, HD), SEND)] * (count - 1)
        + [shape((query_rows, HD), f32), shape((both, HD), f32)]
        + [shape((2, 2 * rows, HD), f32), shape((movers, 2 * KVH, HD), f32)]
        + [shape((movers, rows, HD), f32)],
        in_specs=[VMEM] * (replicas - 2)
        + [ANY, VMEM, VMEM]
        + [VMEM] * count
        + [VMEM] * 2,
        out_specs=[VMEM] * (count + 4),
        scratch_shapes=[
            pltpu.VMEM((count, query_rows + rows, HD), f32),
            pltpu.VMEM((count, both, HD), f32),
            pltpu.VMEM((count, query_rows // 2 + rows, HD), f32),
            pltpu.SMEM(plan.shape, jnp.int32),
            pltpu.SemaphoreType.DMA(()),
        ],
        compiler_params=params(),
        cost_estimate=cost(1.2),
        name="arrive",
    )(*pages_in[1:], plan, weight_near, pages_in[0], *by_start(messages), num, den)
    sums_in = rotate(sums, "mp")

    plan_then, _ = lax.optimization_barrier((plan, marks))

    pool_copy = pl.pallas_call(
        functools.partial(keep_kernel, replicas),
        out_shape=shape(pool.shape, bf16),
        in_specs=[VMEM] * replicas + [ANY],
        out_specs=ANY,
        scratch_shapes=[
            pltpu.SMEM(plan.shape, jnp.int32),
            pltpu.SemaphoreType.DMA(()),
            pltpu.SemaphoreType.DMA((rows + replicas - 1, width // HD)),
        ],
        compiler_params=params(),
        cost_estimate=cost(1.6),
        name="keep",
    )(*pages_in, pool_near, plan_then)

    first, second, pool_after = pl.pallas_call(
        functools.partial(finish_kernel, count, replicas, local_heads, movers),
        out_shape=[
            shape((rows, local_heads * HD), bf16),
            shape((rows, local_heads * HD), bf16),
            shape(pool.shape, bf16),
        ],
        in_specs=[VMEM] * (replicas - 2) + [ANY] * 2 + [VMEM] * (7 + count - 1) + [VMEM, ANY],
        out_specs=[ANY] * 3,
        scratch_shapes=[
            pltpu.SMEM(plan.shape, jnp.int32),
            pltpu.SMEM(lengths.shape, jnp.int32),
            pltpu.VMEM((KV_ROWS, width), f32),
            pltpu.VMEM((movers, 2 * KVH, HD), f32),
            pltpu.VMEM((rows + replicas - 1, WINDOW, width), bf16),
            pltpu.VMEM((2, rows, local_heads * HD), bf16),
            pltpu.SemaphoreType.DMA((2,)),
            pltpu.SemaphoreType.DMA((rows + replicas - 1,)),
            pltpu.SemaphoreType.DMA((2,)),
        ],
        input_output_aliases={8 + replicas - 1 + (count - 1) + 1: 2},
        compiler_params=params(),
        cost_estimate=cost(2.5),
        name="finish",
    )(
        *pages_in[1:],
        *(plan, lengths),
        *(kv, share, marks, messages[0], num, den, pages_in[0]),
        *by_start(sums_in),
        *(pool_near, pool_copy),
    )
    return first, second, pool_after[None, None]


def solution(mesh):
    return jax.shard_map(
        body,
        mesh=mesh,
        in_specs=(
            P(None, ("groups", "replica"), "mp"),
            P("mp", None),
            P(None, ("groups", "replica"), "mp"),
            P(("groups", "replica"), "mp", None, None, None),
            P(("groups", "replica")),
            P(("groups", "replica"), None),
            P(("groups", "replica"), None),
            P("groups", None),
        ),
        out_specs=(
            P(("groups", "replica"), "mp"),
            P(("groups", "replica"), "mp"),
            P(("groups", "replica"), "mp", None, None, None),
        ),
        check_vma=False,
    )
```

```python
import functools
import math

import jax
import jax.numpy as jnp
from jax import lax
from jax.experimental import pallas as pl
from jax.experimental.pallas import tpu as pltpu
from jax.sharding import PartitionSpec as P

H = 32
KVH = 4
HD = 128
GROUP = H // KVH
CAP = 20.0
SCALE = 1.0 / math.sqrt(HD)
WINDOW = 32
KV_ROWS = 24

SMEM = pl.BlockSpec(memory_space=pltpu.SMEM)
VMEM = pl.BlockSpec(memory_space=pltpu.VMEM)
ANY = pl.BlockSpec(memory_space=pl.ANY)
HBM = pl.BlockSpec(memory_space=pltpu.HBM)
SEND = jnp.bfloat16


def swap(value, axis, distance):
    size = lax.axis_size(axis)
    return lax.ppermute(value, axis, [(i, i ^ distance) for i in range(size)])


def exchange(messages, axis):
    received = [swap(messages[d], axis, d + 1) for d in reversed(range(len(messages)))]
    return received[::-1]


def turns(size):
    if size == 4:
        return [[1, 3, 0, 2], [3, 2, 1, 0], [2, 0, 3, 1]]
    return [[(i + s) % size for i in range(size)] for s in range(1, size)]


def rotate(messages, axis):
    steps = turns(lax.axis_size(axis))
    return [lax.ppermute(message, axis, list(enumerate(step))) for message, step in zip(messages, steps)]


def pick(values, index):
    found = jnp.int32(values[0])
    for i, value in enumerate(values[1:], 1):
        found = jnp.where(index == i, value, found)
    return found


def turn_target(axis, k):
    return pick(turns(lax.axis_size(axis))[k - 1], lax.axis_index(axis))


def turn_source(axis, k):
    if k == 0:
        return lax.axis_index(axis)
    step = turns(lax.axis_size(axis))[k - 1]
    return pick([step.index(i) for i in range(len(step))], lax.axis_index(axis))


def start_order(count):
    return [count // 2] + [d for d in range(count - 1, 0, -1) if d != count // 2]


def by_start(values):
    own = len(values) & 1 ^ 1
    order = start_order(len(values)) if own else range(1, len(values) + 1)
    return [values[d - 1 + own] for d in order] + list(values[:own])


def by_distance(values):
    own = len(values) & 1 ^ 1
    order = start_order(len(values)) if own else range(1, len(values) + 1)
    return list(values[len(order) :]) + [values[list(order).index(d)] for d in range(1, len(order) + 1)]


def partner(axis, distance):
    return lax.axis_index(axis) ^ distance


def split(value, size):
    if size & (size - 1) == 0:
        return lax.shift_right_logical(value, size.bit_length() - 1), value & (size - 1)
    return lax.div(value, size), lax.rem(value, size)


def count_up(limit, step, state):
    if limit > 8:
        return lax.fori_loop(0, limit, step, state)
    for i in range(limit):
        state = step(i, state)
    return state


def locate(table, row, column, slots):
    def step(p, found):
        device, slot = split(table[p, row], slots)
        here = device == column
        return jnp.where(here, p, found[0]), jnp.where(here, slot, found[1])

    return count_up(table.shape[0], step, (jnp.int32(0), jnp.int32(0)))


def pair_row(moves, source, target, rows, side):
    def step(j, found):
        valid, row, order, number = found
        ends = [split(moves[i, j], rows) for i in range(2)]
        match = (ends[0][0] == source) & (ends[1][0] == target)
        return (
            jnp.where(match, jnp.int32(1), valid),
            jnp.where(match, ends[side][1], row),
            jnp.where(match, number, order),
            number + jnp.where(ends[side][0] == (source, target)[side], 1, 0),
        )

    return count_up(moves.shape[1], step, (jnp.int32(0),) * 4)[:3]


def head_columns(device, local_heads):
    return pl.ds(pl.multiple_of(split(device * local_heads, GROUP)[0] * HD, HD), HD)


def weight_of(score):
    return jnp.exp(CAP * jnp.tanh(score * (SCALE / CAP)))


def pieces_of(width):
    return [slice(at, at + HD) for at in range(0, width, HD)]


def page_lines(width, page_size):
    return [j * page_size for j in range(width // HD)]


def extra_lines(depth):
    return -(-(2 + depth // HD) // 8) * 8


def start_copies(pairs, sems):
    copies = [pltpu.make_async_copy(*pair, sems.at[i]) for i, pair in enumerate(pairs)]
    for copy in copies:
        copy.start()
    return copies


def wait_for(copies):
    for copy in copies:
        copy.wait()


def leave_kernel(rows, moves_all, table_all, lengths_all, x_all, pool, *refs):
    held, pages, (moves, table, lengths, x, sems, pool_sems) = refs[0], refs[1:-6], refs[-6:]
    me, column = lax.axis_index("replica"), lax.axis_index("mp")
    page_size, width = pool.shape[1:]
    depth = x.shape[1]
    rest = start_copies(
        ((moves_all, moves), (table_all, table), (lengths_all, lengths), (x_all, x)), sems
    )
    copies = start_copies([(pool.at[i], held.at[i]) for i in range(pool.shape[0])], pool_sems)
    wait_for(rest[:2])
    found = [pair_row(moves, me, partner("replica", s + 1), rows, 0)[1] for s in range(len(pages))]
    picks = [locate(table, row, column, pool.shape[0])[1] for row in found]
    wait_for(rest[2:])
    lines = extra_lines(depth)
    sublane = lax.broadcasted_iota(jnp.int32, (lines, HD), 0)
    first_rows = x[:rows, :].astype(jnp.float32)
    row_ids = lax.broadcasted_iota(jnp.int32, (rows, depth), 0)
    for row, page in zip(found, pages):
        high, low = split(lengths[row], 64)
        picked = jnp.sum(jnp.where(row_ids == row, first_rows, 0.0), axis=0, keepdims=True)
        parts = [jnp.zeros((2, HD), jnp.float32)] + [picked[:, piece] for piece in pieces_of(depth)]
        spare = lines - 2 - depth // HD
        parts += [jnp.zeros((spare, HD), jnp.float32)] if spare else []
        extra = jnp.concatenate(parts, axis=0)
        extra = jnp.where(sublane == 0, high.astype(jnp.float32), extra)
        extra = jnp.where(sublane == 1, low.astype(jnp.float32), extra)
        page[page_size * width // HD :, :] = extra.astype(jnp.bfloat16)
    wait_for(copies)
    for slot, page in zip(picks, pages):
        for line, piece in zip(page_lines(width, page_size), pieces_of(width)):
            page[line : line + page_size, :] = held[slot, :, piece]


INDEX, SLOT, KEPT, VALID, ROW, ORDER, NEW_INDEX, NEW_SLOT = range(8)


def make_plan(plan, moves, old_table, new_table, replicas, slots):
    me, column = lax.axis_index("replica"), lax.axis_index("mp")
    rows = old_table.shape[1]
    kept = [jnp.int32(1)] * rows
    for s in range(replicas - 1):
        valid, row, order = pair_row(moves, partner("replica", s + 1), me, rows, 1)
        plan[VALID, s], plan[ROW, s], plan[ORDER, s] = valid, row, order
        plan[NEW_INDEX, s], plan[NEW_SLOT, s] = locate(new_table, row, column, slots)
        kept = [jnp.where((valid == 1) & (row == r), 0, stays) for r, stays in enumerate(kept)]
    for r in range(rows):
        plan[KEPT, r] = kept[r]
        plan[INDEX, r], plan[SLOT, r] = locate(old_table, r, column, slots)


def open_kernel(count, local_heads, replicas, slots, x, q, weight, moves_all, old_all, new_all, *refs):
    outs, (plan_out, held, plan, moves, old_table, new_table, weight_sems, sems) = refs[:-8], refs[-8:]
    tables = start_copies(((moves_all, moves), (old_all, old_table), (new_all, new_table)), sems)
    depth, chunks = weight.shape[0], weight_sems.shape[0]
    spans = [pl.ds(c * (depth // chunks), depth // chunks) for c in range(chunks)]
    loads = start_copies([(weight.at[span], held.at[span]) for span in spans], weight_sems)
    rows = q.shape[1]
    wide = [q[i].astype(jnp.float32) for i in range(2)]
    blocks = [wide[i][:, h * HD : (h + 1) * HD] for i in range(2) for h in range(local_heads)]
    packed = jnp.concatenate(blocks, axis=0).astype(jnp.bfloat16)
    query_rows = packed.shape[0]
    for out in outs:
        out[:query_rows, :] = packed
    wait_for(tables)
    make_plan(plan, moves, old_table, new_table, replicas, slots)
    plan_copy = pltpu.make_async_copy(plan, plan_out, sems.at[3])
    plan_copy.start()
    total = jnp.zeros((x.shape[0], weight.shape[1]), jnp.float32)
    for span, load in zip(spans, loads):
        load.wait()
        total += jnp.dot(x[:, span], held[span, :], preferred_element_type=jnp.float32)
    for j in range(KVH):
        parts = []
        for half in range(2):
            start = (half * KVH + j) * HD
            part = total[:, start : start + HD]
            high = part.astype(jnp.bfloat16)
            parts += [high, (part - high.astype(jnp.float32)).astype(jnp.bfloat16)]
        parts = jnp.concatenate(parts, axis=0)
        for s, out in enumerate(outs):

            @pl.when(split(partner("mp", s) * local_heads, GROUP)[0] == j)
            def _(out=out, parts=parts):
                out[query_rows:, :] = parts

    plan_copy.wait()


def keep_kernel(replicas, *refs):
    pages_in, (pool, plan_all, pool_out, plan, sem, page_sems) = refs[: replicas - 1], refs[replicas - 1 :]
    load = pltpu.make_async_copy(plan_all, plan, sem)
    load.start()
    load.wait()
    slots, page_size, width = pool.shape
    copies = [(plan[VALID, s] == 1, plan[NEW_SLOT, s], page) for s, page in enumerate(pages_in)]
    copies += [(plan[KEPT, r] == 1, plan[SLOT, r], None) for r in range(slots)]
    started = []
    for n, (active, slot, page) in enumerate(copies):
        pairs = [(pool.at[slot], pool_out.at[slot])]
        if page is not None:
            pairs = [
                (page.at[pl.ds(line, page_size)], pool_out.at[slot, :, piece])
                for line, piece in zip(page_lines(width, page_size), pieces_of(width))
            ]
        parts = [pltpu.make_async_copy(*pair, page_sems.at[n, i]) for i, pair in enumerate(pairs)]
        started.append((active, parts))

        @pl.when(active)
        def _(parts=parts):
            for copy in parts:
                copy.start()

    for active, parts in started:
        pl.when(active)(functools.partial(wait_for, parts))


def extra_of(page, page_size, width):
    return page[page_size * width // HD :, :].astype(jnp.float32)


def length_of(extra):
    return extra[0:1] * 64.0 + extra[1:2]


def own_tokens(messages, rows, query_rows, half):
    tokens = 2 * rows
    start = query_rows + 2 * half * tokens
    total = jnp.zeros((tokens, HD), jnp.float32)
    for message in messages:
        total += message[start : start + tokens, :].astype(jnp.float32)
        total += message[start + tokens : start + 2 * tokens, :].astype(jnp.float32)
    return total.astype(jnp.bfloat16).astype(jnp.float32)


def scores_of(q, keys):
    return lax.dot_general(q, keys, (((1,), (1,)), ((), ())), preferred_element_type=jnp.float32)


def attend_kernel(count, local_heads, table, lengths, pool, *refs):
    messages = by_distance(refs[:count])
    num, den, wide = refs[count:]
    column = lax.axis_index("mp")
    rows = lengths.shape[0]
    slots, page_size, width = pool.shape
    both = 2 * local_heads
    for s, message in enumerate(messages):
        wide[s] = message[: both * rows, :].astype(jnp.float32)
    lane = lax.broadcasted_iota(jnp.int32, (both, HD), 1)
    token = lax.broadcasted_iota(jnp.int32, (both, page_size), 1)
    places = [locate(table, r, column, slots) for r in range(rows)]
    columns = [head_columns(partner("mp", s), local_heads) for s in range(count)]
    keys = pool.at[:, :, pl.ds(0, width // 2)]
    values = pool.at[:, :, pl.ds(width // 2, width // 2)]
    cases = [(r, s) for r in range(rows) for s in range(count)]
    scores = {}
    for r, s in cases:
        q = wide[s, pl.ds(r, both, stride=rows), :].astype(jnp.bfloat16)
        scores[r, s] = scores_of(q, keys[places[r][1], :, columns[s]])
    weights = {}
    denominators = [jnp.zeros((both, HD), jnp.float32) for _ in range(count)]
    for r, s in cases:
        inside = token < lengths[r] - places[r][0] * page_size
        weight = jnp.where(inside, weight_of(scores[r, s]), 0.0)
        weights[r, s] = weight.astype(jnp.bfloat16)
        total = jnp.sum(weight, axis=1, keepdims=True)
        denominators[s] += jnp.where(lane == r, total, 0.0)
    for r, s in cases:
        num[s, pl.ds(r, both, stride=rows), :] = jnp.dot(
            weights[r, s], values[places[r][1], :, columns[s]], preferred_element_type=jnp.float32
        )
    for s in range(count):
        den[s] = denominators[s]


def arrive_kernel(count, replicas, local_heads, rows, movers, page_size, *refs):
    refs = list(refs)
    take = lambda n: [refs.pop(0) for _ in range(n)]
    pages_in = take(replicas - 2)
    plan_all, projection = take(2)
    pages_in, messages = take(1) + pages_in, by_distance(take(count))
    num_in, den_in = take(2)
    outs = take(count - 1)
    own_num, own_den, own_kv, own_share, marks, num, den, wide, plan, sem = refs
    load = pltpu.make_async_copy(plan_all, plan, sem)
    load.start()
    depth, width = projection.shape
    half_rows = local_heads * rows

    extra = [extra_of(page, page_size, width) for page in pages_in]
    inputs = [
        jnp.concatenate([part[2 + i : 3 + i] for i in range(depth // HD)], axis=1) for part in extra
    ]
    inputs += [jnp.zeros((8 - len(inputs), depth), jnp.float32)]
    inputs = jnp.concatenate(inputs, axis=0).astype(jnp.bfloat16)
    share = jnp.dot(inputs, projection[...], preferred_element_type=jnp.float32)
    num[:, : 2 * half_rows, :] = num_in[...]
    den[...] = den_in[...]
    for s, message in enumerate(messages):
        wide[s, :half_rows, :] = message[half_rows : 2 * half_rows, :].astype(jnp.float32)
    lengths = [length_of(part) for part in extra]

    load.wait()
    lane = lax.broadcasted_iota(jnp.int32, (local_heads, HD), 1)
    token = lax.broadcasted_iota(jnp.int32, (local_heads, page_size), 1)
    lines = [
        pl.multiple_of(split(partner("mp", s) * local_heads, GROUP)[0] * page_size, page_size) for s in range(count)
    ]
    cases = [(d, s) for d in range(1, replicas) for s in range(count)]
    arrivals = [(plan[VALID, d], plan[ROW, d], plan[ORDER, d]) for d in range(replicas - 1)]
    indices = [plan[NEW_INDEX, d] for d in range(replicas - 1)]
    scores, weights, totals = {}, {}, {}
    for d, s in cases:
        row = arrivals[d - 1][1]
        q = wide[s, pl.ds(row, local_heads, stride=rows), :].astype(jnp.bfloat16)
        scores[d, s] = scores_of(q, pages_in[d - 1][pl.ds(lines[s], page_size), :])
    for d, s in cases:
        inside = (token + indices[d - 1] * page_size).astype(jnp.float32) < lengths[d - 1]
        weight = jnp.where(inside, weight_of(scores[d, s]), 0.0)
        weights[d, s] = weight.astype(jnp.bfloat16)
        totals[d, s] = jnp.sum(weight, axis=1, keepdims=True)
    for d, s in cases:
        values = pages_in[d - 1][pl.ds(lines[s] + KVH * page_size, page_size), :]
        scores[d, s] = jnp.dot(weights[d, s], values, preferred_element_type=jnp.float32)
    for d, (valid, row, _) in enumerate(arrivals, 1):

        @pl.when(valid == 1)
        def _(d=d, row=row):
            for s in range(count):
                num[s, pl.ds(half_rows + row, local_heads, stride=rows), :] = scores[d, s]
                old = den[s, pl.ds(local_heads, local_heads), :]
                den[s, pl.ds(local_heads, local_heads), :] = jnp.where(lane == row, totals[d, s], old)

    arrived = []
    row_ids = lax.broadcasted_iota(jnp.int32, (rows, HD), 0)
    for number in range(movers):
        picked = jnp.zeros((1, width), jnp.float32)
        mark = jnp.zeros((rows, HD), jnp.float32)
        for d, (valid, row, order) in enumerate(arrivals):
            here = (valid == 1) & (order == number)
            picked = jnp.where(here, share[d : d + 1], picked)
            mark = jnp.where(here & (row_ids == row), 1.0, mark)
        part = jnp.concatenate([picked[:, j * HD : (j + 1) * HD] for j in range(2 * KVH)], axis=0)
        high = part.astype(jnp.bfloat16).astype(jnp.float32)
        arrived += [high, part - high]
        own_share[number] = part
        marks[number] = mark
    own_num[...] = num[0, : 2 * half_rows, :]
    own_den[...] = den[0]
    all_kv = []
    for half in range(2):
        own_kv[half] = own_tokens(messages, rows, 2 * half_rows, half)
        all_kv.append(own_kv[half])
    filler = [jnp.zeros((-2 * local_heads % 16, HD), jnp.float32)] if local_heads % 8 else []
    for s, out in enumerate(outs):
        at = lax.axis_index("mp") ^ turn_target("mp", s + 1)
        parts = den[at]
        high = parts.astype(SEND).astype(jnp.float32)
        parts = high + pltpu.roll(parts - high, HD // 2, 1)
        out[...] = jnp.concatenate([num[at, : 2 * half_rows, :], parts] + filler + all_kv + arrived, axis=0).astype(SEND)


def finish_kernel(count, replicas, local_heads, movers, *refs):
    refs = list(refs)
    take = lambda n: [refs.pop(0) for _ in range(n)]
    pages_in = take(replicas - 2)
    plan_all, lengths_all, kv, share, marks, q, num, den = take(8)
    pages_in, messages = take(1) + pages_in, by_distance(take(count - 1))
    pool_raw, _, first, second, pool = take(5)
    plan, lengths, full, arrived, windows, results, sems, write_sems, out_sems = refs
    tables = start_copies(((plan_all, plan), (lengths_all, lengths)), sems)
    column = lax.axis_index("mp")
    rows = lengths.shape[0]
    slots, page_size, width = pool_raw.shape
    both = 2 * local_heads
    query_rows = both * rows
    head = split(column * local_heads, GROUP)[0]

    kv_base = messages[0].shape[0] - 4 * rows - 16 * movers
    for s in range(count):
        device = turn_source("mp", s)
        for half in range(2):
            if s == 0:
                chunk = kv[half]
            else:
                start = kv_base + half * 2 * rows
                chunk = messages[s - 1][start : start + 2 * rows, :].astype(jnp.float32)

            def place(half=half, device=device, chunk=chunk):
                columns = head_columns(device, local_heads)
                full.at[pl.ds(0, 2 * rows), pl.ds(half * (width // 2), width // 2)][:, columns] = chunk

            if local_heads == GROUP:
                place()
            else:
                pl.when(split(device * local_heads, GROUP)[1] == 0)(place)
    for number in range(movers):
        total = share[number]
        for message in messages:
            start = kv_base + 4 * rows + 16 * number
            part = message[start : start + 16, :].astype(jnp.float32)
            total += part[: 2 * KVH] + part[2 * KVH :]
        total = total.astype(jnp.bfloat16).astype(jnp.float32)
        arrived[number] = total
        for j in range(2 * KVH):
            full[2 * rows + number : 2 * rows + number + 1, j * HD : (j + 1) * HD] = total[j : j + 1, :]
    sums = den[...]
    for message in messages:
        part = message[query_rows : query_rows + both, :].astype(jnp.float32)
        sums += part + pltpu.roll(part, HD // 2, 1)
    sums = jnp.transpose(sums)[:rows, :]

    held = []
    for half in range(2):
        value = kv[half, :rows, :]
        for number in range(movers):
            moved = arrived[number, pl.ds(head + half * KVH, 1), :]
            value = jnp.where(marks[number] > 0.5, moved, value)
        held.append(value)
    outs = []

    def finish_step(step, out):
        pieces = []
        for h in range(local_heads):
            at = (step * local_heads + h) * rows
            query = q[at : at + rows, :].astype(jnp.float32)
            numerator = num[at : at + rows, :]
            for message in messages:
                numerator += message[at : at + rows, :].astype(jnp.float32)
            denominator = sums[:, step * local_heads + h : step * local_heads + h + 1]
            extra = [(kv[0, :rows, :], kv[1, :rows, :])]
            if step == 1:
                extra = [held, (kv[0, rows:, :], kv[1, rows:, :])]
            for key, value in extra:
                weight = weight_of(jnp.sum(query * key, axis=1, keepdims=True))
                numerator += weight.astype(jnp.bfloat16).astype(jnp.float32) * value
                denominator += weight
            pieces.append(numerator / denominator)
        results[step] = jnp.concatenate(pieces, axis=1).astype(out.dtype)
        outs.append(pltpu.make_async_copy(results.at[step], out, out_sems.at[step]))
        outs[-1].start()

    finish_step(0, first)
    wait_for(tables)
    plans = []

    def add_plan(active, index, slot, row, length, first_token, source, r=None):
        at = length - index * page_size
        touched = active & (at >= -1) & (at < page_size)
        start = jnp.clip(at, 0, page_size - WINDOW) & -16
        span = pl.ds(pl.multiple_of(start, 16), WINDOW)
        n = len(plans)
        if r is None:
            read = lambda: jnp.concatenate(
                [source[pl.ds(pl.multiple_of(line + start, 16), WINDOW), :] for line in page_lines(width, page_size)],
                axis=1,
            )
        else:
            read = lambda: source[slot, span, :]
        write = pltpu.make_async_copy(windows.at[n], pool.at[slot, span], write_sems.at[n])
        plans.append((touched, read, write, first_token, rows + row, at - start))

    for s, page in enumerate(pages_in):
        length = jnp.max(length_of(extra_of(page, page_size, width))).astype(jnp.int32)
        place = plan[NEW_INDEX, s], plan[NEW_SLOT, s]
        add_plan(plan[VALID, s] == 1, *place, plan[ROW, s], length, 2 * rows + plan[ORDER, s], page)
    for r in range(rows):
        add_plan(plan[KEPT, r] == 1, plan[INDEX, r], plan[SLOT, r], r, lengths[r], r, pool_raw, r)

    place_ids = lax.broadcasted_iota(jnp.int32, (WINDOW, width), 0)
    for n, (touched, read, write, token, next_token, offset) in enumerate(plans):

        @pl.when(touched)
        def _(n=n, read=read, write=write, token=token, next_token=next_token, offset=offset):
            old = read().astype(jnp.float32)
            new = jnp.where(place_ids == offset, full[pl.ds(token, 1), :], old)
            new = jnp.where(place_ids == offset + 1, full[pl.ds(next_token, 1), :], new)
            windows[n] = new.astype(jnp.bfloat16)
            write.start()

    finish_step(1, second)
    for plan in plans:
        pl.when(plan[0])(plan[2].wait)
    wait_for(outs)


def cost(microseconds):
    return pl.CostEstimate(flops=0, transcendentals=0, bytes_accessed=int(microseconds * 3.5e6))


def in_vmem(value):
    return pltpu.with_memory_space_constraint(value, pltpu.VMEM)


def in_hbm(value):
    return pltpu.with_memory_space_constraint(value, pltpu.HBM)


def params(megabytes=32, **rest):
    return pltpu.CompilerParams(vmem_limit_bytes=megabytes << 20, **rest)


def body(layer_input, kv_weight, queries, kv_pool, lengths, block_table, new_table, migrations):
    replicas, count = lax.axis_size("replica"), lax.axis_size("mp")
    rows = lengths.shape[0]
    pool = kv_pool[0, 0]
    slots, page_size, width = pool.shape
    local_heads = queries.shape[2] // HD
    both = 2 * local_heads
    query_rows = both * rows
    depth = layer_input.shape[2]
    f32, bf16 = jnp.float32, jnp.bfloat16
    moves, old_table, table_after = migrations.T, block_table.T, new_table.T
    shape = jax.ShapeDtypeStruct

    message_rows = query_rows + 8 * rows
    movers = migrations.shape[0] // replicas
    inputs = layer_input.reshape(2 * rows, depth)
    pool_near, *leaving = pl.pallas_call(
        functools.partial(leave_kernel, rows),
        out_shape=[shape(pool.shape, bf16)] + [shape((page_size * width // HD + extra_lines(depth), HD), bf16)] * (replicas - 1),
        in_specs=[HBM] * 5,
        out_specs=[VMEM] * replicas,
        scratch_shapes=[
            pltpu.SMEM(moves.shape, jnp.int32),
            pltpu.SMEM(old_table.shape, jnp.int32),
            pltpu.SMEM(lengths.shape, jnp.int32),
            pltpu.VMEM((2 * rows, depth), bf16),
            pltpu.SemaphoreType.DMA((4,)),
            pltpu.SemaphoreType.DMA((slots,)),
        ],
        compiler_params=params(),
        cost_estimate=cost(1.8),
        name="leave",
    )(*map(in_hbm, (moves, old_table, lengths, inputs, pool)))
    pages_in = exchange(leaving, "replica")

    weight_near, inputs_near, queries_near = map(in_vmem, (kv_weight, inputs, queries))
    *sent, plan = pl.pallas_call(
        functools.partial(open_kernel, count, local_heads, replicas, slots),
        out_shape=[shape((message_rows, HD), bf16)] * count + [shape((8, 128), jnp.int32)],
        in_specs=[VMEM] * 2 + [HBM] + [ANY] * 3,
        out_specs=[VMEM] * count + [ANY],
        scratch_shapes=[
            pltpu.VMEM((depth, width), bf16),
            pltpu.SMEM((8, 128), jnp.int32),
            pltpu.SMEM(moves.shape, jnp.int32),
            pltpu.SMEM(old_table.shape, jnp.int32),
            pltpu.SMEM(table_after.shape, jnp.int32),
            pltpu.SemaphoreType.DMA((8,)),
            pltpu.SemaphoreType.DMA((4,)),
        ],
        compiler_params=params(),
        cost_estimate=cost(1.2),
        name="open",
    )(inputs_near, queries_near, in_hbm(kv_weight), moves, old_table, table_after)
    sent, pages_in[0] = lax.optimization_barrier((list(sent), pages_in[0]))
    messages = [sent[0]] + exchange(sent[1:], "mp")

    num, den = pl.pallas_call(
        functools.partial(attend_kernel, count, local_heads),
        out_shape=[shape((count, query_rows, HD), f32), shape((count, both, HD), f32)],
        in_specs=[SMEM, SMEM, VMEM] + [VMEM] * count,
        out_specs=[VMEM, VMEM],
        scratch_shapes=[pltpu.VMEM((count, query_rows, HD), f32)],
        compiler_params=params(),
        cost_estimate=cost(1.5),
        name="attend",
    )(old_table, lengths, pool_near, *by_start(messages))

    sum_rows = query_rows + -(-both // 16) * 16 + 4 * rows + 16 * movers
    *sums, num, den, kv, share, marks = pl.pallas_call(
        functools.partial(arrive_kernel, count, replicas, local_heads, rows, movers, page_size),
        out_shape=[shape((sum_rows, HD), SEND)] * (count - 1)
        + [shape((query_rows, HD), f32), shape((both, HD), f32)]
        + [shape((2, 2 * rows, HD), f32), shape((movers, 2 * KVH, HD), f32)]
        + [shape((movers, rows, HD), f32)],
        in_specs=[VMEM] * (replicas - 2)
        + [ANY, VMEM, VMEM]
        + [VMEM] * count
        + [VMEM] * 2,
        out_specs=[VMEM] * (count + 4),
        scratch_shapes=[
            pltpu.VMEM((count, query_rows + rows, HD), f32),
            pltpu.VMEM((count, both, HD), f32),
            pltpu.VMEM((count, query_rows // 2 + rows, HD), f32),
            pltpu.SMEM(plan.shape, jnp.int32),
            pltpu.SemaphoreType.DMA(()),
        ],
        compiler_params=params(),
        cost_estimate=cost(1.2),
        name="arrive",
    )(*pages_in[1:], plan, weight_near, pages_in[0], *by_start(messages), num, den)
    sums_in = rotate(sums, "mp")

    plan_then, _ = lax.optimization_barrier((plan, marks))

    pool_copy = pl.pallas_call(
        functools.partial(keep_kernel, replicas),
        out_shape=shape(pool.shape, bf16),
        in_specs=[VMEM] * replicas + [ANY],
        out_specs=ANY,
        scratch_shapes=[
            pltpu.SMEM(plan.shape, jnp.int32),
            pltpu.SemaphoreType.DMA(()),
            pltpu.SemaphoreType.DMA((rows + replicas - 1, width // HD)),
        ],
        compiler_params=params(),
        cost_estimate=cost(1.6),
        name="keep",
    )(*pages_in, pool_near, plan_then)

    first, second, pool_after = pl.pallas_call(
        functools.partial(finish_kernel, count, replicas, local_heads, movers),
        out_shape=[
            shape((rows, local_heads * HD), bf16),
            shape((rows, local_heads * HD), bf16),
            shape(pool.shape, bf16),
        ],
        in_specs=[VMEM] * (replicas - 2) + [ANY] * 2 + [VMEM] * (7 + count - 1) + [VMEM, ANY],
        out_specs=[ANY] * 3,
        scratch_shapes=[
            pltpu.SMEM(plan.shape, jnp.int32),
            pltpu.SMEM(lengths.shape, jnp.int32),
            pltpu.VMEM((KV_ROWS, width), f32),
            pltpu.VMEM((movers, 2 * KVH, HD), f32),
            pltpu.VMEM((rows + replicas - 1, WINDOW, width), bf16),
            pltpu.VMEM((2, rows, local_heads * HD), bf16),
            pltpu.SemaphoreType.DMA((2,)),
            pltpu.SemaphoreType.DMA((rows + replicas - 1,)),
            pltpu.SemaphoreType.DMA((2,)),
        ],
        input_output_aliases={8 + replicas - 1 + (count - 1) + 1: 2},
        compiler_params=params(),
        cost_estimate=cost(2.5),
        name="finish",
    )(
        *pages_in[1:],
        *(plan, lengths),
        *(kv, share, marks, messages[0], num, den, pages_in[0]),
        *by_start(sums_in),
        *(pool_near, pool_copy),
    )
    return first, second, pool_after[None, None]


def solution(mesh):
    return jax.shard_map(
        body,
        mesh=mesh,
        in_specs=(
            P(None, ("groups", "replica"), "mp"),
            P("mp", None),
            P(None, ("groups", "replica"), "mp"),
            P(("groups", "replica"), "mp", None, None, None),
            P(("groups", "replica")),
            P(("groups", "replica"), None),
            P(("groups", "replica"), None),
            P("groups", None),
        ),
        out_specs=(
            P(("groups", "replica"), "mp"),
            P(("groups", "replica"), "mp"),
            P(("groups", "replica"), "mp", None, None, None),
        ),
        check_vma=False,
    )
```
